32 devices in a mesh: pair: 8 (over z, x), mo: 4 (over y, core).
Axes of the slice: x: 2, y: 2, z: 4, core: 2. Of those that a mesh axis runs over, the one named last changes fastest.
Arguments:
- integrals: bfloat16 [128, 1000, 1000], P('pair', 'mo'), may hold values from -6 to 6
- coeffs: bfloat16 [1000, 512], replicated, may hold values from -0.1875 to 0.1875
- mirror: int32 [128], replicated, may hold values from 0 to 127, as said below
Outputs:
- combined: float32 [128, 512, 512], P(None, 'pair', 'mo')
The draws below stay inside these ranges and needn't reach their ends.
Inputs may be any that keep to these rules, and one draw needn't show every extreme that they name: mirror pairs the rows: mirror[mirror[k]] = k and mirror[k] != k for every row k; a row and its mirror may lie on any devices.
All inputs are finite; a program needn't handle non-finite values.
Results may differ from the reference program's by a relative error of at most 0.0029.
Values may be sent and summed in bfloat16 or wider, within the bound.
No kernel may reach another device: no remote copies, remote signals or barrier semaphores. Data moves between devices by JAX's collectives and lax.ppermute only.
A program may use at most 128 MiB of HBM per device.

```python
import jax
import jax.numpy as jnp
from jax import lax

NBF = 1000
NMO = 512
ROWS = 128


def draw_mirror(key, part):
    order = jax.random.permutation(key, ROWS).astype(jnp.int32)
    first = order[0::2]
    second = order[1::2]
    paired = jnp.zeros((ROWS,), jnp.int32).at[first].set(second)
    return paired.at[second].set(first)


def steps_of(stream_key, shape, pieces, smallest, high):
    def one(axis_at, blocks):
        heights = jax.random.uniform(jax.random.fold_in(jax.random.fold_in(stream_key, 6), axis_at), (blocks,), jnp.float32, smallest / len(pieces), high / len(pieces))
        return jnp.repeat(jnp.exp(heights), shape[axis_at] // blocks).reshape((-1,) + (1,) * (len(shape) - axis_at - 1))

    level = one(*pieces[0])
    for cut in pieces[1:]:
        level = level * one(*cut)
    return level


def centred(rng, shape, width, limit, split=(), held_as=jnp.bfloat16):
    values = width * jax.random.normal(rng, shape, jnp.float32)
    if split:
        values = values * steps_of(rng, shape, split, -0.22, 0.18)
    return jnp.clip(values, -limit, limit).astype(held_as)


def setup_inputs(seed: int = 0) -> dict:
    seeds = jax.random.split(jax.random.key(seed), 4)
    integrals = centred(seeds[0], (ROWS, NBF, NBF), 1.0, 6.0, ((0, 8), (1, 4)))
    coeffs = centred(seeds[1], (NBF, NMO), NBF ** -0.5, 0.1875)
    mirror = draw_mirror(jax.random.fold_in(seeds[3], 71), 0)
    return {"integrals": integrals, "coeffs": coeffs, "mirror": mirror}


def reference(integrals, coeffs, mirror):
    def one_row(block):
        quarter = jnp.dot(block, coeffs, preferred_element_type=jnp.float32).astype(jnp.bfloat16)
        return jnp.dot(coeffs.T, quarter, preferred_element_type=jnp.float32)

    half = lax.map(one_row, integrals)
    partner = jnp.take(half, mirror.astype(jnp.int32), axis=0)
    return 0.5 * (half + partner)
```

```python
import functools

import jax
import jax.numpy as jnp
from jax import lax
from jax.experimental import pallas as pl
from jax.experimental.pallas import tpu as pltpu
from jax.sharding import PartitionSpec as P

LANES = 128
STEP = 64
CHUNKS = (4, 4, 4, 4)
VMEM = 48 * 1024 * 1024


def quarter_kernel(rows, starts, x_ref, c_ref, *refs):
    outs, acc = refs[:-1], refs[-1]
    step, k_all, depth = x_ref.shape
    x = x_ref[...].reshape(step * k_all, depth)
    for d in range(acc.shape[0]):
        columns = c_ref[:, d * LANES : (d + 1) * LANES]
        acc[d] = jnp.dot(x, columns, preferred_element_type=jnp.float32)
    left = rows - pl.program_id(0) * step
    keep = lax.broadcasted_iota(jnp.int32, (step, LANES), 0) < left
    for out, first in zip(outs, starts):
        for d in range(out.shape[0]):
            for k in range(out.shape[1]):
                block = acc[d, pl.ds(first + k, step, stride=k_all), :]
                out[d, k] = jnp.where(keep, block, 0.0).astype(jnp.bfloat16)


def quarter_of(by_r, coeffs, n_mo, padded):
    rows, k_all, depth = by_r.shape
    orbitals = coeffs.shape[1]
    starts = [sum(CHUNKS[:c]) for c in range(len(CHUNKS))]
    return pl.pallas_call(
        functools.partial(quarter_kernel, rows, starts),
        grid=(padded // STEP,),
        out_shape=[jax.ShapeDtypeStruct((n_mo, kc, padded, LANES), jnp.bfloat16) for kc in CHUNKS],
        in_specs=[
            pl.BlockSpec((STEP, k_all, depth), lambda r: (r, 0, 0)),
            pl.BlockSpec((depth, orbitals), lambda r: (0, 0)),
        ],
        out_specs=[pl.BlockSpec((n_mo, kc, STEP, LANES), lambda r: (0, 0, r, 0)) for kc in CHUNKS],
        scratch_shapes=[pltpu.VMEM((n_mo, STEP * k_all, LANES), jnp.float32)],
        compiler_params=pltpu.CompilerParams(vmem_limit_bytes=VMEM),
        cost_estimate=pl.CostEstimate(
            flops=2 * rows * k_all * depth * orbitals,
            bytes_accessed=2 * (by_r.size + coeffs.size + rows * k_all * orbitals),
            transcendentals=0,
        ),
        name="quarter",
    )(by_r, coeffs)


def half_kernel(a_ref, t_ref, out_ref):
    n_mo, pair, padded, lanes = a_ref.shape
    columns = [a_ref[:, k].reshape(n_mo * padded, lanes) for k in range(pair)]
    half = jnp.dot(
        t_ref[...], jnp.concatenate(columns, axis=1), preferred_element_type=jnp.float32
    ).astype(jnp.bfloat16)
    n_pair, _, block, _ = out_ref.shape
    for k in range(pair):
        out_ref[:, k] = half[:, k * lanes : (k + 1) * lanes].reshape(n_pair, block, lanes)


def half_of(arrived, turned, n_pair):
    n_mo, kc, padded, lanes = arrived.shape
    orbitals = turned.shape[0]
    block = orbitals // n_pair
    return pl.pallas_call(
        half_kernel,
        grid=(kc // 2,),
        out_shape=jax.ShapeDtypeStruct((n_pair, kc, block, lanes), jnp.bfloat16),
        in_specs=[
            pl.BlockSpec((n_mo, 2, padded, lanes), lambda k: (0, k, 0, 0)),
            pl.BlockSpec(turned.shape, lambda k: (0, 0)),
        ],
        out_specs=pl.BlockSpec((n_pair, 2, block, lanes), lambda k: (0, k, 0, 0)),
        compiler_params=pltpu.CompilerParams(vmem_limit_bytes=VMEM),
        cost_estimate=pl.CostEstimate(
            flops=2 * orbitals * n_mo * padded * kc * lanes,
            bytes_accessed=2 * (arrived.size + turned.size + orbitals * kc * lanes),
            transcendentals=0,
        ),
        name="half",
    )(arrived, turned)


def combine_kernel(per_step, mirror_ref, *refs):
    pieces, out_ref, held, sems = refs[:-3], refs[-3], refs[-2], refs[-1]
    step = pl.program_id(0)

    @pl.when(step == 0)
    def _():
        first = 0
        copies = []
        for c, piece in enumerate(pieces):
            kc = piece.shape[1]
            copies.append(pltpu.make_async_copy(piece, held.at[:, first : first + kc], sems.at[c]))
            first += kc
        for copy in copies:
            copy.start()
        for copy in copies:
            copy.wait()

    k_all = held.shape[1]
    for n in range(per_step):
        k = step * per_step + n
        m = mirror_ref[k]
        own = held[k // k_all, lax.rem(k, k_all)].astype(jnp.float32)
        partner = held[m // k_all, lax.rem(m, k_all)].astype(jnp.float32)
        out_ref[n] = 0.5 * (own + partner)


def combine(pieces, mirror):
    n_pair, _, block, lanes = pieces[0].shape
    k_all = sum(p.shape[1] for p in pieces)
    rows = n_pair * k_all
    per_step = max(1, 16 * 64 // block)
    return pl.pallas_call(
        functools.partial(combine_kernel, per_step),
        grid_spec=pltpu.PrefetchScalarGridSpec(
            num_scalar_prefetch=1,
            grid=(rows // per_step,),
            in_specs=[pl.BlockSpec(memory_space=pl.ANY)] * len(pieces),
            out_specs=pl.BlockSpec((per_step, block, lanes), lambda k, m: (k, 0, 0)),
            scratch_shapes=[
                pltpu.VMEM((n_pair, k_all, block, lanes), jnp.bfloat16),
                pltpu.SemaphoreType.DMA((len(pieces),)),
            ],
        ),
        out_shape=jax.ShapeDtypeStruct((rows, block, lanes), jnp.float32),
        compiler_params=pltpu.CompilerParams(vmem_limit_bytes=VMEM),
        cost_estimate=pl.CostEstimate(
            flops=2 * rows * block * lanes,
            bytes_accessed=6 * rows * block * lanes,
            transcendentals=0,
        ),
        name="combine",
    )(mirror, *pieces)


def on_device(n_pair, n_mo, integrals, coeffs, mirror):
    k_all, rows, depth = integrals.shape
    orbitals = coeffs.shape[1]
    padded = -(-rows // STEP) * STEP
    by_r = jnp.transpose(integrals, (1, 0, 2))
    turned = jnp.pad(coeffs.T.reshape(orbitals, n_mo, rows), ((0, 0), (0, 0), (0, padded - rows)))
    turned = turned.reshape(orbitals, n_mo * padded)
    pieces = []
    for quarter in quarter_of(by_r, coeffs, n_mo, padded):
        arrived = lax.all_to_all(quarter, "mo", split_axis=0, concat_axis=0, tiled=True)
        half = half_of(arrived, turned, n_pair)
        pieces.append(lax.all_to_all(half, "pair", split_axis=0, concat_axis=0, tiled=True))
    return combine(pieces, mirror)


def solution(mesh):
    return jax.shard_map(
        functools.partial(on_device, mesh.shape["pair"], mesh.shape["mo"]),
        mesh=mesh,
        in_specs=(P("pair", "mo", None), P(), P()),
        out_specs=P(None, "pair", "mo"),
        check_vma=False,
    )
```

```python
import functools

import jax
import jax.numpy as jnp
from jax import lax
from jax.experimental import pallas as pl
from jax.experimental.pallas import tpu as pltpu
from jax.sharding import PartitionSpec as P

LANES = 128
STEP = 64
CHUNKS = (4, 4, 4, 4)
VMEM = 48 * 1024 * 1024


def quarter_kernel(rows, me_ref, x_ref, c_ref, *refs):
    outs, acc = refs[:-1], refs[-1]
    step, k_all, depth = x_ref.shape
    x = x_ref[...].reshape(step * k_all, depth)
    product = jnp.dot(x, c_ref[...], preferred_element_type=jnp.float32)
    for d in range(2):
        acc[d] = product[:, d * LANES : (d + 1) * LANES]
    left = rows - pl.program_id(0) * step
    keep = lax.broadcasted_iota(jnp.int32, (step, LANES), 0) < left
    first = 0
    for c in range(len(CHUNKS)):
        for flip in range(2):
            out = outs[2 * c + flip]
            d = (me_ref[0] & 1) ^ flip
            for k in range(out.shape[0]):
                block = acc[d, pl.ds(first + k, step, stride=k_all), :]
                out[k] = jnp.where(keep, block, 0.0).astype(jnp.bfloat16)
        first += CHUNKS[c]


def quarter_of(me, by_r, coeffs, far, padded):
    rows, k_all, depth = by_r.shape
    outs = [jax.ShapeDtypeStruct((kc, padded, LANES), jnp.bfloat16) for kc in CHUNKS for _ in range(2)]
    out = pl.pallas_call(
        functools.partial(quarter_kernel, rows),
        grid_spec=pltpu.PrefetchScalarGridSpec(
            num_scalar_prefetch=1,
            grid=(padded // STEP,),
            in_specs=[
                pl.BlockSpec((STEP, k_all, depth), lambda r, me: (r, 0, 0)),
                pl.BlockSpec((depth, 2 * LANES), lambda r, me: (0, (me[0] >> 1) ^ far)),
            ],
            out_specs=[pl.BlockSpec((o.shape[0], STEP, LANES), lambda r, me: (0, r, 0)) for o in outs],
            scratch_shapes=[pltpu.VMEM((2, STEP * k_all, LANES), jnp.float32)],
        ),
        out_shape=outs,
        compiler_params=pltpu.CompilerParams(vmem_limit_bytes=VMEM),
        cost_estimate=pl.CostEstimate(
            flops=2 * rows * k_all * depth * 2 * LANES,
            bytes_accessed=2 * (by_r.size + (depth + padded * k_all) * 2 * LANES),
            transcendentals=0,
        ),
        name=f"quarter{far}",
    )(me, by_r, coeffs)
    return [out[2 * c : 2 * c + 2] for c in range(len(CHUNKS))]


def half_kernel(me_ref, *refs):
    arrived, t_ref, out_ref = refs[:-2], refs[-2], refs[-1]
    n_pair, pair, block, lanes = out_ref.shape
    half = None
    for o, a_ref in enumerate(arrived):
        columns = jnp.concatenate([a_ref[k] for k in range(pair)], axis=1)
        part = jnp.dot(t_ref[me_ref[0] ^ o], columns, preferred_element_type=jnp.float32)
        half = part if half is None else half + part
    half = half.astype(jnp.bfloat16)
    for k in range(pair):
        out_ref[:, k] = half[:, k * lanes : (k + 1) * lanes].reshape(n_pair, block, lanes)


def half_of(me, arrived, turned, n_pair):
    kc, padded, lanes = arrived[0].shape
    n_mo, orbitals, _ = turned.shape
    block = orbitals // n_pair
    return pl.pallas_call(
        half_kernel,
        grid_spec=pltpu.PrefetchScalarGridSpec(
            num_scalar_prefetch=1,
            grid=(kc // 2,),
            in_specs=[pl.BlockSpec((2, padded, lanes), lambda k, me: (k, 0, 0))] * n_mo
            + [pl.BlockSpec(turned.shape, lambda k, me: (0, 0, 0))],
            out_specs=pl.BlockSpec((n_pair, 2, block, lanes), lambda k, me: (0, k, 0, 0)),
        ),
        out_shape=jax.ShapeDtypeStruct((n_pair, kc, block, lanes), jnp.bfloat16),
        compiler_params=pltpu.CompilerParams(vmem_limit_bytes=VMEM),
        cost_estimate=pl.CostEstimate(
            flops=2 * orbitals * n_mo * padded * kc * lanes,
            bytes_accessed=2 * (n_mo * arrived[0].size + turned.size + orbitals * kc * lanes),
            transcendentals=0,
        ),
        name="half",
    )(me, *arrived, turned)


def combine_kernel(per_step, mirror_ref, *refs):
    pieces, out_ref, held, sems = refs[:-3], refs[-3], refs[-2], refs[-1]
    step = pl.program_id(0)

    @pl.when(step == 0)
    def _():
        first = 0
        copies = []
        for c, piece in enumerate(pieces):
            kc = piece.shape[1]
            copies.append(pltpu.make_async_copy(piece, held.at[:, first : first + kc], sems.at[c]))
            first += kc
        for copy in copies:
            copy.start()
        for copy in copies:
            copy.wait()

    k_all = held.shape[1]
    for n in range(per_step):
        k = step * per_step + n
        m = mirror_ref[k]
        own = held[k // k_all, lax.rem(k, k_all)].astype(jnp.float32)
        partner = held[m // k_all, lax.rem(m, k_all)].astype(jnp.float32)
        out_ref[n] = 0.5 * (own + partner)


def combine(pieces, mirror):
    n_pair, _, block, lanes = pieces[0].shape
    k_all = sum(p.shape[1] for p in pieces)
    rows = n_pair * k_all
    per_step = max(1, 32 * 64 // block)
    return pl.pallas_call(
        functools.partial(combine_kernel, per_step),
        grid_spec=pltpu.PrefetchScalarGridSpec(
            num_scalar_prefetch=1,
            grid=(rows // per_step,),
            in_specs=[pl.BlockSpec(memory_space=pl.ANY)] * len(pieces),
            out_specs=pl.BlockSpec((per_step, block, lanes), lambda k, m: (k, 0, 0)),
            scratch_shapes=[
                pltpu.VMEM((n_pair, k_all, block, lanes), jnp.bfloat16),
                pltpu.SemaphoreType.DMA((len(pieces),)),
            ],
        ),
        out_shape=jax.ShapeDtypeStruct((rows, block, lanes), jnp.float32),
        compiler_params=pltpu.CompilerParams(vmem_limit_bytes=VMEM),
        cost_estimate=pl.CostEstimate(
            flops=2 * rows * block * lanes,
            bytes_accessed=6 * rows * block * lanes,
            transcendentals=0,
        ),
        name="combine",
    )(mirror, *pieces)


def flipped(x, axis, size, offset):
    if offset == 0:
        return x
    return lax.ppermute(x, axis, [(i, i ^ offset) for i in range(size)])


def on_device(n_pair, n_mo, integrals, coeffs, mirror):
    k_all, rows, depth = integrals.shape
    orbitals = coeffs.shape[1]
    padded = -(-rows // STEP) * STEP
    by_r = jnp.transpose(integrals, (1, 0, 2))
    me = lax.axis_index("mo").astype(jnp.int32).reshape(1)
    turned = jnp.pad(coeffs.reshape(n_mo, rows, orbitals), ((0, 0), (0, padded - rows), (0, 0)))
    turned = jnp.transpose(turned, (0, 2, 1))
    quarters = [[None] * n_mo for _ in CHUNKS]
    for far in reversed(range(n_mo // 2)):
        for c, blocks in enumerate(quarter_of(me, by_r, coeffs, far, padded)):
            quarters[c][2 * far : 2 * far + 2] = blocks
    pieces = []
    for blocks in quarters:
        arrived = [flipped(b, "mo", n_mo, o) for o, b in enumerate(blocks)]
        half = half_of(me, arrived, turned, n_pair)
        pieces.append(lax.all_to_all(half, "pair", split_axis=0, concat_axis=0, tiled=True))
    return combine(pieces, mirror)


def solution(mesh):
    return jax.shard_map(
        functools.partial(on_device, mesh.shape["pair"], mesh.shape["mo"]),
        mesh=mesh,
        in_specs=(P("pair", "mo", None), P(), P()),
        out_specs=P(None, "pair", "mo"),
        check_vma=False,
    )
```

```python
import functools

import jax
import jax.numpy as jnp
from jax import lax
from jax.experimental import pallas as pl
from jax.experimental.pallas import tpu as pltpu
from jax.sharding import PartitionSpec as P

LANES = 128
STEP = 64
CHUNKS = (4, 4, 4, 4)
VMEM = 24 * 1024 * 1024


def quarter_kernel(rows, place_ref, x_ref, c_ref, *refs):
    outs, acc = refs[:-1], refs[-1]
    step, k_all, depth = x_ref.shape
    x = x_ref[...].reshape(step * k_all, depth)
    product = jnp.dot(x, c_ref[...], preferred_element_type=jnp.float32)
    for d in range(2):
        acc[d] = product[:, d * LANES : (d + 1) * LANES]
    left = rows - pl.program_id(0) * step
    keep = lax.broadcasted_iota(jnp.int32, (step, LANES), 0) < left
    first = 0
    for c in range(len(CHUNKS)):
        for flip in range(2):
            out = outs[2 * c + flip]
            d = (place_ref[0] & 1) ^ flip
            for k in range(out.shape[0]):
                block = acc[d, pl.ds(first + k, step, stride=k_all), :]
                out[k] = jnp.where(keep, block, 0.0).astype(jnp.bfloat16)
        first += CHUNKS[c]


def quarter_of(place, by_r, coeffs, far, padded):
    rows, k_all, depth = by_r.shape
    outs = [jax.ShapeDtypeStruct((kc, padded, LANES), jnp.bfloat16) for kc in CHUNKS for _ in range(2)]
    out = pl.pallas_call(
        functools.partial(quarter_kernel, rows),
        grid_spec=pltpu.PrefetchScalarGridSpec(
            num_scalar_prefetch=1,
            grid=(padded // STEP,),
            in_specs=[
                pl.BlockSpec((STEP, k_all, depth), lambda r, place: (r, 0, 0)),
                pl.BlockSpec((depth, 2 * LANES), lambda r, place: (0, (place[0] >> 1) ^ far)),
            ],
            out_specs=[pl.BlockSpec((o.shape[0], STEP, LANES), lambda r, place: (0, r, 0)) for o in outs],
            scratch_shapes=[pltpu.VMEM((2, STEP * k_all, LANES), jnp.float32)],
        ),
        out_shape=outs,
        compiler_params=pltpu.CompilerParams(vmem_limit_bytes=VMEM),
        cost_estimate=pl.CostEstimate(
            flops=2 * rows * k_all * depth * 2 * LANES,
            bytes_accessed=2 * (by_r.size + (depth + padded * k_all) * 2 * LANES),
            transcendentals=0,
        ),
        name=f"quarter{far}",
    )(place, by_r, coeffs)
    return [out[2 * c : 2 * c + 2] for c in range(len(CHUNKS))]


def half_kernel(n_mo, place_ref, *refs):
    arrived, t_ref, outs, held = refs[:n_mo], refs[n_mo], refs[n_mo + 1 : -1], refs[-1]
    pair, block, lanes = outs[0].shape
    half = None
    for o, a_ref in enumerate(arrived):
        columns = jnp.concatenate([a_ref[k] for k in range(pair)], axis=1)
        part = jnp.dot(t_ref[place_ref[0] ^ o], columns, preferred_element_type=jnp.float32)
        half = part if half is None else half + part
    held[...] = half
    for o, out in enumerate(outs):
        start = pl.multiple_of((place_ref[1] ^ o) * block, block)
        for k in range(pair):
            out[k] = held[pl.ds(start, block), k * lanes : (k + 1) * lanes].astype(jnp.bfloat16)


def half_of(place, arrived, turned, n_pair):
    kc, padded, lanes = arrived[0].shape
    n_mo, orbitals, _ = turned.shape
    block = orbitals // n_pair
    return pl.pallas_call(
        functools.partial(half_kernel, n_mo),
        grid_spec=pltpu.PrefetchScalarGridSpec(
            num_scalar_prefetch=1,
            grid=(kc // 2,),
            in_specs=[pl.BlockSpec((2, padded, lanes), lambda k, place: (k, 0, 0))] * n_mo
            + [pl.BlockSpec(turned.shape, lambda k, place: (0, 0, 0))],
            out_specs=[pl.BlockSpec((2, block, lanes), lambda k, place: (k, 0, 0))] * n_pair,
            scratch_shapes=[pltpu.VMEM((orbitals, 2 * lanes), jnp.float32)],
        ),
        out_shape=[jax.ShapeDtypeStruct((kc, block, lanes), jnp.bfloat16)] * n_pair,
        compiler_params=pltpu.CompilerParams(vmem_limit_bytes=VMEM),
        cost_estimate=pl.CostEstimate(
            flops=2 * orbitals * n_mo * padded * kc * lanes,
            bytes_accessed=2 * (n_mo * arrived[0].size + turned.size + orbitals * kc * lanes),
            transcendentals=0,
        ),
        name="half",
    )(place, *arrived, turned)


def combine_kernel(n_pair, per_step, mirror_ref, place_ref, *refs):
    pieces, out_ref, held, sems = refs[:-3], refs[-3], refs[-2], refs[-1]
    step = pl.program_id(0)

    @pl.when(step == 0)
    def _():
        copies = []
        first = 0
        for n, piece in enumerate(pieces):
            source, kc = place_ref[1] ^ (n % n_pair), piece.shape[0]
            copies.append(pltpu.make_async_copy(piece, held.at[source, first : first + kc], sems.at[n]))
            if n % n_pair == n_pair - 1:
                first += kc
        for copy in copies:
            copy.start()
        for copy in copies:
            copy.wait()

    k_all = held.shape[1]
    for n in range(per_step):
        k = step * per_step + n
        m = mirror_ref[k]
        own = held[k // k_all, lax.rem(k, k_all)].astype(jnp.float32)
        partner = held[m // k_all, lax.rem(m, k_all)].astype(jnp.float32)
        out_ref[n] = 0.5 * (own + partner)


def combine(pieces, mirror, place, n_pair):
    _, block, lanes = pieces[0].shape
    k_all = sum(p.shape[0] for p in pieces) // n_pair
    rows = n_pair * k_all
    per_step = max(1, 32 * 64 // block)
    return pl.pallas_call(
        functools.partial(combine_kernel, n_pair, per_step),
        grid_spec=pltpu.PrefetchScalarGridSpec(
            num_scalar_prefetch=2,
            grid=(rows // per_step,),
            in_specs=[pl.BlockSpec(memory_space=pl.ANY)] * len(pieces),
            out_specs=pl.BlockSpec((per_step, block, lanes), lambda k, m, place: (k, 0, 0)),
            scratch_shapes=[
                pltpu.VMEM((n_pair, k_all, block, lanes), jnp.bfloat16),
                pltpu.SemaphoreType.DMA((len(pieces),)),
            ],
        ),
        out_shape=jax.ShapeDtypeStruct((rows, block, lanes), jnp.float32),
        compiler_params=pltpu.CompilerParams(vmem_limit_bytes=VMEM),
        cost_estimate=pl.CostEstimate(
            flops=2 * rows * block * lanes,
            bytes_accessed=6 * rows * block * lanes,
            transcendentals=0,
        ),
        name="combine",
    )(mirror, place, *pieces)


def flipped(x, axis, size, offset):
    if offset == 0:
        return x
    return lax.ppermute(x, axis, [(i, i ^ offset) for i in range(size)])


def on_device(n_pair, n_mo, integrals, coeffs, mirror):
    k_all, rows, depth = integrals.shape
    orbitals = coeffs.shape[1]
    padded = -(-rows // STEP) * STEP
    by_r = jnp.transpose(integrals, (1, 0, 2))
    place = jnp.stack([lax.axis_index("mo"), lax.axis_index("pair")]).astype(jnp.int32)
    turned = jnp.pad(coeffs.reshape(n_mo, rows, orbitals), ((0, 0), (0, padded - rows), (0, 0)))
    turned = jnp.transpose(turned, (0, 2, 1))
    quarters = [[None] * n_mo for _ in CHUNKS]
    for far in reversed(range(n_mo // 2)):
        for c, blocks in enumerate(quarter_of(place, by_r, coeffs, far, padded)):
            quarters[c][2 * far : 2 * far + 2] = blocks
    pieces = []
    for blocks in quarters:
        arrived = [flipped(b, "mo", n_mo, o) for o, b in enumerate(blocks)]
        half = half_of(place, arrived, turned, n_pair)
        pieces += [flipped(h, "pair", n_pair, o) for o, h in enumerate(half)]
    return combine(pieces, mirror, place, n_pair)


def solution(mesh):
    return jax.shard_map(
        functools.partial(on_device, mesh.shape["pair"], mesh.shape["mo"]),
        mesh=mesh,
        in_specs=(P("pair", "mo", None), P(), P()),
        out_specs=P(None, "pair", "mo"),
        check_vma=False,
    )
```

```python
import functools

import jax
import jax.numpy as jnp
from jax import lax
from jax.experimental import pallas as pl
from jax.experimental.pallas import tpu as pltpu
from jax.sharding import PartitionSpec as P

LANES = 128
STEP = 64
CHUNKS = (4, 4, 4, 4)
GROUPS = ((0, 1), (2,), (3,))
MIB = 1024 * 1024
CHEAP = pl.CostEstimate(flops=1024, bytes_accessed=1024, transcendentals=0)
IN_VMEM = pl.BlockSpec(memory_space=pltpu.VMEM)
IN_SMEM = pl.BlockSpec(memory_space=pltpu.SMEM)
ANYWHERE = pl.BlockSpec(memory_space=pl.ANY)
IN_HBM = pl.BlockSpec(memory_space=pltpu.MemorySpace.HBM)


def quarter_kernel(rows, far, n_later, place_ref, x_ref, c_hbm, *refs):
    refs = refs[2 * n_later :]
    outs, (acc, c_ref, held, c_sem, sems) = refs[:-5], refs[-5:]
    at = pl.program_id(0)
    step, k_all, depth = x_ref.shape
    padded = held.shape[2]

    @pl.when(at == 0)
    def _():
        first = pl.multiple_of(((place_ref[0] >> 1) ^ far) * 2 * LANES, 2 * LANES)
        copy = pltpu.make_async_copy(c_hbm.at[:, pl.ds(first, 2 * LANES)], c_ref, c_sem)
        copy.start()
        copy.wait()

    x = x_ref[...].reshape(step * k_all, depth)
    product = jnp.dot(x, c_ref[...], preferred_element_type=jnp.float32)
    for d in range(2):
        acc[d] = product[:, d * LANES : (d + 1) * LANES]
    here = pl.ds(pl.multiple_of(at * step, step), step)
    keep = lax.broadcasted_iota(jnp.int32, (step, LANES), 0) < rows - at * step
    first = 0
    for n, out in enumerate(outs):
        d = (place_ref[0] & 1) ^ (n & 1)
        kc = out.shape[0]
        for k in range(first, first + kc):
            block = acc[d, pl.ds(k, step, stride=k_all), :]
            held[n & 1, k, here] = jnp.where(keep, block, 0.0).astype(jnp.bfloat16)
        mine = held.at[n & 1, pl.ds(first, kc)]
        pltpu.make_async_copy(mine.at[:, here], out.at[:, here], sems.at[n]).start()
        if n & 1:
            first += kc

    @pl.when(at == padded // step - 1)
    def _():
        first = 0
        for n, out in enumerate(outs):
            kc = out.shape[0]
            pltpu.make_async_copy(held.at[n & 1, pl.ds(first, kc)], out, sems.at[n]).wait()
            if n & 1:
                first += kc


def quarter_of(place, by_r, coeffs, far, padded, chunks, later=()):
    rows, k_all, depth = by_r.shape
    outs = [jax.ShapeDtypeStruct((kc, padded, LANES), jnp.bfloat16) for kc in chunks for _ in range(2)]
    out = pl.pallas_call(
        functools.partial(quarter_kernel, rows, far, len(later)),
        grid_spec=pltpu.PrefetchScalarGridSpec(
            num_scalar_prefetch=1,
            grid=(padded // STEP,),
            in_specs=[pl.BlockSpec((STEP, k_all, depth), lambda r, place: (r, 0, 0))]
            + [IN_HBM] * (1 + len(later)),
            out_specs=[IN_HBM] * (len(later) + len(outs)),
            scratch_shapes=[
                pltpu.VMEM((2, STEP * k_all, LANES), jnp.float32),
                pltpu.VMEM((depth, 2 * LANES), jnp.bfloat16),
                pltpu.VMEM((2, k_all, padded, LANES), jnp.bfloat16),
                pltpu.SemaphoreType.DMA,
                pltpu.SemaphoreType.DMA((len(outs),)),
            ],
        ),
        out_shape=[jax.ShapeDtypeStruct(x.shape, x.dtype) for x in later] + outs,
        input_output_aliases={3 + n: n for n in range(len(later))},
        compiler_params=pltpu.CompilerParams(vmem_limit_bytes=50 * MIB),
        cost_estimate=CHEAP,
        name=f"quarter{far}",
    )(place, by_r, coeffs, *later)
    n = len(later)
    return list(out[:n]), list(out[n:])


def turn_kernel(rows, c_ref, out_ref):
    n_mo, orbitals, padded = out_ref.shape
    none = jnp.zeros((padded - rows, orbitals), jnp.float32)
    for n in range(n_mo):
        part = c_ref[n * rows : (n + 1) * rows, :].astype(jnp.float32)
        out_ref[n] = jnp.concatenate([part, none], axis=0).T.astype(jnp.bfloat16)


def turn(coeffs, n_mo, padded):
    depth, orbitals = coeffs.shape
    return pl.pallas_call(
        functools.partial(turn_kernel, depth // n_mo),
        in_specs=[IN_VMEM],
        out_specs=IN_VMEM,
        out_shape=jax.ShapeDtypeStruct((n_mo, orbitals, padded), jnp.bfloat16),
        compiler_params=pltpu.CompilerParams(vmem_limit_bytes=24 * MIB),
        cost_estimate=CHEAP,
        name="turn",
    )(coeffs)


def half_kernel(first, n_mo, n_near, place_ref, *refs):
    blocks, t_ref, refs = refs[:n_mo], refs[n_mo], refs[n_mo + 1 :]
    far, near, held = refs[-n_near - 2], refs[-n_near - 1 : -1], refs[-1]
    kc, block, lanes = near[0].shape
    for k in range(0, kc, 2):
        half = None
        for o, a_ref in enumerate(blocks):
            at = k if a_ref.shape[0] == kc else first + k
            columns = jnp.concatenate([a_ref[at], a_ref[at + 1]], axis=1)
            part = jnp.dot(t_ref[place_ref[0] ^ o], columns, preferred_element_type=jnp.float32)
            half = part if half is None else half + part
        held[...] = half
        for o in range(2 * n_near):
            start = pl.multiple_of((place_ref[1] ^ o) * block, block)
            for n in range(2):
                piece = held[pl.ds(start, block), n * lanes : (n + 1) * lanes].astype(jnp.bfloat16)
                if o < n_near:
                    near[o][k + n] = piece
                else:
                    far[o - n_near, k + n] = piece


def half_of(place, blocks, turned, n_pair, first, kc, later, after):
    n_mo, orbitals, padded = turned.shape
    lanes = blocks[0].shape[-1]
    block, n_near = orbitals // n_pair, n_pair // 2
    piece = jax.ShapeDtypeStruct((kc, block, lanes), jnp.bfloat16)
    far = jax.ShapeDtypeStruct((n_near, *piece.shape), jnp.bfloat16)
    out = pl.pallas_call(
        functools.partial(half_kernel, first, n_mo, n_near),
        in_specs=[IN_SMEM]
        + [IN_VMEM] * (n_mo + 1)
        + [IN_HBM] * len(later)
        + [ANYWHERE] * len(after),
        out_specs=[IN_HBM] * len(later) + [IN_VMEM] * (1 + n_near),
        out_shape=[jax.ShapeDtypeStruct(x.shape, x.dtype) for x in later] + [far] + [piece] * n_near,
        scratch_shapes=[pltpu.VMEM((orbitals, 2 * lanes), jnp.float32)],
        input_output_aliases={n_mo + 2 + n: n for n in range(len(later))},
        compiler_params=pltpu.CompilerParams(vmem_limit_bytes=24 * MIB),
        cost_estimate=CHEAP,
        name="half",
    )(place, *blocks, turned, *later, *after)
    n = len(later)
    return out[:n], out[n], out[n + 1 :]


def merge_kernel(n_near, n_chunks, *refs):
    near, far, outs = refs[: n_chunks * (n_near - 1)], refs[n_chunks * (n_near - 1) :], refs[1 - n_near :]
    for o, out in enumerate(outs, 1):
        at = 0
        for c in range(n_chunks):
            x = near[c * (n_near - 1) + o - 1]
            out[at : at + x.shape[0]] = x[...]
            at += x.shape[0]
        for c in range(n_chunks):
            kc = far[c].shape[1]
            out[at : at + kc] = far[c][o]
            at += kc


def merge(near, far, after):
    n_near, _, block, lanes = far[0].shape
    size = 2 * sum(x.shape[1] for x in far)
    parts = [x for chunk in near for x in chunk[1:]]
    return pl.pallas_call(
        functools.partial(merge_kernel, n_near, len(far)),
        in_specs=[IN_VMEM] * (len(parts) + len(far)) + [ANYWHERE] * len(after),
        out_specs=[IN_VMEM] * (n_near - 1),
        out_shape=[jax.ShapeDtypeStruct((size, block, lanes), jnp.bfloat16)] * (n_near - 1),
        compiler_params=pltpu.CompilerParams(vmem_limit_bytes=24 * MIB),
        cost_estimate=CHEAP,
        name="merge",
    )(*parts, *far, *after)


def combine_kernel(sources, per_step, mirror_ref, place_ref, *refs):
    pieces, out_ref, held = refs[:-2], refs[-2], refs[-1]
    step = pl.program_id(0)

    @pl.when(step == 0)
    def _():
        for piece, parts in zip(pieces, sources):
            for offset, at, first, kc in parts:
                held[place_ref[1] ^ offset, first : first + kc] = piece[...] if at is None else piece[at]

    k_all = held.shape[1]
    for n in range(per_step):
        k = step * per_step + n
        m = mirror_ref[k]
        own = held[k // k_all, lax.rem(k, k_all)].astype(jnp.float32)
        partner = held[m // k_all, lax.rem(m, k_all)].astype(jnp.float32)
        out_ref[n] = 0.5 * (own + partner)


def combine(pieces, sources, mirror, place, n_pair):
    _, block, lanes = pieces[0].shape
    k_all = sum(CHUNKS)
    rows = n_pair * k_all
    per_step = max(1, 32 * 64 // block)
    return pl.pallas_call(
        functools.partial(combine_kernel, sources, per_step),
        grid_spec=pltpu.PrefetchScalarGridSpec(
            num_scalar_prefetch=2,
            grid=(rows // per_step,),
            in_specs=[IN_VMEM] * len(pieces),
            out_specs=pl.BlockSpec((per_step, block, lanes), lambda k, m, place: (k, 0, 0)),
            scratch_shapes=[pltpu.VMEM((n_pair, k_all, block, lanes), jnp.bfloat16)],
        ),
        out_shape=jax.ShapeDtypeStruct((rows, block, lanes), jnp.float32),
        compiler_params=pltpu.CompilerParams(vmem_limit_bytes=24 * MIB),
        cost_estimate=CHEAP,
        name="combine",
    )(mirror, place, *pieces)


def flipped(x, axis, size, offset):
    return lax.ppermute(x, axis, [(i, i ^ offset) for i in range(size)])


def on_device(n_pair, n_mo, integrals, coeffs, mirror):
    k_all, rows, depth = integrals.shape
    orbitals = coeffs.shape[1]
    padded = -(-rows // STEP) * STEP
    n_near = n_pair // 2
    by_r = jnp.transpose(integrals, (1, 0, 2))
    place = jnp.stack([lax.axis_index("mo"), lax.axis_index("pair")]).astype(jnp.int32)
    turned = turn(coeffs, n_mo, padded)
    _, queue = quarter_of(place, by_r, coeffs, 1, padded, CHUNKS)
    queue[2:3], (own, beside) = quarter_of(place, by_r, coeffs, 0, padded, (k_all,), queue[2:3])
    beside = flipped(beside, "mo", n_mo, 1)

    firsts = [sum(CHUNKS[:c]) for c in range(len(CHUNKS))]
    pieces, sources, near, far = [], [], {}, {}
    for c, kc in enumerate(CHUNKS):
        across = [flipped(x, "mo", n_mo, 2 + n) for n, x in enumerate(queue[2 * c : 2 * c + 2])]
        coming = slice(2 * c + 3, 2 * c + 5)
        after = [far[c - 2]] if c >= 2 else []
        queue[coming], out, near[c] = half_of(
            place, [own, beside, *across], turned, n_pair, firsts[c], kc, queue[coming], after
        )
        far[c] = flipped(out, "pair", n_pair, n_near)
        pieces += [near[c][0], far[c]]
        sources += [((0, None, firsts[c], kc),), ((n_near, 0, firsts[c], kc),)]
    after = []
    for group in GROUPS:
        start, size = firsts[group[0]], sum(CHUNKS[c] for c in group)
        messages = merge([near[c] for c in group], [far[c] for c in group], after)
        after = [flipped(x, "pair", n_pair, o) for o, x in enumerate(messages, 1)]
        pieces += after
        for o in range(1, n_near):
            sources.append(((o, slice(0, size), start, size), (o ^ n_near, slice(size, 2 * size), start, size)))
    return combine(pieces, sources, mirror, place, n_pair)


def solution(mesh):
    return jax.shard_map(
        functools.partial(on_device, mesh.shape["pair"], mesh.shape["mo"]),
        mesh=mesh,
        in_specs=(P("pair", "mo", None), P(), P()),
        out_specs=P(None, "pair", "mo"),
        check_vma=False,
    )
```

```python
import functools

import jax
import jax.numpy as jnp
from jax import lax
from jax.experimental import pallas as pl
from jax.experimental.pallas import tpu as pltpu
from jax.sharding import PartitionSpec as P

LANES = 128
STEP = 64
CHUNKS = (4, 4, 4, 4)
PART = 256
ROWS_IN_TILE = 8
ALONG = 3
MIB = 1024 * 1024
COST = pl.CostEstimate(flops=1024, bytes_accessed=1024, transcendentals=0)
IN_VMEM = pl.BlockSpec(memory_space=pltpu.VMEM)
IN_SMEM = pl.BlockSpec(memory_space=pltpu.SMEM)
ANYWHERE = pl.BlockSpec(memory_space=pl.ANY)
IN_HBM = pl.BlockSpec(memory_space=pltpu.MemorySpace.HBM)


def quarter_kernel(rows, far, n_after, place_ref, x_ref, c_hbm, *refs):
    refs = refs[n_after:]
    outs, (acc, c_ref, held, c_sem, sems) = refs[:-5], refs[-5:]
    at = pl.program_id(0)
    step, k_all, depth = x_ref.shape
    padded = held.shape[2]
    across = ALONG * step + 1

    @pl.when(at == 0)
    def _():
        first = pl.multiple_of(((place_ref[0] >> 1) ^ far) * 2 * LANES, 2 * LANES)
        copy = pltpu.make_async_copy(c_hbm.at[:, pl.ds(first, 2 * LANES)], c_ref, c_sem)
        copy.start()
        copy.wait()

    many = PART // k_all
    for r in range(0, step, many):
        x = x_ref[r : r + many].reshape(PART, depth)
        product = jnp.dot(x, c_ref[...], preferred_element_type=jnp.float32)
        for n in range(many):
            for k in range(0, k_all, ROWS_IN_TILE):
                line = n * k_all + k
                rows_at = pl.ds(k * across + (r + n) * ALONG, ROWS_IN_TILE, stride=across)
                for d in range(2):
                    acc[d, rows_at, :] = product[line : line + ROWS_IN_TILE, d * LANES : (d + 1) * LANES]
    here = pl.ds(pl.multiple_of(at * step, step), step)
    keep = lax.broadcasted_iota(jnp.int32, (step, LANES), 0) < rows - at * step
    first = 0
    for n, out in enumerate(outs):
        d = (place_ref[0] & 1) ^ (n & 1)
        kc = out.shape[0]
        for k in range(first, first + kc):
            block = acc[d, pl.ds(k * across, step, stride=ALONG), :]
            held[n & 1, k, here] = jnp.where(keep, block, 0.0).astype(jnp.bfloat16)
        mine = held.at[n & 1, pl.ds(first, kc)]
        pltpu.make_async_copy(mine.at[:, here], out.at[:, here], sems.at[n]).start()
        if n & 1:
            first += kc

    @pl.when(at == padded // step - 1)
    def _():
        first = 0
        for n, out in enumerate(outs):
            kc = out.shape[0]
            pltpu.make_async_copy(held.at[n & 1, pl.ds(first, kc)], out, sems.at[n]).wait()
            if n & 1:
                first += kc


def quarter_of(place, by_r, coeffs, far, padded, chunks, after=()):
    rows, k_all, depth = by_r.shape
    outs = [jax.ShapeDtypeStruct((kc, padded, LANES), jnp.bfloat16) for kc in chunks for _ in range(2)]
    out = pl.pallas_call(
        functools.partial(quarter_kernel, rows, far, len(after)),
        grid_spec=pltpu.PrefetchScalarGridSpec(
            num_scalar_prefetch=1,
            grid=(padded // STEP,),
            in_specs=[pl.BlockSpec((STEP, k_all, depth), lambda r, place: (r, 0, 0))]
            + [IN_HBM]
            + [ANYWHERE] * len(after),
            out_specs=[IN_HBM] * len(outs),
            scratch_shapes=[
                pltpu.VMEM((2, (ALONG * STEP + 1) * k_all, LANES), jnp.float32),
                pltpu.VMEM((depth, 2 * LANES), jnp.bfloat16),
                pltpu.VMEM((2, k_all, padded, LANES), jnp.bfloat16),
                pltpu.SemaphoreType.DMA,
                pltpu.SemaphoreType.DMA((len(outs),)),
            ],
        ),
        out_shape=outs,
        compiler_params=pltpu.CompilerParams(vmem_limit_bytes=50 * MIB),
        cost_estimate=COST,
        name=f"quarter{far}",
    )(place, by_r, coeffs, *after)
    return list(out)


def turn_kernel(rows, c_ref, out_ref):
    n_mo, orbitals, padded = out_ref.shape
    none = jnp.zeros((padded - rows, orbitals), jnp.float32)
    for n in range(n_mo):
        part = c_ref[n * rows : (n + 1) * rows, :].astype(jnp.float32)
        out_ref[n] = jnp.concatenate([part, none], axis=0).T.astype(jnp.bfloat16)


def turn(coeffs, n_mo, padded):
    depth, orbitals = coeffs.shape
    return pl.pallas_call(
        functools.partial(turn_kernel, depth // n_mo),
        in_specs=[IN_VMEM],
        out_specs=IN_VMEM,
        out_shape=jax.ShapeDtypeStruct((n_mo, orbitals, padded), jnp.bfloat16),
        compiler_params=pltpu.CompilerParams(vmem_limit_bytes=24 * MIB),
        cost_estimate=COST,
        name="turn",
    )(coeffs)


def half_kernel(n_mo, place_ref, *refs):
    blocks, t_ref, (keep, send, held) = refs[:n_mo], refs[n_mo], refs[-3:]
    _, near, kc, block, lanes = keep.shape
    for k in range(0, kc, 2):
        half = None
        for o, a_ref in enumerate(blocks):
            columns = jnp.concatenate([a_ref[k], a_ref[k + 1]], axis=1)
            part = jnp.dot(t_ref[place_ref[0] ^ o], columns, preferred_element_type=jnp.float32)
            half = part if half is None else half + part
        held[...] = half
        for o in range(2 * near):
            start = pl.multiple_of((place_ref[1] ^ o) * block, block)
            for n in range(2):
                piece = held[pl.ds(start, block), n * lanes : (n + 1) * lanes].astype(jnp.bfloat16)
                if o < near:
                    keep[0, o, k + n] = piece
                else:
                    send[0, o - near, k + n] = piece


def half_of(place, blocks, turned, n_pair, after):
    n_mo, orbitals, _ = turned.shape
    kc, _, lanes = blocks[0].shape
    block, near = orbitals // n_pair, n_pair // 2
    return pl.pallas_call(
        functools.partial(half_kernel, n_mo),
        in_specs=[IN_SMEM] + [IN_VMEM] * (n_mo + 1) + [ANYWHERE] * len(after),
        out_specs=[IN_VMEM] * 2,
        out_shape=[jax.ShapeDtypeStruct((1, near, kc, block, lanes), jnp.bfloat16)] * 2,
        scratch_shapes=[pltpu.VMEM((orbitals, 2 * lanes), jnp.float32)],
        compiler_params=pltpu.CompilerParams(vmem_limit_bytes=24 * MIB),
        cost_estimate=COST,
        name="half",
    )(place, *blocks, turned, *after)


def merge_kernel(n, flip, *refs):
    at = 0
    for x in refs[:n]:
        for i in range(x.shape[0]):
            refs[-1][at] = x[i, flip : 2 * flip]
            at += 1


def merge(parts, flip, after):
    shape = (sum(x.shape[0] for x in parts), flip, *parts[0].shape[2:])
    return pl.pallas_call(
        functools.partial(merge_kernel, len(parts), flip),
        in_specs=[IN_VMEM] * len(parts) + [ANYWHERE] * len(after),
        out_specs=IN_VMEM,
        out_shape=jax.ShapeDtypeStruct(shape, jnp.bfloat16),
        compiler_params=pltpu.CompilerParams(vmem_limit_bytes=24 * MIB),
        cost_estimate=COST,
        name=f"merge{flip}",
    )(*parts, *after)


def combine_kernel(sources, per_step, mirror_ref, place_ref, *refs):
    pieces, out_ref, held = refs[:-2], refs[-2], refs[-1]
    step = pl.program_id(0)

    @pl.when(step == 0)
    def _():
        for piece, (offsets, first) in zip(pieces, sources):
            for n, offset in enumerate(offsets):
                held[place_ref[1] ^ offset, first : first + piece.shape[2]] = piece[n, 0]

    k_all = held.shape[1]
    for n in range(per_step):
        k = step * per_step + n
        m = mirror_ref[k]
        own = held[k // k_all, lax.rem(k, k_all)].astype(jnp.float32)
        partner = held[m // k_all, lax.rem(m, k_all)].astype(jnp.float32)
        out_ref[n] = 0.5 * (own + partner)


def combine(pieces, sources, mirror, place, n_pair):
    block, lanes = pieces[0].shape[-2:]
    k_all = sum(CHUNKS)
    rows = n_pair * k_all
    per_step = max(1, 32 * 64 // block)
    return pl.pallas_call(
        functools.partial(combine_kernel, sources, per_step),
        grid_spec=pltpu.PrefetchScalarGridSpec(
            num_scalar_prefetch=2,
            grid=(rows // per_step,),
            in_specs=[IN_VMEM] * len(pieces),
            out_specs=pl.BlockSpec((per_step, block, lanes), lambda k, m, place: (k, 0, 0)),
            scratch_shapes=[pltpu.VMEM((n_pair, k_all, block, lanes), jnp.bfloat16)],
        ),
        out_shape=jax.ShapeDtypeStruct((rows, block, lanes), jnp.float32),
        compiler_params=pltpu.CompilerParams(vmem_limit_bytes=24 * MIB),
        cost_estimate=COST,
        name="combine",
    )(mirror, place, *pieces)


def flipped(x, axis, size, offset, name):
    with jax.named_scope(name):
        return lax.ppermute(x, axis, [(i, i ^ offset) for i in range(size)])


def on_device(n_pair, n_mo, integrals, coeffs, mirror):
    rows = integrals.shape[1]
    padded = -(-rows // STEP) * STEP
    n_near = n_pair // 2
    by_r = jnp.transpose(integrals, (1, 0, 2))
    place = jnp.stack([lax.axis_index("mo"), lax.axis_index("pair")]).astype(jnp.int32)
    turned = turn(coeffs, n_mo, padded)
    queue = quarter_of(place, by_r, coeffs, 1, padded, CHUNKS)
    arrived = [flipped(x, "mo", n_mo, 2 + (m & 1), f"y{m}") for m, x in enumerate(queue)]
    near = quarter_of(place, by_r, coeffs, 0, padded, CHUNKS, queue[:1])
    beside = [flipped(x, "mo", n_mo, 1, f"beside{c}") for c, x in enumerate(near[1::2])]

    n_chunks = len(CHUNKS)
    firsts = [sum(CHUNKS[:c]) for c in range(n_chunks)]
    flips = [1 << n for n in reversed(range(n_pair.bit_length() - 1))]
    parts, offsets, halves, messages = [], [], [], [[] for _ in flips]
    for t in range(n_chunks + len(flips)):
        for level, flip in enumerate(flips):
            c = t - level
            if not 0 <= c < n_chunks:
                continue
            if level == 0:
                blocks = [near[2 * c], beside[c], *arrived[2 * c : 2 * c + 2]]
                after = [m[-1] for m in messages[1:] if m]
                keep, message = half_of(place, blocks, turned, n_pair, after)
                parts.append([keep])
                offsets.append([[0]])
            else:
                after = [messages[level - 1][-1]] if c + 1 < n_chunks else []
                if flip == 1 and c:
                    after.append(parts[c - 1][-1])
                message = merge(parts[c], flip, after)
            messages[level].append(message)
            offsets[c].append([o ^ flip for group in offsets[c] for o in group])
            parts[c].append(flipped(message, "pair", n_pair, flip, f"z{flip}c{c}"))
    pieces = [x for chunk in parts for x in chunk]
    sources = [(tuple(group), first) for chunk, first in zip(offsets, firsts) for group in chunk]
    return combine(pieces, sources, mirror, place, n_pair)


def solution(mesh):
    return jax.shard_map(
        functools.partial(on_device, mesh.shape["pair"], mesh.shape["mo"]),
        mesh=mesh,
        in_specs=(P("pair", "mo", None), P(), P()),
        out_specs=P(None, "pair", "mo"),
        check_vma=False,
    )
```

```python
import functools

import jax
import jax.numpy as jnp
from jax import lax
from jax.experimental import pallas as pl
from jax.experimental.pallas import tpu as pltpu
from jax.sharding import PartitionSpec as P

LANES = 128
STEP = 64
CHUNKS = (4, 4, 4, 4)
LATE = 2
PART = 256
MIB = 1024 * 1024
COST = pl.CostEstimate(flops=1024, bytes_accessed=1024, transcendentals=0)
IN_VMEM = pl.BlockSpec(memory_space=pltpu.VMEM)
IN_SMEM = pl.BlockSpec(memory_space=pltpu.SMEM)
ANYWHERE = pl.BlockSpec(memory_space=pl.ANY)
IN_HBM = pl.BlockSpec(memory_space=pltpu.MemorySpace.HBM)


def quarter_kernel(rows, far, n_after, place_ref, x_ref, c_hbm, *refs):
    refs = refs[n_after:]
    outs, (c_ref, turn_ref, held, c_sem, sems) = refs[:-5], refs[-5:]
    at = pl.program_id(0)
    step, k_all, depth = x_ref.shape
    padded = held.shape[2]
    many = PART // k_all

    @pl.when(at == 0)
    def _():
        first = pl.multiple_of(((place_ref[0] >> 1) ^ far) * 2 * LANES, 2 * LANES)
        copy = pltpu.make_async_copy(c_hbm.at[:, pl.ds(first, 2 * LANES)], c_ref, c_sem)
        copy.start()
        to = lax.broadcasted_iota(jnp.int32, (PART, PART), 0)
        source = lax.broadcasted_iota(jnp.int32, (PART, PART), 1)
        turn_ref[...] = (source == to % many * k_all + to // many).astype(jnp.float32).astype(jnp.bfloat16)
        copy.wait()

    x = x_ref[...].reshape(step * k_all, depth)
    product = jnp.dot(x, c_ref[...], preferred_element_type=jnp.float32)
    line = lax.broadcasted_iota(jnp.int32, product.shape, 0)
    product = jnp.where(line < (rows - at * step) * k_all, product, 0.0).astype(jnp.bfloat16)
    for part in range(step // many):
        lines = jnp.dot(
            turn_ref[...], product[part * PART : (part + 1) * PART], preferred_element_type=jnp.float32
        ).astype(jnp.bfloat16)
        here = pl.ds(pl.multiple_of(at * step + part * many, many), many)
        for k in range(k_all):
            for d in range(2):
                held[d, k, here] = lines[k * many : (k + 1) * many, d * LANES : (d + 1) * LANES]
    here = pl.ds(pl.multiple_of(at * step, step), step)
    first = 0
    for n, out in enumerate(outs):
        d = (place_ref[0] & 1) ^ (n & 1)
        kc = out.shape[0]
        pltpu.make_async_copy(held.at[d, pl.ds(first, kc), here], out.at[:, here], sems.at[n]).start()
        if n & 1:
            first += kc

    @pl.when(at == padded // step - 1)
    def _():
        first = 0
        for n, out in enumerate(outs):
            d = (place_ref[0] & 1) ^ (n & 1)
            kc = out.shape[0]
            pltpu.make_async_copy(held.at[d, pl.ds(first, kc)], out, sems.at[n]).wait()
            if n & 1:
                first += kc


def quarter_of(place, by_r, coeffs, far, padded, chunks, after=()):
    rows, k_all, depth = by_r.shape
    outs = [jax.ShapeDtypeStruct((kc, padded, LANES), jnp.bfloat16) for kc in chunks for _ in range(2)]
    out = pl.pallas_call(
        functools.partial(quarter_kernel, rows, far, len(after)),
        grid_spec=pltpu.PrefetchScalarGridSpec(
            num_scalar_prefetch=1,
            grid=(padded // STEP,),
            in_specs=[pl.BlockSpec((STEP, k_all, depth), lambda r, place: (r, 0, 0))]
            + [IN_HBM]
            + [ANYWHERE] * len(after),
            out_specs=[IN_HBM] * len(outs),
            scratch_shapes=[
                pltpu.VMEM((depth, 2 * LANES), jnp.bfloat16),
                pltpu.VMEM((PART, PART), jnp.bfloat16),
                pltpu.VMEM((2, k_all, padded, LANES), jnp.bfloat16),
                pltpu.SemaphoreType.DMA,
                pltpu.SemaphoreType.DMA((len(outs),)),
            ],
        ),
        out_shape=outs,
        compiler_params=pltpu.CompilerParams(vmem_limit_bytes=50 * MIB),
        cost_estimate=COST,
        name=f"quarter{far}",
    )(place, by_r, coeffs, *after)
    return list(out)


def turn_kernel(rows, c_ref, out_ref):
    n_mo, orbitals, padded = out_ref.shape
    none = jnp.zeros((padded - rows, orbitals), jnp.float32)
    for n in range(n_mo):
        part = c_ref[n * rows : (n + 1) * rows, :].astype(jnp.float32)
        out_ref[n] = jnp.concatenate([part, none], axis=0).T.astype(jnp.bfloat16)


def turn(coeffs, n_mo, padded):
    depth, orbitals = coeffs.shape
    return pl.pallas_call(
        functools.partial(turn_kernel, depth // n_mo),
        in_specs=[IN_VMEM],
        out_specs=IN_VMEM,
        out_shape=jax.ShapeDtypeStruct((n_mo, orbitals, padded), jnp.bfloat16),
        compiler_params=pltpu.CompilerParams(vmem_limit_bytes=24 * MIB),
        cost_estimate=COST,
        name="turn",
    )(coeffs)


def half_kernel(n_mo, plans, place_ref, *refs):
    blocks, t_ref, held = refs[:n_mo], refs[n_mo], refs[-1]
    outs = refs[-1 - 2 * len(plans) : -1]
    lanes = held.shape[1] // 2
    for p, (first, kc, owners) in enumerate(plans):
        for k in range(0, kc, 2):
            half = None
            for o, a_ref in enumerate(blocks):
                columns = jnp.concatenate([a_ref[first + k], a_ref[first + k + 1]], axis=1)
                part = jnp.dot(t_ref[place_ref[0] ^ o], columns, preferred_element_type=jnp.float32)
                half = part if half is None else half + part
            held[...] = half
            for out, its in zip(outs[2 * p : 2 * p + 2], owners):
                block = out.shape[3]
                for at, o in enumerate(its):
                    start = pl.multiple_of((place_ref[1] ^ o) * block, block)
                    for n in range(2):
                        piece = held[pl.ds(start, block), n * lanes : (n + 1) * lanes]
                        out[0, at, k + n] = piece.astype(jnp.bfloat16)


def half_of(place, blocks, turned, plans, after):
    n_mo, orbitals, _ = turned.shape
    lanes = blocks[0].shape[-1]
    shapes = [
        (1, len(its), kc, orbitals // sum(len(x) for x in owners), lanes)
        for _, kc, owners in plans
        for its in owners
    ]
    return pl.pallas_call(
        functools.partial(half_kernel, n_mo, plans),
        in_specs=[IN_SMEM] + [IN_VMEM] * (n_mo + 1) + [ANYWHERE] * len(after),
        out_specs=[IN_VMEM] * len(shapes),
        out_shape=[jax.ShapeDtypeStruct(shape, jnp.bfloat16) for shape in shapes],
        scratch_shapes=[pltpu.VMEM((orbitals, 2 * lanes), jnp.float32)],
        compiler_params=pltpu.CompilerParams(vmem_limit_bytes=24 * MIB),
        cost_estimate=COST,
        name="half",
    )(place, *blocks, turned, *after)


def merge_kernel(picks, *refs):
    at = 0
    for x, pick in zip(refs, picks):
        for i in range(x.shape[0]):
            for n, o in enumerate(pick):
                refs[-1][at, n] = x[i, o]
            at += 1


def merge(parts, picks, after):
    shape = (sum(x.shape[0] for x in parts), len(picks[0]), *parts[0].shape[2:])
    return pl.pallas_call(
        functools.partial(merge_kernel, picks),
        in_specs=[IN_VMEM] * len(parts) + [ANYWHERE] * len(after),
        out_specs=IN_VMEM,
        out_shape=jax.ShapeDtypeStruct(shape, jnp.bfloat16),
        compiler_params=pltpu.CompilerParams(vmem_limit_bytes=24 * MIB),
        cost_estimate=COST,
        name="merge",
    )(*parts, *after)


def combine_kernel(sources, k_all, per_step, mirror_ref, place_ref, *refs):
    pieces, out_ref, held = refs[:-2], refs[-2], refs[-1]
    step = pl.program_id(0)

    @pl.when(step == 0)
    def _():
        for piece, (offsets, first) in zip(pieces, sources):
            for n, offset in enumerate(offsets):
                row = (place_ref[1] ^ offset) * k_all + first
                held[pl.ds(row, piece.shape[2])] = piece[n, 0]

    for n in range(per_step):
        k = step * per_step + n
        out_ref[n] = 0.5 * (held[k].astype(jnp.float32) + held[mirror_ref[k]].astype(jnp.float32))


def combine(pieces, sources, mirror, place, n_pair):
    block, lanes = pieces[0].shape[-2:]
    k_all = sum(CHUNKS)
    rows = n_pair * k_all
    per_step = max(1, 32 * 64 // block)
    return pl.pallas_call(
        functools.partial(combine_kernel, sources, k_all, per_step),
        grid_spec=pltpu.PrefetchScalarGridSpec(
            num_scalar_prefetch=2,
            grid=(rows // per_step,),
            in_specs=[IN_VMEM] * len(pieces),
            out_specs=pl.BlockSpec((per_step, block, lanes), lambda k, m, place: (k, 0, 0)),
            scratch_shapes=[pltpu.VMEM((rows, block, lanes), jnp.bfloat16)],
        ),
        out_shape=jax.ShapeDtypeStruct((rows, block, lanes), jnp.float32),
        compiler_params=pltpu.CompilerParams(vmem_limit_bytes=24 * MIB),
        cost_estimate=COST,
        name="combine",
    )(mirror, place, *pieces)


def flipped(x, axis, size, offset, name):
    with jax.named_scope(name):
        return lax.ppermute(x, axis, [(i, i ^ offset) for i in range(size)])


def on_device(n_pair, n_mo, integrals, coeffs, mirror):
    rows = integrals.shape[1]
    padded = -(-rows // STEP) * STEP
    n_near = n_pair // 2
    by_r = jnp.transpose(integrals, (1, 0, 2))
    place = jnp.stack([lax.axis_index("mo"), lax.axis_index("pair")]).astype(jnp.int32)
    turned = turn(coeffs, n_mo, padded)
    queue = quarter_of(place, by_r, coeffs, 1, padded, CHUNKS)
    arrived = [flipped(x, "mo", n_mo, 2 + (m & 1), f"y{m}") for m, x in enumerate(queue)]
    near = quarter_of(place, by_r, coeffs, 0, padded, CHUNKS, queue[:1])
    beside = [flipped(x, "mo", n_mo, 1, f"beside{c}") for c, x in enumerate(near[1::2])]

    down = tuple(1 << n for n in reversed(range(n_pair.bit_length() - 1)))
    last = len(CHUNKS) - 1
    units = [(c, 0, kc - LATE * (c == last), down) for c, kc in enumerate(CHUNKS)]
    units.append((last, CHUNKS[-1] - LATE, LATE, down[::-1]))
    firsts = [sum(CHUNKS[:c]) + at for c, at, _, _ in units]
    steps = [(c, c, 0) for c in range(len(CHUNKS))]
    for level in range(1, len(down)):
        steps += [(c + level + level / 10, c, level) for c in range(len(CHUNKS))]
        steps.append((last + level - 0.85, last + 1, level))
    parts, owners, offsets = [[] for _ in units], [[] for _ in units], [[[0]] for _ in units]
    token = []

    def send(unit, level, message, sent):
        flip = units[unit][3][level]
        offsets[unit].append([o ^ flip for group in offsets[unit] for o in group])
        owners[unit].append([o ^ flip for o in sent])
        parts[unit].append(flipped(message, "pair", n_pair, flip, f"z{flip}c{unit}"))

    def split(unit, level):
        flips = units[unit][3]
        left = [o for o in range(n_pair) if not o & sum(flips[:level])]
        return [o for o in left if not o & flips[level]], [o for o in left if o & flips[level]]

    for _, n, level in sorted(steps):
        if level == 0:
            mine = [unit for unit, plan in enumerate(units) if plan[0] == n]
            plans = [(units[unit][1], units[unit][2], split(unit, 0)) for unit in mine]
            blocks = [near[2 * n], beside[n], *arrived[2 * n : 2 * n + 2]]
            out = half_of(place, blocks, turned, plans, token)
            for m, unit in enumerate(mine):
                parts[unit].append(out[2 * m])
                owners[unit].append(plans[m][2][0])
                send(unit, 0, out[2 * m + 1], plans[m][2][1])
            token = list(out[:1])
        else:
            sent = split(n, level)[1]
            after = token + ([parts[n - 2][-1]] if level == len(down) - 1 and 1 < n <= last else [])
            message = merge(parts[n], [[its.index(o) for o in sent] for its in owners[n]], after)
            send(n, level, message, sent)
            token = [message]
    pieces = [x for chunk in parts for x in chunk]
    sources = [(tuple(group), first) for chunk, first in zip(offsets, firsts) for group in chunk]
    return combine(pieces, sources, mirror, place, n_pair)


def solution(mesh):
    return jax.shard_map(
        functools.partial(on_device, mesh.shape["pair"], mesh.shape["mo"]),
        mesh=mesh,
        in_specs=(P("pair", "mo", None), P(), P()),
        out_specs=P(None, "pair", "mo"),
        check_vma=False,
    )
```

```python
import functools

import jax
import jax.numpy as jnp
from jax import lax
from jax.experimental import pallas as pl
from jax.experimental.pallas import tpu as pltpu
from jax.sharding import PartitionSpec as P

LANES = 128
STEP = 64
CHUNKS = (4, 4, 4, 4)
PART = 256
MIB = 1024 * 1024
COST = pl.CostEstimate(flops=1024, bytes_accessed=1024, transcendentals=0)
IN_VMEM = pl.BlockSpec(memory_space=pltpu.VMEM)
IN_SMEM = pl.BlockSpec(memory_space=pltpu.SMEM)
ANYWHERE = pl.BlockSpec(memory_space=pl.ANY)
IN_HBM = pl.BlockSpec(memory_space=pltpu.MemorySpace.HBM)


def quarter_kernel(rows, n_mo, blocks, place_ref, x_ref, c_hbm, *refs):
    outs, (c_ref, turn_ref, held, c_sem, sems) = refs[:-5], refs[-5:]
    at = pl.program_id(0)
    step, k_all, depth = x_ref.shape
    padded = held.shape[2]
    many = PART // k_all

    @pl.when(at == 0)
    def _():
        copy = pltpu.make_async_copy(c_hbm, c_ref, c_sem)
        copy.start()
        to = lax.broadcasted_iota(jnp.int32, (PART, PART), 0)
        source = lax.broadcasted_iota(jnp.int32, (PART, PART), 1)
        turn_ref[...] = (source == to % many * k_all + to // many).astype(jnp.float32).astype(jnp.bfloat16)
        copy.wait()

    x = x_ref[...].reshape(step * k_all, depth)
    product = jnp.dot(x, c_ref[...], preferred_element_type=jnp.float32)
    line = lax.broadcasted_iota(jnp.int32, product.shape, 0)
    product = jnp.where(line < (rows - at * step) * k_all, product, 0.0).astype(jnp.bfloat16)
    for part in range(step // many):
        lines = jnp.dot(
            turn_ref[...], product[part * PART : (part + 1) * PART], preferred_element_type=jnp.float32
        ).astype(jnp.bfloat16)
        here = pl.ds(pl.multiple_of(at * step + part * many, many), many)
        for k in range(k_all):
            for d in range(n_mo):
                held[d, k, here] = lines[k * many : (k + 1) * many, d * LANES : (d + 1) * LANES]
    here = pl.ds(pl.multiple_of(at * step, step), step)
    for n, (out, (o, first)) in enumerate(zip(outs, blocks)):
        mine = held.at[place_ref[0] ^ o, pl.ds(first, out.shape[0])]
        pltpu.make_async_copy(mine.at[:, here], out.at[:, here], sems.at[n]).start()

    @pl.when(at == padded // step - 1)
    def _():
        for n, (out, (o, first)) in enumerate(zip(outs, blocks)):
            mine = held.at[place_ref[0] ^ o, pl.ds(first, out.shape[0])]
            pltpu.make_async_copy(mine, out, sems.at[n]).wait()


def quarter_of(place, by_r, coeffs, n_mo, padded):
    rows, k_all, depth = by_r.shape
    orbitals = coeffs.shape[1]
    blocks = [(0, 0), (1, 0)] + [(o, sum(CHUNKS[:c])) for c in range(len(CHUNKS)) for o in range(2, n_mo)]
    sizes = [k_all] * 2 + [kc for kc in CHUNKS for _ in range(2, n_mo)]
    outs = [jax.ShapeDtypeStruct((kc, padded, LANES), jnp.bfloat16) for kc in sizes]
    out = pl.pallas_call(
        functools.partial(quarter_kernel, rows, n_mo, blocks),
        grid_spec=pltpu.PrefetchScalarGridSpec(
            num_scalar_prefetch=1,
            grid=(padded // STEP,),
            in_specs=[pl.BlockSpec((STEP, k_all, depth), lambda r, place: (r, 0, 0)), IN_HBM],
            out_specs=[IN_HBM] * len(outs),
            scratch_shapes=[
                pltpu.VMEM((depth, orbitals), jnp.bfloat16),
                pltpu.VMEM((PART, PART), jnp.bfloat16),
                pltpu.VMEM((n_mo, k_all, padded, LANES), jnp.bfloat16),
                pltpu.SemaphoreType.DMA,
                pltpu.SemaphoreType.DMA((len(outs),)),
            ],
        ),
        out_shape=outs,
        compiler_params=pltpu.CompilerParams(vmem_limit_bytes=50 * MIB),
        cost_estimate=COST,
        name="quarter",
    )(place, by_r, coeffs)
    far = n_mo - 2
    return out[:2], [out[2 + far * c : 2 + far * (c + 1)] for c in range(len(CHUNKS))]


def turn_kernel(rows, c_ref, *refs):
    out_ref = refs[-1]
    n_mo, orbitals, padded = out_ref.shape
    none = jnp.zeros((padded - rows, orbitals), jnp.float32)
    for n in range(n_mo):
        part = c_ref[n * rows : (n + 1) * rows, :].astype(jnp.float32)
        out_ref[n] = jnp.concatenate([part, none], axis=0).T.astype(jnp.bfloat16)


def turn(coeffs, n_mo, padded, later, after):
    depth, orbitals = coeffs.shape
    out = pl.pallas_call(
        functools.partial(turn_kernel, depth // n_mo),
        in_specs=[IN_VMEM] + [IN_HBM] * len(later) + [ANYWHERE] * len(after),
        out_specs=[IN_HBM] * len(later) + [IN_VMEM],
        out_shape=[jax.ShapeDtypeStruct(x.shape, x.dtype) for x in later]
        + [jax.ShapeDtypeStruct((n_mo, orbitals, padded), jnp.bfloat16)],
        input_output_aliases={1 + n: n for n in range(len(later))},
        compiler_params=pltpu.CompilerParams(vmem_limit_bytes=24 * MIB),
        cost_estimate=COST,
        name="turn",
    )(coeffs, *later, *after)
    return out[-1], list(out[:-1])


def half_kernel(n_mo, first, owners, place_ref, *refs):
    blocks, t_ref, held = refs[:n_mo], refs[n_mo], refs[-1]
    outs = refs[-1 - len(owners) : -1]
    kc, block, lanes = outs[0].shape[2:]
    firsts = [first if x.shape[0] > kc else 0 for x in blocks]
    columns = [jnp.concatenate([x[at + k] for k in range(kc)], axis=1) for x, at in zip(blocks, firsts)]
    turned = [t_ref[place_ref[0] ^ o] for o in range(n_mo)]
    held[...] = jnp.dot(
        jnp.concatenate(turned, axis=1), jnp.concatenate(columns, axis=0), preferred_element_type=jnp.float32
    )
    for out, its in zip(outs, owners):
        for at, o in enumerate(its):
            start = pl.multiple_of((place_ref[1] ^ o) * block, block)
            for k in range(kc):
                out[0, at, k] = held[pl.ds(start, block), k * lanes : (k + 1) * lanes].astype(jnp.bfloat16)


def half_of(place, blocks, turned, first, owners, after):
    n_mo, orbitals, _ = turned.shape
    kc, _, lanes = blocks[-1].shape
    block = orbitals // sum(len(its) for its in owners)
    return pl.pallas_call(
        functools.partial(half_kernel, n_mo, first, owners),
        in_specs=[IN_SMEM] + [IN_VMEM] * (n_mo + 1) + [ANYWHERE] * len(after),
        out_specs=[IN_VMEM] * len(owners),
        out_shape=[jax.ShapeDtypeStruct((1, len(its), kc, block, lanes), jnp.bfloat16) for its in owners],
        scratch_shapes=[pltpu.VMEM((orbitals, kc * lanes), jnp.float32)],
        compiler_params=pltpu.CompilerParams(vmem_limit_bytes=24 * MIB),
        cost_estimate=COST,
        name="half",
    )(place, *blocks, turned, *after)


def merge_kernel(picks, *refs):
    at = 0
    for x, pick in zip(refs, picks):
        for i in range(x.shape[0]):
            for n, o in enumerate(pick):
                refs[-1][at, n] = x[i, o]
            at += 1


def merge(parts, picks, after):
    shape = (sum(x.shape[0] for x in parts), len(picks[0]), *parts[0].shape[2:])
    return pl.pallas_call(
        functools.partial(merge_kernel, picks),
        in_specs=[IN_VMEM] * len(parts) + [ANYWHERE] * len(after),
        out_specs=IN_VMEM,
        out_shape=jax.ShapeDtypeStruct(shape, jnp.bfloat16),
        compiler_params=pltpu.CompilerParams(vmem_limit_bytes=24 * MIB),
        cost_estimate=COST,
        name="merge",
    )(*parts, *after)


def combine_kernel(sources, k_all, per_step, mirror_ref, place_ref, *refs):
    pieces, out_ref, held = refs[:-2], refs[-2], refs[-1]
    step = pl.program_id(0)

    @pl.when(step == 0)
    def _():
        for piece, (offsets, first) in zip(pieces, sources):
            for n, offset in enumerate(offsets):
                row = (place_ref[1] ^ offset) * k_all + first
                held[pl.ds(row, piece.shape[2])] = piece[n, 0]

    for n in range(per_step):
        k = step * per_step + n
        out_ref[n] = 0.5 * (held[k].astype(jnp.float32) + held[mirror_ref[k]].astype(jnp.float32))


def combine(pieces, sources, mirror, place, n_pair):
    block, lanes = pieces[0].shape[-2:]
    k_all = sum(CHUNKS)
    rows = n_pair * k_all
    per_step = max(1, 32 * 64 // block)
    return pl.pallas_call(
        functools.partial(combine_kernel, sources, k_all, per_step),
        grid_spec=pltpu.PrefetchScalarGridSpec(
            num_scalar_prefetch=2,
            grid=(rows // per_step,),
            in_specs=[IN_VMEM] * len(pieces),
            out_specs=pl.BlockSpec((per_step, block, lanes), lambda k, m, place: (k, 0, 0)),
            scratch_shapes=[pltpu.VMEM((rows, block, lanes), jnp.bfloat16)],
        ),
        out_shape=jax.ShapeDtypeStruct((rows, block, lanes), jnp.float32),
        compiler_params=pltpu.CompilerParams(vmem_limit_bytes=24 * MIB),
        cost_estimate=COST,
        name="combine",
    )(mirror, place, *pieces)


def flipped(x, axis, size, offset, name):
    with jax.named_scope(name):
        return lax.ppermute(x, axis, [(i, i ^ offset) for i in range(size)])


def on_device(n_pair, n_mo, integrals, coeffs, mirror):
    rows = integrals.shape[1]
    padded = -(-rows // STEP) * STEP
    n_near = n_pair // 2
    by_r = jnp.transpose(integrals, (1, 0, 2))
    place = jnp.stack([lax.axis_index("mo"), lax.axis_index("pair")]).astype(jnp.int32)
    (own, beside), queue = quarter_of(place, by_r, coeffs, n_mo, padded)
    beside = flipped(beside, "mo", n_mo, 1, "beside")
    last = len(CHUNKS) - 1
    firsts = [sum(CHUNKS[:c]) for c in range(last + 1)]
    down = [1 << n for n in reversed(range(n_pair.bit_length() - 1))]
    orders = [down] * last + [down[::-1]]
    turned, parts, owners, offsets, token = None, [[] for _ in CHUNKS], [[] for _ in CHUNKS], [[] for _ in CHUNKS], []

    def arrive(c):
        return [flipped(x, "mo", n_mo, o, f"y{2 * c + o - 2}") for o, x in enumerate(queue[c], 2)]

    arrived = [arrive(0)]
    turned, queue[1] = turn(coeffs, n_mo, padded, queue[1], arrived[0][:1])
    arrived += [arrive(c) for c in range(1, last + 1)]

    steps = [(c, c, 0) for c in range(last + 1)]
    for n in range(1, len(down)):
        steps += [(c + n + (0.5 - n / 10 if c + n == last else n / 10), c, n) for c in range(last)]
        steps.append((last + n - (0.55 if n == 1 else 0.95), last, n))
    for _, c, level in sorted(steps):
        flips = orders[c]
        flip, gone = flips[level], sum(flips[:level])
        left = [o for o in range(n_pair) if not o & gone]
        kept, sent = [o for o in left if not o & flip], [o for o in left if o & flip]
        if level == 0:
            keep, message = half_of(place, [own, beside, *arrived[c]], turned, firsts[c], [kept, sent], token)
            parts[c], owners[c], offsets[c] = [keep], [kept], [[0]]
        else:
            after = token + (parts[c - 1][-1:] if level == len(flips) - 1 and 0 < c < last else [])
            message = merge(parts[c], [[its.index(o) for o in sent] for its in owners[c]], after)
        token = [message]
        offsets[c].append([o ^ flip for group in offsets[c] for o in group])
        owners[c].append([o ^ flip for o in sent])
        parts[c].append(flipped(message, "pair", n_pair, flip, f"z{flip}c{c}"))
    pieces = [x for chunk in parts for x in chunk]
    sources = [(tuple(group), first) for chunk, first in zip(offsets, firsts) for group in chunk]
    return combine(pieces, sources, mirror, place, n_pair)


def solution(mesh):
    return jax.shard_map(
        functools.partial(on_device, mesh.shape["pair"], mesh.shape["mo"]),
        mesh=mesh,
        in_specs=(P("pair", "mo", None), P(), P()),
        out_specs=P(None, "pair", "mo"),
        check_vma=False,
    )
```

```python
import functools

import jax
import jax.numpy as jnp
from jax import lax
from jax.experimental import pallas as pl
from jax.experimental.pallas import tpu as pltpu
from jax.sharding import PartitionSpec as P

LANES = 128
STEP = 64
BATCHES = ((4, 4), (4, 4))
CHUNKS = sum(BATCHES, ())
LATE = 2
PART = 256
MIB = 1024 * 1024
COST = pl.CostEstimate(flops=1024, bytes_accessed=1024, transcendentals=0)
IN_VMEM = pl.BlockSpec(memory_space=pltpu.VMEM)
IN_SMEM = pl.BlockSpec(memory_space=pltpu.SMEM)
ANYWHERE = pl.BlockSpec(memory_space=pl.ANY)
IN_HBM = pl.BlockSpec(memory_space=pltpu.MemorySpace.HBM)


def quarter_kernel(rows, n_mo, blocks, n_after, place_ref, x_ref, c_hbm, *refs):
    refs = refs[n_after:]
    outs, (c_ref, turn_ref, held, c_sem, sems) = refs[:-5], refs[-5:]
    at = pl.program_id(0)
    step, some, depth = x_ref.shape
    padded = held.shape[2]
    many = PART // some

    @pl.when(at == 0)
    def _():
        copy = pltpu.make_async_copy(c_hbm, c_ref, c_sem)
        copy.start()
        to = lax.broadcasted_iota(jnp.int32, (PART, PART), 0)
        source = lax.broadcasted_iota(jnp.int32, (PART, PART), 1)
        turn_ref[...] = (source == to % many * some + to // many).astype(jnp.float32).astype(jnp.bfloat16)
        copy.wait()

    x = x_ref[...].reshape(step * some, depth)
    product = jnp.dot(x, c_ref[...], preferred_element_type=jnp.float32)
    line = lax.broadcasted_iota(jnp.int32, product.shape, 0)
    product = jnp.where(line < (rows - at * step) * some, product, 0.0).astype(jnp.bfloat16)
    for part in range(step // many):
        lines = jnp.dot(
            turn_ref[...], product[part * PART : (part + 1) * PART], preferred_element_type=jnp.float32
        ).astype(jnp.bfloat16)
        here = pl.ds(pl.multiple_of(at * step + part * many, many), many)
        for k in range(some):
            for d in range(n_mo):
                held[d, k, here] = lines[k * many : (k + 1) * many, d * LANES : (d + 1) * LANES]
    here = pl.ds(pl.multiple_of(at * step, step), step)
    for n, (out, (o, first)) in enumerate(zip(outs, blocks)):
        mine = held.at[place_ref[0] ^ o, pl.ds(first, out.shape[0])]
        pltpu.make_async_copy(mine.at[:, here], out.at[:, here], sems.at[n]).start()

    @pl.when(at == padded // step - 1)
    def _():
        for n, (out, (o, first)) in enumerate(zip(outs, blocks)):
            mine = held.at[place_ref[0] ^ o, pl.ds(first, out.shape[0])]
            pltpu.make_async_copy(mine, out, sems.at[n]).wait()


def quarter_of(place, by_r, coeffs, n_mo, padded, batch, after):
    rows, _, depth = by_r.shape
    orbitals = coeffs.shape[1]
    chunks = BATCHES[batch]
    some = sum(chunks)
    blocks = [(0, 0), (1, 0)] + [(o, sum(chunks[:c])) for c in range(len(chunks)) for o in range(2, n_mo)]
    sizes = [some] * 2 + [kc for kc in chunks for _ in range(2, n_mo)]
    outs = [jax.ShapeDtypeStruct((kc, padded, LANES), jnp.bfloat16) for kc in sizes]
    out = pl.pallas_call(
        functools.partial(quarter_kernel, rows, n_mo, blocks, len(after)),
        grid_spec=pltpu.PrefetchScalarGridSpec(
            num_scalar_prefetch=1,
            grid=(padded // STEP,),
            in_specs=[pl.BlockSpec((STEP, some, depth), lambda r, place: (r, batch, 0)), IN_HBM]
            + [ANYWHERE] * len(after),
            out_specs=[IN_HBM] * len(outs),
            scratch_shapes=[
                pltpu.VMEM((depth, orbitals), jnp.bfloat16),
                pltpu.VMEM((PART, PART), jnp.bfloat16),
                pltpu.VMEM((n_mo, some, padded, LANES), jnp.bfloat16),
                pltpu.SemaphoreType.DMA,
                pltpu.SemaphoreType.DMA((len(outs),)),
            ],
        ),
        out_shape=outs,
        compiler_params=pltpu.CompilerParams(vmem_limit_bytes=50 * MIB),
        cost_estimate=COST,
        name="quarter",
    )(place, by_r, coeffs, *after)
    far = n_mo - 2
    return out[:2], [out[2 + far * c : 2 + far * (c + 1)] for c in range(len(chunks))]


def turn_kernel(rows, c_ref, *refs):
    out_ref = refs[-1]
    n_mo, orbitals, padded = out_ref.shape
    none = jnp.zeros((padded - rows, orbitals), jnp.float32)
    for n in range(n_mo):
        part = c_ref[n * rows : (n + 1) * rows, :].astype(jnp.float32)
        out_ref[n] = jnp.concatenate([part, none], axis=0).T.astype(jnp.bfloat16)


def turn(coeffs, n_mo, padded, later, after):
    depth, orbitals = coeffs.shape
    out = pl.pallas_call(
        functools.partial(turn_kernel, depth // n_mo),
        in_specs=[IN_VMEM] + [IN_HBM] * len(later) + [ANYWHERE] * len(after),
        out_specs=[IN_HBM] * len(later) + [IN_VMEM],
        out_shape=[jax.ShapeDtypeStruct(x.shape, x.dtype) for x in later]
        + [jax.ShapeDtypeStruct((n_mo, orbitals, padded), jnp.bfloat16)],
        input_output_aliases={1 + n: n for n in range(len(later))},
        compiler_params=pltpu.CompilerParams(vmem_limit_bytes=24 * MIB),
        cost_estimate=COST,
        name="turn",
    )(coeffs, *later, *after)
    return out[-1], list(out[:-1])


def half_kernel(n_mo, first, plans, place_ref, *refs):
    blocks, t_ref, held = refs[:n_mo], refs[n_mo], refs[-1]
    outs = refs[-1 - len(plans) : -1]
    block, lanes = outs[0].shape[-2:]
    kc = blocks[-1].shape[0]
    firsts = [first if x.shape[0] > kc else 0 for x in blocks]
    columns = [jnp.concatenate([x[at + k] for k in range(kc)], axis=1) for x, at in zip(blocks, firsts)]
    turned = [t_ref[place_ref[0] ^ o] for o in range(n_mo)]
    held[...] = jnp.dot(
        jnp.concatenate(turned, axis=1), jnp.concatenate(columns, axis=0), preferred_element_type=jnp.float32
    )
    for out, (at, rows, owners) in zip(outs, plans):
        for n, o in enumerate(owners):
            start = pl.multiple_of((place_ref[1] ^ o) * block, block)
            for k in range(rows):
                piece = held[pl.ds(start, block), (at + k) * lanes : (at + k + 1) * lanes]
                out[0, n, k] = piece.astype(jnp.bfloat16)


def half_of(place, blocks, turned, n_pair, first, plans, after):
    n_mo, orbitals, _ = turned.shape
    kc, _, lanes = blocks[-1].shape
    block = orbitals // n_pair
    return pl.pallas_call(
        functools.partial(half_kernel, n_mo, first, plans),
        in_specs=[IN_SMEM] + [IN_VMEM] * (n_mo + 1) + [ANYWHERE] * len(after),
        out_specs=[IN_VMEM] * len(plans),
        out_shape=[
            jax.ShapeDtypeStruct((1, len(owners), rows, block, lanes), jnp.bfloat16) for _, rows, owners in plans
        ],
        scratch_shapes=[pltpu.VMEM((orbitals, kc * lanes), jnp.float32)],
        compiler_params=pltpu.CompilerParams(vmem_limit_bytes=24 * MIB),
        cost_estimate=COST,
        name="half",
    )(place, *blocks, turned, *after)


def merge_kernel(picks, *refs):
    at = 0
    for x, pick in zip(refs, picks):
        for i in range(x.shape[0]):
            for n, o in enumerate(pick):
                refs[-1][at, n] = x[i, o]
            at += 1


def merge(parts, picks, later, after):
    shape = (sum(x.shape[0] for x in parts), len(picks[0]), *parts[0].shape[2:])
    n = len(parts)
    out = pl.pallas_call(
        functools.partial(merge_kernel, picks),
        in_specs=[IN_VMEM] * n + [IN_HBM] * len(later) + [ANYWHERE] * len(after),
        out_specs=[IN_HBM] * len(later) + [IN_VMEM],
        out_shape=[jax.ShapeDtypeStruct(x.shape, x.dtype) for x in later]
        + [jax.ShapeDtypeStruct(shape, jnp.bfloat16)],
        input_output_aliases={n + m: m for m in range(len(later))},
        compiler_params=pltpu.CompilerParams(vmem_limit_bytes=24 * MIB),
        cost_estimate=COST,
        name="merge",
    )(*parts, *later, *after)
    return out[-1], out[:-1]


def combine_kernel(sources, k_all, per_step, mirror_ref, place_ref, *refs):
    pieces, out_ref, held = refs[:-2], refs[-2], refs[-1]
    step = pl.program_id(0)

    @pl.when(step == 0)
    def _():
        for piece, (offsets, first) in zip(pieces, sources):
            for n, offset in enumerate(offsets):
                row = (place_ref[1] ^ offset) * k_all + first
                held[pl.ds(row, piece.shape[2])] = piece[n, 0]

    for n in range(per_step):
        k = step * per_step + n
        out_ref[n] = 0.5 * (held[k].astype(jnp.float32) + held[mirror_ref[k]].astype(jnp.float32))


def combine(pieces, sources, mirror, place, n_pair):
    block, lanes = pieces[0].shape[-2:]
    k_all = sum(CHUNKS)
    rows = n_pair * k_all
    per_step = max(1, 32 * 64 // block)
    return pl.pallas_call(
        functools.partial(combine_kernel, sources, k_all, per_step),
        grid_spec=pltpu.PrefetchScalarGridSpec(
            num_scalar_prefetch=2,
            grid=(rows // per_step,),
            in_specs=[IN_VMEM] * len(pieces),
            out_specs=pl.BlockSpec((per_step, block, lanes), lambda k, m, place: (k, 0, 0)),
            scratch_shapes=[pltpu.VMEM((rows, block, lanes), jnp.bfloat16)],
        ),
        out_shape=jax.ShapeDtypeStruct((rows, block, lanes), jnp.float32),
        compiler_params=pltpu.CompilerParams(vmem_limit_bytes=24 * MIB),
        cost_estimate=COST,
        name="combine",
    )(mirror, place, *pieces)


def flipped(x, axis, size, offset, name):
    with jax.named_scope(name):
        return lax.ppermute(x, axis, [(i, i ^ offset) for i in range(size)])


def on_device(n_pair, n_mo, integrals, coeffs, mirror):
    rows = integrals.shape[1]
    padded = -(-rows // STEP) * STEP
    n_near = n_pair // 2
    by_r = jnp.transpose(integrals, (1, 0, 2))
    place = jnp.stack([lax.axis_index("mo"), lax.axis_index("pair")]).astype(jnp.int32)
    last = len(CHUNKS) - 1
    firsts = [sum(CHUNKS[:c]) for c in range(last + 1)]

    near, queue, token = [], [], []
    for batch, chunks in enumerate(BATCHES):
        (own, beside), far = quarter_of(place, by_r, coeffs, n_mo, padded, batch, token)
        beside = flipped(beside, "mo", n_mo, 1, f"beside{batch}")
        near += [(own, beside, sum(chunks[:c])) for c in range(len(chunks))]
        queue += far
        token = [own]

    def arrive(c):
        return [flipped(x, "mo", n_mo, o, f"y{2 * c + o - 2}") for o, x in enumerate(queue[c], 2)]

    arrived = [arrive(0)]
    turned, queue[1] = turn(coeffs, n_mo, padded, queue[1], arrived[0][:1] + token)
    arrived += [arrive(c) for c in range(1, last + 1)]

    down = [1 << n for n in reversed(range(n_pair.bit_length() - 1))]
    units = [(c, 0, kc - LATE * (c == last), down) for c, kc in enumerate(CHUNKS)]
    units.append((last, CHUNKS[-1] - LATE, LATE, down[::-1]))
    steps = [(c, c, 0) for c in range(last + 1)]
    for n in range(1, len(down)):
        steps += [(c + n + n / 10 + 0.3 * (c + n >= last), c, n) for c in range(last + 1)]
        steps.append((last + n - 0.55 + 0.1 * (n == 1), last + 1, n))
    parts, owners, offsets = [[] for _ in units], [[] for _ in units], [[[0]] for _ in units]
    waiting, token = {}, []

    def split(u, level):
        flips = units[u][3]
        left = [o for o in range(n_pair) if not o & sum(flips[:level])]
        return [o for o in left if not o & flips[level]], [o for o in left if o & flips[level]]

    def send(u, level, message):
        flip, sent = units[u][3][level], split(u, level)[1]
        offsets[u].append([o ^ flip for group in offsets[u] for o in group])
        owners[u].append([o ^ flip for o in sent])
        parts[u].append(flipped(message, "pair", n_pair, flip, f"z{flip}c{u}"))

    for _, u, level in sorted(steps):
        if level == 0:
            mine = [n for n, unit in enumerate(units) if unit[0] == u]
            plans = [(units[n][1], units[n][2], some) for n in mine for some in split(n, 0)]
            blocks = [*near[u][:2], *arrived[u]]
            out = half_of(place, blocks, turned, n_pair, near[u][2], plans, token)
            for m, n in enumerate(mine):
                parts[n].append(out[2 * m])
                owners[n].append(split(n, 0)[0])
                if 0 < n <= last:
                    waiting[n] = out[2 * m + 1]
                else:
                    send(n, 0, out[2 * m + 1])
            token = [out[0]]
        else:
            picks = [[its.index(o) for o in split(u, level)[1]] for its in owners[u]]
            later = [waiting.pop(u + 1)] if level == 1 and u + 1 in waiting else []
            done = parts[u - 2][-1:] if level == len(down) - 1 and 1 < u <= last else []
            if u > last and level == len(down) - 1:
                done = parts[last][1:2]
            message, later = merge(parts[u], picks, later, token + done)
            send(u, level, message)
            for x in later:
                send(u + 1, 0, x)
            token = [message]
    firsts = [firsts[c] + at for c, at, _, _ in units]
    pieces = [x for chunk in parts for x in chunk]
    sources = [(tuple(group), first) for chunk, first in zip(offsets, firsts) for group in chunk]
    return combine(pieces, sources, mirror, place, n_pair)


def solution(mesh):
    return jax.shard_map(
        functools.partial(on_device, mesh.shape["pair"], mesh.shape["mo"]),
        mesh=mesh,
        in_specs=(P("pair", "mo", None), P(), P()),
        out_specs=P(None, "pair", "mo"),
        check_vma=False,
    )
```

```python
import functools

import jax
import jax.numpy as jnp
from jax import lax
from jax.experimental import pallas as pl
from jax.experimental.pallas import tpu as pltpu
from jax.sharding import PartitionSpec as P

LANES = 128
STEP = 64
BATCHES = ((4, 4), (4, 4))
CHUNKS = sum(BATCHES, ())
SIZES = ((1,), (1,), (1, 2), (-1, 2))
PART = 256
MIB = 1024 * 1024
COST = pl.CostEstimate(flops=1024, bytes_accessed=1024, transcendentals=0)
IN_VMEM = pl.BlockSpec(memory_space=pltpu.VMEM)
IN_SMEM = pl.BlockSpec(memory_space=pltpu.SMEM)
ANYWHERE = pl.BlockSpec(memory_space=pl.ANY)
IN_HBM = pl.BlockSpec(memory_space=pltpu.MemorySpace.HBM)


def quarter_kernel(rows, n_mo, blocks, n_after, place_ref, x_ref, c_ref, *refs):
    refs = refs[n_after:]
    outs, (turn_ref, held, sems) = refs[:-3], refs[-3:]
    at = pl.program_id(0)
    step, some, depth = x_ref.shape
    padded = held.shape[2]
    many = PART // some

    @pl.when(at == 0)
    def _():
        to = lax.broadcasted_iota(jnp.int32, (PART, PART), 0)
        source = lax.broadcasted_iota(jnp.int32, (PART, PART), 1)
        bits = many.bit_length() - 1
        is_source = source == (to & (many - 1)) * some + (to >> bits)
        turn_ref[...] = jnp.where(is_source, 1.0, 0.0).astype(jnp.bfloat16)

    x = x_ref[...].reshape(step * some, depth)
    product = jnp.dot(x, c_ref[...], preferred_element_type=jnp.float32)
    line = lax.broadcasted_iota(jnp.int32, product.shape, 0)
    product = jnp.where(line < (rows - at * step) * some, product, 0.0).astype(jnp.bfloat16)
    for part in range(step // many):
        lines = jnp.dot(
            turn_ref[...], product[part * PART : (part + 1) * PART], preferred_element_type=jnp.float32
        ).astype(jnp.bfloat16)
        here = pl.ds(pl.multiple_of(at * step + part * many, many), many)
        for k in range(some):
            for d in range(n_mo):
                held[d, k, here] = lines[k * many : (k + 1) * many, d * LANES : (d + 1) * LANES]
    here = pl.ds(pl.multiple_of(at * step, step), step)
    for n, (out, (o, first)) in enumerate(zip(outs, blocks)):
        mine = held.at[place_ref[0] ^ o, pl.ds(first, out.shape[0])]
        pltpu.make_async_copy(mine.at[:, here], out.at[:, here], sems.at[n]).start()

    @pl.when(at == padded // step - 1)
    def _():
        for n, (out, (o, first)) in enumerate(zip(outs, blocks)):
            mine = held.at[place_ref[0] ^ o, pl.ds(first, out.shape[0])]
            pltpu.make_async_copy(mine, out, sems.at[n]).wait()


def quarter_of(place, by_r, coeffs, n_mo, padded, batch, after):
    rows, _, depth = by_r.shape
    orbitals = coeffs.shape[1]
    chunks = BATCHES[batch]
    some = sum(chunks)
    blocks = [(0, 0), (1, 0)] + [(o, sum(chunks[:c])) for c in range(len(chunks)) for o in range(2, n_mo)]
    sizes = [some] * 2 + [kc for kc in chunks for _ in range(2, n_mo)]
    outs = [jax.ShapeDtypeStruct((kc, padded, LANES), jnp.bfloat16) for kc in sizes]
    out = pl.pallas_call(
        functools.partial(quarter_kernel, rows, n_mo, blocks, len(after)),
        grid_spec=pltpu.PrefetchScalarGridSpec(
            num_scalar_prefetch=1,
            grid=(padded // STEP,),
            in_specs=[pl.BlockSpec((STEP, some, depth), lambda r, place: (r, batch, 0)), IN_VMEM]
            + [ANYWHERE] * len(after),
            out_specs=[IN_HBM] * len(outs),
            scratch_shapes=[
                pltpu.VMEM((PART, PART), jnp.bfloat16),
                pltpu.VMEM((n_mo, some, padded, LANES), jnp.bfloat16),
                pltpu.SemaphoreType.DMA((len(outs),)),
            ],
        ),
        out_shape=outs,
        compiler_params=pltpu.CompilerParams(vmem_limit_bytes=50 * MIB),
        cost_estimate=COST,
        name="quarter",
    )(place, by_r, coeffs, *after)
    far = n_mo - 2
    return out[:2], [out[2 + far * c : 2 + far * (c + 1)] for c in range(len(chunks))]


def turn_kernel(rows, c_ref, *refs):
    out_ref = refs[-1]
    n_mo, orbitals, padded = out_ref.shape
    none = jnp.zeros((padded - rows, orbitals), jnp.float32)
    for n in range(n_mo):
        part = c_ref[n * rows : (n + 1) * rows, :].astype(jnp.float32)
        out_ref[n] = jnp.concatenate([part, none], axis=0).T.astype(jnp.bfloat16)


def turn(coeffs, n_mo, padded, later, after):
    depth, orbitals = coeffs.shape
    out = pl.pallas_call(
        functools.partial(turn_kernel, depth // n_mo),
        in_specs=[IN_VMEM] + [IN_HBM] * len(later) + [ANYWHERE] * len(after),
        out_specs=[IN_HBM] * len(later) + [IN_VMEM],
        out_shape=[jax.ShapeDtypeStruct(x.shape, x.dtype) for x in later]
        + [jax.ShapeDtypeStruct((n_mo, orbitals, padded), jnp.bfloat16)],
        input_output_aliases={1 + n: n for n in range(len(later))},
        compiler_params=pltpu.CompilerParams(vmem_limit_bytes=24 * MIB),
        cost_estimate=COST,
        name="turn",
    )(coeffs, *later, *after)
    return out[-1], list(out[:-1])


def half_kernel(n_mo, first, owners, place_ref, *refs):
    blocks, t_ref, held = refs[:n_mo], refs[n_mo], refs[-1]
    outs = refs[-1 - len(owners) : -1]
    kc, block, lanes = outs[0].shape[2:]
    firsts = [first if x.shape[0] > kc else 0 for x in blocks]
    columns = [jnp.concatenate([x[at + k] for k in range(kc)], axis=1) for x, at in zip(blocks, firsts)]
    turned = [t_ref[place_ref[0] ^ o] for o in range(n_mo)]
    held[...] = jnp.dot(
        jnp.concatenate(turned, axis=1), jnp.concatenate(columns, axis=0), preferred_element_type=jnp.float32
    )
    for out, its in zip(outs, owners):
        for at, o in enumerate(its):
            start = pl.multiple_of((place_ref[1] ^ o) * block, block)
            for k in range(kc):
                out[0, at, k] = held[pl.ds(start, block), k * lanes : (k + 1) * lanes].astype(jnp.bfloat16)


def half_of(place, blocks, turned, first, owners, after):
    n_mo, orbitals, _ = turned.shape
    kc, _, lanes = blocks[-1].shape
    block = orbitals // sum(len(its) for its in owners)
    return pl.pallas_call(
        functools.partial(half_kernel, n_mo, first, owners),
        in_specs=[IN_SMEM] + [IN_VMEM] * (n_mo + 1) + [ANYWHERE] * len(after),
        out_specs=[IN_VMEM] * len(owners),
        out_shape=[jax.ShapeDtypeStruct((1, len(its), kc, block, lanes), jnp.bfloat16) for its in owners],
        scratch_shapes=[pltpu.VMEM((orbitals, kc * lanes), jnp.float32)],
        compiler_params=pltpu.CompilerParams(vmem_limit_bytes=24 * MIB),
        cost_estimate=COST,
        name="half",
    )(place, *blocks, turned, *after)


def merge_kernel(n_parts, picks, *refs):
    outs = refs[len(refs) - len(picks) :]
    for out, its in zip(outs, picks):
        at = 0
        for x, pick in zip(refs[:n_parts], its):
            for i in range(x.shape[0]):
                for n, o in enumerate(pick):
                    out[at, n] = x[i, o]
                at += 1


def merge(parts, picks, later, after):
    lines, n = sum(x.shape[0] for x in parts), len(parts)
    out = pl.pallas_call(
        functools.partial(merge_kernel, n, picks),
        in_specs=[IN_VMEM] * n + [IN_HBM] * len(later) + [ANYWHERE] * len(after),
        out_specs=[IN_HBM] * len(later) + [IN_VMEM] * len(picks),
        out_shape=[jax.ShapeDtypeStruct(x.shape, x.dtype) for x in later]
        + [jax.ShapeDtypeStruct((lines, len(its[0]), *parts[0].shape[2:]), jnp.bfloat16) for its in picks],
        input_output_aliases={n + m: m for m in range(len(later))},
        compiler_params=pltpu.CompilerParams(vmem_limit_bytes=24 * MIB),
        cost_estimate=COST,
        name="merge",
    )(*parts, *later, *after)
    return list(out[len(later) :]), list(out[: len(later)])


def wait_kernel(*refs):
    refs[-1][...] = jnp.zeros_like(refs[-1])


def wait_for(after):
    return pl.pallas_call(
        wait_kernel,
        in_specs=[ANYWHERE] * len(after),
        out_specs=IN_VMEM,
        out_shape=jax.ShapeDtypeStruct((8, LANES), jnp.float32),
        compiler_params=pltpu.CompilerParams(vmem_limit_bytes=24 * MIB),
        cost_estimate=COST,
        name="wait",
    )(*after)


def combine_kernel(sources, k_all, per_step, mirror_ref, place_ref, *refs):
    pieces, out_ref, held = refs[: len(sources)], refs[-2], refs[-1]
    step = pl.program_id(0)

    @pl.when(step == 0)
    def _():
        for piece, (offsets, first) in zip(pieces, sources):
            for n, offset in enumerate(offsets):
                row = (place_ref[1] ^ offset) * k_all + first
                held[pl.ds(row, piece.shape[2])] = piece[n, 0]

    for n in range(per_step):
        k = step * per_step + n
        out_ref[n] = 0.5 * (held[k].astype(jnp.float32) + held[mirror_ref[k]].astype(jnp.float32))


def combine(pieces, sources, mirror, place, n_pair, after):
    block, lanes = pieces[0].shape[-2:]
    k_all = sum(CHUNKS)
    rows = n_pair * k_all
    per_step = max(1, 32 * 64 // block)
    return pl.pallas_call(
        functools.partial(combine_kernel, sources, k_all, per_step),
        grid_spec=pltpu.PrefetchScalarGridSpec(
            num_scalar_prefetch=2,
            grid=(rows // per_step,),
            in_specs=[IN_VMEM] * len(pieces) + [ANYWHERE] * len(after),
            out_specs=pl.BlockSpec((per_step, block, lanes), lambda k, m, place: (k, 0, 0)),
            scratch_shapes=[pltpu.VMEM((rows, block, lanes), jnp.bfloat16)],
        ),
        out_shape=jax.ShapeDtypeStruct((rows, block, lanes), jnp.float32),
        compiler_params=pltpu.CompilerParams(vmem_limit_bytes=24 * MIB),
        cost_estimate=COST,
        name="combine",
    )(mirror, place, *pieces, *after)


def flipped(x, axis, size, offset, name):
    with jax.named_scope(name):
        return lax.ppermute(x, axis, [(i, i ^ offset) for i in range(size)])


def digits(n_pair, sizes):
    bits = [1 << n for n in reversed(range(n_pair.bit_length() - 1))]
    masks = []
    while bits:
        size = sizes[min(len(masks), len(sizes) - 1)]
        some = bits[:size] if size > 0 else bits[size:]
        masks.append(sum(some))
        bits = [bit for bit in bits if bit not in some]
    return masks


def on_device(n_pair, n_mo, integrals, coeffs, mirror):
    rows = integrals.shape[1]
    padded = -(-rows // STEP) * STEP
    n_near = n_pair // 2
    by_r = jnp.transpose(integrals, (1, 0, 2))
    place = jnp.stack([lax.axis_index("mo"), lax.axis_index("pair")]).astype(jnp.int32)
    last = len(CHUNKS) - 1
    firsts = [sum(CHUNKS[:c]) for c in range(last + 1)]

    near, queue, token = [], [], []
    for batch, chunks in enumerate(BATCHES):
        (own, beside), far = quarter_of(place, by_r, coeffs, n_mo, padded, batch, token)
        beside = flipped(beside, "mo", n_mo, 1, f"beside{batch}")
        near += [(own, beside, sum(chunks[:c])) for c in range(len(chunks))]
        queue += far
        token = [own]

    def arrive(c):
        return [flipped(x, "mo", n_mo, o, f"y{2 * c + o - 2}") for o, x in enumerate(queue[c], 2)]

    arrived = [arrive(0)]
    turned, queue[1] = turn(coeffs, n_mo, padded, queue[1], arrived[0][:1] + token)
    arrived += [arrive(c) for c in range(1, last + 1)]

    steps = [(c, c, 0) for c in range(last + 1)]
    levels = [digits(n_pair, sizes) for sizes in SIZES]
    for c, masks in enumerate(levels):
        steps += [(c + n + n / 10 - 0.95 * (c == last), c, n) for n in range(1, len(masks))]
    parts, owners, offsets, token = [[] for _ in CHUNKS], [[] for _ in CHUNKS], [[] for _ in CHUNKS], []
    waiting = []

    def plan(c, level):
        mask, gone = levels[c][level], sum(levels[c][:level])
        flips = [o for o in range(1, n_pair) if not o & ~mask][::-1]
        left = [o for o in range(n_pair) if not o & gone]
        return [o for o in left if not o & mask], flips, [[o for o in left if o & mask == flip] for flip in flips]

    def send(c, level, messages):
        _, flips, sent = plan(c, level)
        before = [o for group in offsets[c] for o in group]
        for flip, some, message in zip(flips, sent, messages):
            offsets[c].append([o ^ flip for o in before])
            owners[c].append([o ^ flip for o in some])
            parts[c].append(flipped(message, "pair", n_pair, flip, f"z{flip}c{c}"))

    for _, c, level in sorted(steps):
        kept, _, sent = plan(c, level)
        if level == 0:
            blocks = [*near[c][:2], *arrived[c]]
            keep, *messages = half_of(place, blocks, turned, near[c][2], [kept, *sent], token)
            parts[c], owners[c], offsets[c] = [keep], [kept], [[0]]
        else:
            picks = [[[its.index(o) for o in some] for its in owners[c]] for some in sent]
            done = parts[c - 1][-1:] if level == 2 and c else []
            later = waiting if c == last and level == 1 else []
            messages, later = merge(parts[c], picks, later, token + done)
            if later:
                send(last - 1, 1, later)
        token = messages[:1]
        if c == last - 1 and level == 1:
            waiting = messages
        else:
            send(c, level, messages)
    token = [wait_for([x for x in parts[last][-3:]] + token)]
    pieces = [x for chunk in parts for x in chunk]
    sources = [(tuple(group), first) for chunk, first in zip(offsets, firsts) for group in chunk]
    return combine(pieces, sources, mirror, place, n_pair, token)


def solution(mesh):
    return jax.shard_map(
        functools.partial(on_device, mesh.shape["pair"], mesh.shape["mo"]),
        mesh=mesh,
        in_specs=(P("pair", "mo", None), P(), P()),
        out_specs=P(None, "pair", "mo"),
        check_vma=False,
    )
```

```python
import functools

import jax
import jax.numpy as jnp
from jax import lax
from jax.experimental import pallas as pl
from jax.experimental.pallas import tpu as pltpu
from jax.sharding import PartitionSpec as P

LANES = 128
STEP = 64
BATCHES = ((4, 4), (5, 3))
CHUNKS = sum(BATCHES, ())
SIZES = ((1,), (1,), (1, 2), (-1, 2))
PART = 256
MIB = 1024 * 1024
COST = pl.CostEstimate(flops=1024, bytes_accessed=1024, transcendentals=0)
IN_VMEM = pl.BlockSpec(memory_space=pltpu.VMEM)
IN_SMEM = pl.BlockSpec(memory_space=pltpu.SMEM)
ANYWHERE = pl.BlockSpec(memory_space=pl.ANY)
IN_HBM = pl.BlockSpec(memory_space=pltpu.MemorySpace.HBM)


def quarter_kernel(rows, n_mo, blocks, n_after, place_ref, x_ref, c_ref, *refs):
    refs = refs[n_after:]
    outs, (turn_ref, held, sems) = refs[:-3], refs[-3:]
    at = pl.program_id(0)
    step, some, depth = x_ref.shape
    padded = held.shape[2]
    many = PART // some

    @pl.when(at == 0)
    def _():
        to = lax.broadcasted_iota(jnp.int32, (PART, PART), 0)
        source = lax.broadcasted_iota(jnp.int32, (PART, PART), 1)
        bits = many.bit_length() - 1
        is_source = source == (to & (many - 1)) * some + (to >> bits)
        turn_ref[...] = jnp.where(is_source, 1.0, 0.0).astype(jnp.bfloat16)

    def fill(limit):
        x = x_ref[...].reshape(step * some, depth)
        product = jnp.dot(x, c_ref[...], preferred_element_type=jnp.float32)
        if limit is not None:
            line = lax.broadcasted_iota(jnp.int32, product.shape, 0)
            product = jnp.where(line < limit * some, product, 0.0)
        product = product.astype(jnp.bfloat16)
        for part in range(step // many):
            lines = jnp.dot(
                turn_ref[...], product[part * PART : (part + 1) * PART], preferred_element_type=jnp.float32
            ).astype(jnp.bfloat16)
            here = pl.ds(pl.multiple_of(at * step + part * many, many), many)
            for k in range(some):
                for d in range(n_mo):
                    held[d, k, here] = lines[k * many : (k + 1) * many, d * LANES : (d + 1) * LANES]

    steps = padded // step
    pl.when(at < steps - 1)(lambda: fill(None))
    pl.when(at == steps - 1)(lambda: fill(rows - (steps - 1) * step))
    here = pl.ds(pl.multiple_of(at * step, step), step)
    for n, (out, (o, first)) in enumerate(zip(outs, blocks)):
        mine = held.at[place_ref[0] ^ o, pl.ds(first, out.shape[0])]
        pltpu.make_async_copy(mine.at[:, here], out.at[:, here], sems.at[n]).start()

    @pl.when(at == padded // step - 1)
    def _():
        for n, (out, (o, first)) in enumerate(zip(outs, blocks)):
            mine = held.at[place_ref[0] ^ o, pl.ds(first, out.shape[0])]
            pltpu.make_async_copy(mine, out, sems.at[n]).wait()


def quarter_of(place, by_r, coeffs, n_mo, padded, batch, after):
    rows, _, depth = by_r.shape
    orbitals = coeffs.shape[1]
    chunks = BATCHES[batch]
    some = sum(chunks)
    blocks = [(0, 0), (1, 0)] + [(o, sum(chunks[:c])) for c in range(len(chunks)) for o in range(2, n_mo)]
    sizes = [some] * 2 + [kc for kc in chunks for _ in range(2, n_mo)]
    outs = [jax.ShapeDtypeStruct((kc, padded, LANES), jnp.bfloat16) for kc in sizes]
    out = pl.pallas_call(
        functools.partial(quarter_kernel, rows, n_mo, blocks, len(after)),
        grid_spec=pltpu.PrefetchScalarGridSpec(
            num_scalar_prefetch=1,
            grid=(padded // STEP,),
            in_specs=[pl.BlockSpec((STEP, some, depth), lambda r, place: (r, batch, 0)), IN_VMEM]
            + [ANYWHERE] * len(after),
            out_specs=[IN_HBM] * len(outs),
            scratch_shapes=[
                pltpu.VMEM((PART, PART), jnp.bfloat16),
                pltpu.VMEM((n_mo, some, padded, LANES), jnp.bfloat16),
                pltpu.SemaphoreType.DMA((len(outs),)),
            ],
        ),
        out_shape=outs,
        compiler_params=pltpu.CompilerParams(vmem_limit_bytes=50 * MIB),
        cost_estimate=COST,
        name="quarter",
    )(place, by_r, coeffs, *after)
    far = n_mo - 2
    return out[:2], [out[2 + far * c : 2 + far * (c + 1)] for c in range(len(chunks))]


def turn_kernel(rows, c_ref, *refs):
    out_ref = refs[-1]
    n_mo, orbitals, padded = out_ref.shape
    none = jnp.zeros((padded - rows, orbitals), jnp.float32)
    for n in range(n_mo):
        part = c_ref[n * rows : (n + 1) * rows, :].astype(jnp.float32)
        out_ref[n] = jnp.concatenate([part, none], axis=0).T.astype(jnp.bfloat16)


def turn(coeffs, n_mo, padded, later, after):
    depth, orbitals = coeffs.shape
    out = pl.pallas_call(
        functools.partial(turn_kernel, depth // n_mo),
        in_specs=[IN_VMEM] + [IN_HBM] * len(later) + [ANYWHERE] * len(after),
        out_specs=[IN_HBM] * len(later) + [IN_VMEM],
        out_shape=[jax.ShapeDtypeStruct(x.shape, x.dtype) for x in later]
        + [jax.ShapeDtypeStruct((n_mo, orbitals, padded), jnp.bfloat16)],
        input_output_aliases={1 + n: n for n in range(len(later))},
        compiler_params=pltpu.CompilerParams(vmem_limit_bytes=24 * MIB),
        cost_estimate=COST,
        name="turn",
    )(coeffs, *later, *after)
    return out[-1], list(out[:-1])


def half_kernel(n_mo, first, owners, place_ref, *refs):
    blocks, t_ref, held = refs[:n_mo], refs[n_mo], refs[-1]
    outs = refs[-1 - len(owners) : -1]
    kc, block, lanes = outs[0].shape[2:]
    firsts = [first if x.shape[0] > kc else 0 for x in blocks]
    columns = [jnp.concatenate([x[at + k] for k in range(kc)], axis=1) for x, at in zip(blocks, firsts)]
    turned = [t_ref[place_ref[0] ^ o] for o in range(n_mo)]
    held[...] = jnp.dot(
        jnp.concatenate(turned, axis=1), jnp.concatenate(columns, axis=0), preferred_element_type=jnp.float32
    )
    for out, its in zip(outs, owners):
        for at, o in enumerate(its):
            start = pl.multiple_of((place_ref[1] ^ o) * block, block)
            for k in range(kc):
                out[0, at, k] = held[pl.ds(start, block), k * lanes : (k + 1) * lanes].astype(jnp.bfloat16)


def half_of(place, blocks, turned, first, owners, after):
    n_mo, orbitals, _ = turned.shape
    kc, _, lanes = blocks[-1].shape
    block = orbitals // sum(len(its) for its in owners)
    return pl.pallas_call(
        functools.partial(half_kernel, n_mo, first, owners),
        in_specs=[IN_SMEM] + [IN_VMEM] * (n_mo + 1) + [ANYWHERE] * len(after),
        out_specs=[IN_VMEM] * len(owners),
        out_shape=[jax.ShapeDtypeStruct((1, len(its), kc, block, lanes), jnp.bfloat16) for its in owners],
        scratch_shapes=[pltpu.VMEM((orbitals, kc * lanes), jnp.float32)],
        compiler_params=pltpu.CompilerParams(vmem_limit_bytes=24 * MIB),
        cost_estimate=COST,
        name="half",
    )(place, *blocks, turned, *after)


def merge_kernel(n_parts, picks, *refs):
    outs = refs[len(refs) - len(picks) :]
    for out, its in zip(outs, picks):
        at = 0
        for x, pick in zip(refs[:n_parts], its):
            for i in range(x.shape[0]):
                for n, o in enumerate(pick):
                    out[at, n] = x[i, o]
                at += 1


def merge(parts, picks, later, after):
    lines, n = sum(x.shape[0] for x in parts), len(parts)
    out = pl.pallas_call(
        functools.partial(merge_kernel, n, picks),
        in_specs=[IN_VMEM] * n + [IN_HBM] * len(later) + [ANYWHERE] * len(after),
        out_specs=[IN_HBM] * len(later) + [IN_VMEM] * len(picks),
        out_shape=[jax.ShapeDtypeStruct(x.shape, x.dtype) for x in later]
        + [jax.ShapeDtypeStruct((lines, len(its[0]), *parts[0].shape[2:]), jnp.bfloat16) for its in picks],
        input_output_aliases={n + m: m for m in range(len(later))},
        compiler_params=pltpu.CompilerParams(vmem_limit_bytes=24 * MIB),
        cost_estimate=COST,
        name="merge",
    )(*parts, *later, *after)
    return list(out[len(later) :]), list(out[: len(later)])


def wait_kernel(*refs):
    refs[-1][...] = jnp.zeros_like(refs[-1])


def wait_for(after):
    return pl.pallas_call(
        wait_kernel,
        in_specs=[ANYWHERE] * len(after),
        out_specs=IN_VMEM,
        out_shape=jax.ShapeDtypeStruct((8, LANES), jnp.float32),
        compiler_params=pltpu.CompilerParams(vmem_limit_bytes=24 * MIB),
        cost_estimate=COST,
        name="wait",
    )(*after)


def combine_kernel(sources, k_all, per_step, mirror_ref, place_ref, *refs):
    pieces, out_ref, held = refs[: len(sources)], refs[-2], refs[-1]
    step = pl.program_id(0)

    @pl.when(step == 0)
    def _():
        for piece, (offsets, first) in zip(pieces, sources):
            for n, offset in enumerate(offsets):
                row = (place_ref[1] ^ offset) * k_all + first
                held[pl.ds(row, piece.shape[2])] = piece[n, 0]

    for n in range(per_step):
        k = step * per_step + n
        out_ref[n] = 0.5 * (held[k].astype(jnp.float32) + held[mirror_ref[k]].astype(jnp.float32))


def combine(pieces, sources, mirror, place, n_pair, after):
    block, lanes = pieces[0].shape[-2:]
    k_all = sum(CHUNKS)
    rows = n_pair * k_all
    per_step = max(1, 32 * 64 // block)
    return pl.pallas_call(
        functools.partial(combine_kernel, sources, k_all, per_step),
        grid_spec=pltpu.PrefetchScalarGridSpec(
            num_scalar_prefetch=2,
            grid=(rows // per_step,),
            in_specs=[IN_VMEM] * len(pieces) + [ANYWHERE] * len(after),
            out_specs=pl.BlockSpec((per_step, block, lanes), lambda k, m, place: (k, 0, 0)),
            scratch_shapes=[pltpu.VMEM((rows, block, lanes), jnp.bfloat16)],
        ),
        out_shape=jax.ShapeDtypeStruct((rows, block, lanes), jnp.float32),
        compiler_params=pltpu.CompilerParams(vmem_limit_bytes=24 * MIB),
        cost_estimate=COST,
        name="combine",
    )(mirror, place, *pieces, *after)


def flipped(x, axis, size, offset, name):
    with jax.named_scope(name):
        return lax.ppermute(x, axis, [(i, i ^ offset) for i in range(size)])


def digits(n_pair, sizes):
    bits = [1 << n for n in reversed(range(n_pair.bit_length() - 1))]
    masks = []
    while bits:
        size = sizes[min(len(masks), len(sizes) - 1)]
        some = bits[:size] if size > 0 else bits[size:]
        masks.append(sum(some))
        bits = [bit for bit in bits if bit not in some]
    return masks


def on_device(n_pair, n_mo, integrals, coeffs, mirror):
    rows = integrals.shape[1]
    padded = -(-rows // STEP) * STEP
    n_near = n_pair // 2
    by_r = jnp.transpose(integrals, (1, 0, 2))
    place = jnp.stack([lax.axis_index("mo"), lax.axis_index("pair")]).astype(jnp.int32)
    last = len(CHUNKS) - 1
    firsts = [sum(CHUNKS[:c]) for c in range(last + 1)]

    near, queue, token = [], [], []
    for batch, chunks in enumerate(BATCHES):
        (own, beside), far = quarter_of(place, by_r, coeffs, n_mo, padded, batch, token)
        beside = flipped(beside, "mo", n_mo, 1, f"beside{batch}")
        near += [(own, beside, sum(chunks[:c])) for c in range(len(chunks))]
        queue += far
        token = [own]

    def arrive(c):
        return [flipped(x, "mo", n_mo, o, f"y{2 * c + o - 2}") for o, x in enumerate(queue[c], 2)]

    arrived = [arrive(0)]
    turned, queue[1] = turn(coeffs, n_mo, padded, queue[1], arrived[0][:1] + token)
    arrived += [arrive(c) for c in range(1, last + 1)]

    steps = [(c, c, 0) for c in range(last + 1)]
    levels = [digits(n_pair, sizes) for sizes in SIZES]
    for c, masks in enumerate(levels):
        steps += [(c + n + n / 10 - 0.95 * (c == last), c, n) for n in range(1, len(masks))]
    parts, owners, offsets, token = [[] for _ in CHUNKS], [[] for _ in CHUNKS], [[] for _ in CHUNKS], []
    waiting = []

    def plan(c, level):
        mask, gone = levels[c][level], sum(levels[c][:level])
        flips = [o for o in range(1, n_pair) if not o & ~mask][::-1]
        left = [o for o in range(n_pair) if not o & gone]
        return [o for o in left if not o & mask], flips, [[o for o in left if o & mask == flip] for flip in flips]

    def send(c, level, messages):
        _, flips, sent = plan(c, level)
        before = [o for group in offsets[c] for o in group]
        for flip, some, message in zip(flips, sent, messages):
            offsets[c].append([o ^ flip for o in before])
            owners[c].append([o ^ flip for o in some])
            parts[c].append(flipped(message, "pair", n_pair, flip, f"z{flip}c{c}"))

    for _, c, level in sorted(steps):
        kept, _, sent = plan(c, level)
        if level == 0:
            blocks = [*near[c][:2], *arrived[c]]
            keep, *messages = half_of(place, blocks, turned, near[c][2], [kept, *sent], token)
            parts[c], owners[c], offsets[c] = [keep], [kept], [[0]]
        else:
            picks = [[[its.index(o) for o in some] for its in owners[c]] for some in sent]
            done = parts[c - 1][-1:] if level == 2 and c else []
            later = waiting if c == last and level == 1 else []
            messages, later = merge(parts[c], picks, later, token + done)
            if later:
                send(last - 1, 1, later)
        token = messages[:1]
        if c == last - 1 and level == 1:
            waiting = messages
        else:
            send(c, level, messages)
    for x in parts[last][-3:]:
        token = [wait_for([x, *token])]
    pieces = [x for chunk in parts for x in chunk]
    sources = [(tuple(group), first) for chunk, first in zip(offsets, firsts) for group in chunk]
    return combine(pieces, sources, mirror, place, n_pair, token)


def solution(mesh):
    return jax.shard_map(
        functools.partial(on_device, mesh.shape["pair"], mesh.shape["mo"]),
        mesh=mesh,
        in_specs=(P("pair", "mo", None), P(), P()),
        out_specs=P(None, "pair", "mo"),
        check_vma=False,
    )
```

```python
import functools

import jax
import jax.numpy as jnp
from jax import lax
from jax.experimental import pallas as pl
from jax.experimental.pallas import tpu as pltpu
from jax.sharding import PartitionSpec as P

LANES = 128
STEP = 64
BATCHES = ((4, 4), (4, 4))
CHUNKS = sum(BATCHES, ())
SIZES = ((1,), (1,), (1, 2), (-1, 2))
PART = 256
MIB = 1024 * 1024
COST = pl.CostEstimate(flops=1024, bytes_accessed=1024, transcendentals=0)
IN_VMEM = pl.BlockSpec(memory_space=pltpu.VMEM)
IN_SMEM = pl.BlockSpec(memory_space=pltpu.SMEM)
ANYWHERE = pl.BlockSpec(memory_space=pl.ANY)
IN_HBM = pl.BlockSpec(memory_space=pltpu.MemorySpace.HBM)


def quarter_kernel(rows, far, n_after, place_ref, x_ref, c_ref, *refs):
    outs, turn_ref = refs[n_after:-1], refs[-1]
    at = pl.program_id(0)
    step, some, depth = x_ref.shape
    padded = outs[0].shape[1]
    many = PART // some

    @pl.when(at == 0)
    def _():
        to = lax.broadcasted_iota(jnp.int32, (PART, PART), 0)
        source = lax.broadcasted_iota(jnp.int32, (PART, PART), 1)
        bits = many.bit_length() - 1
        is_source = source == (to & (many - 1)) * some + (to >> bits)
        turn_ref[...] = jnp.where(is_source, 1.0, 0.0).astype(jnp.bfloat16)

    def fill(limit):
        x = x_ref[...].reshape(step * some, depth)
        odd = (place_ref[0] & 1) == 1
        for n, which in enumerate(far):
            columns = pl.ds(pl.multiple_of(((place_ref[0] >> 1) ^ which) * 2 * LANES, 2 * LANES), 2 * LANES)
            product = jnp.dot(x, c_ref[:, columns], preferred_element_type=jnp.float32)
            if limit is not None:
                line = lax.broadcasted_iota(jnp.int32, product.shape, 0)
                product = jnp.where(line < limit * some, product, 0.0)
            low, high = product[:, :LANES], product[:, LANES:]
            product = [jnp.where(odd, high, low).astype(jnp.bfloat16), jnp.where(odd, low, high).astype(jnp.bfloat16)]
            product = jnp.concatenate(product, axis=1)
            for part in range(step // many):
                lines = jnp.dot(
                    turn_ref[...], product[part * PART : (part + 1) * PART], preferred_element_type=jnp.float32
                ).astype(jnp.bfloat16)
                here = pl.ds(pl.multiple_of(at * step + part * many, many), many)
                mine = outs[n * len(outs) // len(far) : (n + 1) * len(outs) // len(far)]
                for o in range(2):
                    k = 0
                    for out in mine[o::2]:
                        for row in range(out.shape[0]):
                            out[row, here] = lines[k * many : (k + 1) * many, o * LANES : (o + 1) * LANES]
                            k += 1

    steps = padded // step
    pl.when(at < steps - 1)(lambda: fill(None))
    pl.when(at == steps - 1)(lambda: fill(rows - (steps - 1) * step))


def quarter_of(place, by_r, coeffs, padded, batch, far, after):
    rows, _, depth = by_r.shape
    chunks = BATCHES[batch]
    some = sum(chunks)
    outs = [
        jax.ShapeDtypeStruct((kc, padded, LANES), jnp.bfloat16) for _ in far for kc in chunks for _ in range(2)
    ]
    out = pl.pallas_call(
        functools.partial(quarter_kernel, rows, far, len(after)),
        grid_spec=pltpu.PrefetchScalarGridSpec(
            num_scalar_prefetch=1,
            grid=(padded // STEP,),
            in_specs=[pl.BlockSpec((STEP, some, depth), lambda r, place: (r, batch, 0)), IN_VMEM]
            + [ANYWHERE] * len(after),
            out_specs=[IN_VMEM] * len(outs),
            scratch_shapes=[pltpu.VMEM((PART, PART), jnp.bfloat16)],
        ),
        out_shape=outs,
        compiler_params=pltpu.CompilerParams(vmem_limit_bytes=52 * MIB),
        cost_estimate=COST,
        name="quarter",
    )(place, by_r, coeffs, *after)
    pairs = [list(out[n : n + 2]) for n in range(0, len(out), 2)]
    return [pairs[n * len(chunks) : (n + 1) * len(chunks)] for n in range(len(far))]


def turn_kernel(rows, c_ref, *refs):
    out_ref = refs[-1]
    n_mo, orbitals, padded = out_ref.shape
    none = jnp.zeros((padded - rows, orbitals), jnp.float32)
    for n in range(n_mo):
        part = c_ref[n * rows : (n + 1) * rows, :].astype(jnp.float32)
        out_ref[n] = jnp.concatenate([part, none], axis=0).T.astype(jnp.bfloat16)


def turn(coeffs, n_mo, padded, later, after):
    depth, orbitals = coeffs.shape
    out = pl.pallas_call(
        functools.partial(turn_kernel, depth // n_mo),
        in_specs=[IN_VMEM] + [IN_HBM] * len(later) + [ANYWHERE] * len(after),
        out_specs=[IN_HBM] * len(later) + [IN_VMEM],
        out_shape=[jax.ShapeDtypeStruct(x.shape, x.dtype) for x in later]
        + [jax.ShapeDtypeStruct((n_mo, orbitals, padded), jnp.bfloat16)],
        input_output_aliases={1 + n: n for n in range(len(later))},
        compiler_params=pltpu.CompilerParams(vmem_limit_bytes=24 * MIB),
        cost_estimate=COST,
        name="turn",
    )(coeffs, *later, *after)
    return out[-1], list(out[:-1])


def half_kernel(n_mo, owners, place_ref, *refs):
    blocks, t_ref, held = refs[:n_mo], refs[n_mo], refs[-1]
    outs = refs[-1 - len(owners) : -1]
    kc, block, lanes = outs[0].shape[2:]
    columns = [jnp.concatenate([x[k] for k in range(kc)], axis=1) for x in blocks]
    turned = [t_ref[place_ref[0] ^ o] for o in range(n_mo)]
    held[...] = jnp.dot(
        jnp.concatenate(turned, axis=1), jnp.concatenate(columns, axis=0), preferred_element_type=jnp.float32
    )
    for out, its in zip(outs, owners):
        for at, o in enumerate(its):
            start = pl.multiple_of((place_ref[1] ^ o) * block, block)
            for k in range(kc):
                out[0, at, k] = held[pl.ds(start, block), k * lanes : (k + 1) * lanes].astype(jnp.bfloat16)


def half_of(place, blocks, turned, owners, after):
    n_mo, orbitals, _ = turned.shape
    kc, _, lanes = blocks[-1].shape
    block = orbitals // sum(len(its) for its in owners)
    return pl.pallas_call(
        functools.partial(half_kernel, n_mo, owners),
        in_specs=[IN_SMEM] + [IN_VMEM] * (n_mo + 1) + [ANYWHERE] * len(after),
        out_specs=[IN_VMEM] * len(owners),
        out_shape=[jax.ShapeDtypeStruct((1, len(its), kc, block, lanes), jnp.bfloat16) for its in owners],
        scratch_shapes=[pltpu.VMEM((orbitals, kc * lanes), jnp.float32)],
        compiler_params=pltpu.CompilerParams(vmem_limit_bytes=24 * MIB),
        cost_estimate=COST,
        name="half",
    )(place, *blocks, turned, *after)


def merge_kernel(n_parts, picks, *refs):
    outs = refs[len(refs) - len(picks) :]
    for out, its in zip(outs, picks):
        at = 0
        for x, pick in zip(refs[:n_parts], its):
            for i in range(x.shape[0]):
                for n, o in enumerate(pick):
                    out[at, n] = x[i, o]
                at += 1


def merge(parts, picks, later, after):
    lines, n = sum(x.shape[0] for x in parts), len(parts)
    out = pl.pallas_call(
        functools.partial(merge_kernel, n, picks),
        in_specs=[IN_VMEM] * n + [IN_HBM] * len(later) + [ANYWHERE] * len(after),
        out_specs=[IN_HBM] * len(later) + [IN_VMEM] * len(picks),
        out_shape=[jax.ShapeDtypeStruct(x.shape, x.dtype) for x in later]
        + [jax.ShapeDtypeStruct((lines, len(its[0]), *parts[0].shape[2:]), jnp.bfloat16) for its in picks],
        input_output_aliases={n + m: m for m in range(len(later))},
        compiler_params=pltpu.CompilerParams(vmem_limit_bytes=24 * MIB),
        cost_estimate=COST,
        name="merge",
    )(*parts, *later, *after)
    return list(out[len(later) :]), list(out[: len(later)])


def wait_kernel(*refs):
    refs[-1][...] = jnp.zeros_like(refs[-1])


def wait_for(after):
    return pl.pallas_call(
        wait_kernel,
        in_specs=[ANYWHERE] * len(after),
        out_specs=IN_VMEM,
        out_shape=jax.ShapeDtypeStruct((8, LANES), jnp.float32),
        compiler_params=pltpu.CompilerParams(vmem_limit_bytes=24 * MIB),
        cost_estimate=COST,
        name="wait",
    )(*after)


def combine_kernel(sources, k_all, per_step, mirror_ref, place_ref, *refs):
    pieces, out_ref, held = refs[: len(sources)], refs[-2], refs[-1]
    step = pl.program_id(0)

    @pl.when(step == 0)
    def _():
        for piece, (offsets, first) in zip(pieces, sources):
            for n, offset in enumerate(offsets):
                row = (place_ref[1] ^ offset) * k_all + first
                held[pl.ds(row, piece.shape[2])] = piece[n, 0]

    for n in range(per_step):
        k = step * per_step + n
        out_ref[n] = 0.5 * (held[k].astype(jnp.float32) + held[mirror_ref[k]].astype(jnp.float32))


def combine(pieces, sources, mirror, place, n_pair, after):
    block, lanes = pieces[0].shape[-2:]
    k_all = sum(CHUNKS)
    rows = n_pair * k_all
    per_step = max(1, 32 * 64 // block)
    return pl.pallas_call(
        functools.partial(combine_kernel, sources, k_all, per_step),
        grid_spec=pltpu.PrefetchScalarGridSpec(
            num_scalar_prefetch=2,
            grid=(rows // per_step,),
            in_specs=[IN_VMEM] * len(pieces) + [ANYWHERE] * len(after),
            out_specs=pl.BlockSpec((per_step, block, lanes), lambda k, m, place: (k, 0, 0)),
            scratch_shapes=[pltpu.VMEM((rows, block, lanes), jnp.bfloat16)],
        ),
        out_shape=jax.ShapeDtypeStruct((rows, block, lanes), jnp.float32),
        compiler_params=pltpu.CompilerParams(vmem_limit_bytes=24 * MIB),
        cost_estimate=COST,
        name="combine",
    )(mirror, place, *pieces, *after)


def flipped(x, axis, size, offset, name):
    with jax.named_scope(name):
        return lax.ppermute(x, axis, [(i, i ^ offset) for i in range(size)])


def digits(n_pair, sizes):
    bits = [1 << n for n in reversed(range(n_pair.bit_length() - 1))]
    masks = []
    while bits:
        size = sizes[min(len(masks), len(sizes) - 1)]
        some = bits[:size] if size > 0 else bits[size:]
        masks.append(sum(some))
        bits = [bit for bit in bits if bit not in some]
    return masks


def on_device(n_pair, n_mo, integrals, coeffs, mirror):
    rows = integrals.shape[1]
    padded = -(-rows // STEP) * STEP
    n_near = n_pair // 2
    by_r = jnp.transpose(integrals, (1, 0, 2))
    place = jnp.stack([lax.axis_index("mo"), lax.axis_index("pair")]).astype(jnp.int32)
    last = len(CHUNKS) - 1
    firsts = [sum(CHUNKS[:c]) for c in range(last + 1)]

    others = list(range(1, n_mo // 2))
    blocks = quarter_of(place, by_r, coeffs, padded, 0, others, [])
    queue = [sum(some, []) for some in zip(*blocks)]
    (near,) = quarter_of(place, by_r, coeffs, padded, 0, [0], queue[0][:1])
    token = near[0][:1]
    for batch in range(1, len(BATCHES)):
        blocks = quarter_of(place, by_r, coeffs, padded, batch, [0, *others], token)
        near += blocks[0]
        queue += [sum(some, []) for some in zip(*blocks[1:])]
        token = blocks[0][0][:1]
    near = [(own, flipped(beside, "mo", n_mo, 1, f"beside{c}")) for c, (own, beside) in enumerate(near)]

    def arrive(c):
        return [flipped(x, "mo", n_mo, o, f"y{2 * c + o - 2}") for o, x in enumerate(queue[c], 2)]

    arrived = [arrive(0)]
    turned, queue[1] = turn(coeffs, n_mo, padded, queue[1], arrived[0][:1] + token)
    arrived += [arrive(c) for c in range(1, last + 1)]

    steps = [(c, c, 0) for c in range(last + 1)]
    levels = [digits(n_pair, sizes) for sizes in SIZES]
    for c, masks in enumerate(levels):
        steps += [(c + n + n / 10 - 0.95 * (c == last), c, n) for n in range(1, len(masks))]
    parts, owners, offsets, token = [[] for _ in CHUNKS], [[] for _ in CHUNKS], [[] for _ in CHUNKS], []
    waiting = []

    def plan(c, level):
        mask, gone = levels[c][level], sum(levels[c][:level])
        flips = [o for o in range(1, n_pair) if not o & ~mask][::-1]
        left = [o for o in range(n_pair) if not o & gone]
        return [o for o in left if not o & mask], flips, [[o for o in left if o & mask == flip] for flip in flips]

    def send(c, level, messages):
        _, flips, sent = plan(c, level)
        before = [o for group in offsets[c] for o in group]
        for flip, some, message in zip(flips, sent, messages):
            offsets[c].append([o ^ flip for o in before])
            owners[c].append([o ^ flip for o in some])
            parts[c].append(flipped(message, "pair", n_pair, flip, f"z{flip}c{c}"))

    for _, c, level in sorted(steps):
        kept, _, sent = plan(c, level)
        if level == 0:
            blocks = [*near[c], *arrived[c]]
            keep, *messages = half_of(place, blocks, turned, [kept, *sent], token)
            parts[c], owners[c], offsets[c] = [keep], [kept], [[0]]
        else:
            picks = [[[its.index(o) for o in some] for its in owners[c]] for some in sent]
            done = parts[c - 1][-1:] if level == 2 and c else []
            later = waiting if c == last and level == 1 else []
            messages, later = merge(parts[c], picks, later, token + done)
            if later:
                send(last - 1, 1, later)
        token = messages[:1]
        if c == last - 1 and level == 1:
            waiting = messages
        else:
            send(c, level, messages)
    for x in parts[last][-3:]:
        token = [wait_for([x, *token])]
    pieces = [x for chunk in parts for x in chunk]
    sources = [(tuple(group), first) for chunk, first in zip(offsets, firsts) for group in chunk]
    return combine(pieces, sources, mirror, place, n_pair, token)


def solution(mesh):
    return jax.shard_map(
        functools.partial(on_device, mesh.shape["pair"], mesh.shape["mo"]),
        mesh=mesh,
        in_specs=(P("pair", "mo", None), P(), P()),
        out_specs=P(None, "pair", "mo"),
        check_vma=False,
    )
```

```python
import functools

import jax
import jax.numpy as jnp
from jax import lax
from jax.experimental import pallas as pl
from jax.experimental.pallas import tpu as pltpu
from jax.sharding import PartitionSpec as P

LANES = 128
STEP = 32
BATCHES = ((4, 4), (4, 4))
CHUNKS = sum(BATCHES, ())
SIZES = ((1,), (1,), (1, 2), (-1, 2))
PART = 256
MIB = 1024 * 1024
COST = pl.CostEstimate(flops=1024, bytes_accessed=1024, transcendentals=0)
IN_VMEM = pl.BlockSpec(memory_space=pltpu.VMEM)
IN_SMEM = pl.BlockSpec(memory_space=pltpu.SMEM)
ANYWHERE = pl.BlockSpec(memory_space=pl.ANY)
IN_HBM = pl.BlockSpec(memory_space=pltpu.MemorySpace.HBM)


def quarter_kernel(rows, n_mo, blocks, n_after, place_ref, x_ref, c_ref, *refs):
    refs = refs[n_after:]
    outs, (turn_ref, held, sems) = refs[:-3], refs[-3:]
    at = pl.program_id(0)
    step, some, depth = x_ref.shape
    padded = held.shape[2]
    many = PART // some

    @pl.when(at == 0)
    def _():
        to = lax.broadcasted_iota(jnp.int32, (PART, PART), 0)
        source = lax.broadcasted_iota(jnp.int32, (PART, PART), 1)
        bits = many.bit_length() - 1
        is_source = source == (to & (many - 1)) * some + (to >> bits)
        turn_ref[...] = jnp.where(is_source, 1.0, 0.0).astype(jnp.bfloat16)

    x = x_ref[...].reshape(step * some, depth)
    product = jnp.dot(x, c_ref[...], preferred_element_type=jnp.float32)
    line = lax.broadcasted_iota(jnp.int32, product.shape, 0)
    product = jnp.where(line < (rows - at * step) * some, product, 0.0).astype(jnp.bfloat16)
    for part in range(step // many):
        lines = jnp.dot(
            turn_ref[...], product[part * PART : (part + 1) * PART], preferred_element_type=jnp.float32
        ).astype(jnp.bfloat16)
        here = pl.ds(pl.multiple_of(at * step + part * many, many), many)
        for k in range(some):
            for d in range(n_mo):
                held[d, k, here] = lines[k * many : (k + 1) * many, d * LANES : (d + 1) * LANES]
    here = pl.ds(pl.multiple_of(at * step, step), step)
    for n, (out, (o, first)) in enumerate(zip(outs, blocks)):
        mine = held.at[place_ref[0] ^ o, pl.ds(first, out.shape[0])]
        pltpu.make_async_copy(mine.at[:, here], out.at[:, here], sems.at[n]).start()

    @pl.when(at == padded // step - 1)
    def _():
        for n, (out, (o, first)) in enumerate(zip(outs, blocks)):
            mine = held.at[place_ref[0] ^ o, pl.ds(first, out.shape[0])]
            pltpu.make_async_copy(mine, out, sems.at[n]).wait()


def quarter_of(place, by_r, coeffs, n_mo, padded, batch, after):
    rows, _, depth = by_r.shape
    orbitals = coeffs.shape[1]
    chunks = BATCHES[batch]
    some = sum(chunks)
    blocks = [(0, 0), (1, 0)] + [(o, sum(chunks[:c])) for c in range(len(chunks)) for o in range(2, n_mo)]
    sizes = [some] * 2 + [kc for kc in chunks for _ in range(2, n_mo)]
    outs = [jax.ShapeDtypeStruct((kc, padded, LANES), jnp.bfloat16) for kc in sizes]
    out = pl.pallas_call(
        functools.partial(quarter_kernel, rows, n_mo, blocks, len(after)),
        grid_spec=pltpu.PrefetchScalarGridSpec(
            num_scalar_prefetch=1,
            grid=(padded // STEP,),
            in_specs=[pl.BlockSpec((STEP, some, depth), lambda r, place: (r, batch, 0)), IN_VMEM]
            + [ANYWHERE] * len(after),
            out_specs=[IN_HBM] * len(outs),
            scratch_shapes=[
                pltpu.VMEM((PART, PART), jnp.bfloat16),
                pltpu.VMEM((n_mo, some, padded, LANES), jnp.bfloat16),
                pltpu.SemaphoreType.DMA((len(outs),)),
            ],
        ),
        out_shape=outs,
        compiler_params=pltpu.CompilerParams(vmem_limit_bytes=51 * MIB),
        cost_estimate=COST,
        name="quarter",
    )(place, by_r, coeffs, *after)
    far = n_mo - 2
    return out[:2], [out[2 + far * c : 2 + far * (c + 1)] for c in range(len(chunks))]


def turn_kernel(rows, c_ref, *refs):
    out_ref = refs[-1]
    n_mo, orbitals, padded = out_ref.shape
    none = jnp.zeros((padded - rows, orbitals), jnp.float32)
    for n in range(n_mo):
        part = c_ref[n * rows : (n + 1) * rows, :].astype(jnp.float32)
        out_ref[n] = jnp.concatenate([part, none], axis=0).T.astype(jnp.bfloat16)


def turn(coeffs, n_mo, padded, later, after):
    depth, orbitals = coeffs.shape
    out = pl.pallas_call(
        functools.partial(turn_kernel, depth // n_mo),
        in_specs=[IN_VMEM] + [IN_HBM] * len(later) + [ANYWHERE] * len(after),
        out_specs=[IN_HBM] * len(later) + [IN_VMEM],
        out_shape=[jax.ShapeDtypeStruct(x.shape, x.dtype) for x in later]
        + [jax.ShapeDtypeStruct((n_mo, orbitals, padded), jnp.bfloat16)],
        input_output_aliases={1 + n: n for n in range(len(later))},
        compiler_params=pltpu.CompilerParams(vmem_limit_bytes=24 * MIB),
        cost_estimate=COST,
        name="turn",
    )(coeffs, *later, *after)
    return out[-1], list(out[:-1])


def half_kernel(n_mo, first, owners, place_ref, *refs):
    blocks, t_ref, held = refs[:n_mo], refs[n_mo], refs[-1]
    outs = refs[-1 - len(owners) : -1]
    kc, block, lanes = outs[0].shape[2:]

    @pl.loop(0, kc // 2)
    def _(pair):
        columns = []
        for x in blocks:
            at = 2 * pair + (first if x.shape[0] > kc else 0)
            columns.append(jnp.concatenate([x[at], x[at + 1]], axis=1))
        turned = [t_ref[place_ref[0] ^ o] for o in range(n_mo)]
        held[...] = jnp.dot(
            jnp.concatenate(turned, axis=1), jnp.concatenate(columns, axis=0), preferred_element_type=jnp.float32
        )
        for out, its in zip(outs, owners):
            for at, o in enumerate(its):
                start = pl.multiple_of((place_ref[1] ^ o) * block, block)
                for n in range(2):
                    piece = held[pl.ds(start, block), n * lanes : (n + 1) * lanes]
                    out[0, at, 2 * pair + n] = piece.astype(jnp.bfloat16)


def half_of(place, blocks, turned, first, owners, after):
    n_mo, orbitals, _ = turned.shape
    kc, _, lanes = blocks[-1].shape
    block = orbitals // sum(len(its) for its in owners)
    return pl.pallas_call(
        functools.partial(half_kernel, n_mo, first, owners),
        in_specs=[IN_SMEM] + [IN_VMEM] * (n_mo + 1) + [ANYWHERE] * len(after),
        out_specs=[IN_VMEM] * len(owners),
        out_shape=[jax.ShapeDtypeStruct((1, len(its), kc, block, lanes), jnp.bfloat16) for its in owners],
        scratch_shapes=[pltpu.VMEM((orbitals, 2 * lanes), jnp.float32)],
        compiler_params=pltpu.CompilerParams(vmem_limit_bytes=24 * MIB),
        cost_estimate=COST,
        name="half",
    )(place, *blocks, turned, *after)


def merge_kernel(n_parts, picks, *refs):
    outs = refs[len(refs) - len(picks) :]
    for out, its in zip(outs, picks):
        at = 0
        for x, pick in zip(refs[:n_parts], its):
            for i in range(x.shape[0]):
                for n, o in enumerate(pick):
                    out[at, n] = x[i, o]
                at += 1


def merge(parts, picks, later, after):
    lines, n = sum(x.shape[0] for x in parts), len(parts)
    out = pl.pallas_call(
        functools.partial(merge_kernel, n, picks),
        in_specs=[IN_VMEM] * n + [IN_HBM] * len(later) + [ANYWHERE] * len(after),
        out_specs=[IN_HBM] * len(later) + [IN_VMEM] * len(picks),
        out_shape=[jax.ShapeDtypeStruct(x.shape, x.dtype) for x in later]
        + [jax.ShapeDtypeStruct((lines, len(its[0]), *parts[0].shape[2:]), jnp.bfloat16) for its in picks],
        input_output_aliases={n + m: m for m in range(len(later))},
        compiler_params=pltpu.CompilerParams(vmem_limit_bytes=24 * MIB),
        cost_estimate=COST,
        name="merge",
    )(*parts, *later, *after)
    return list(out[len(later) :]), list(out[: len(later)])


def wait_kernel(*refs):
    refs[-1][...] = jnp.zeros_like(refs[-1])


def wait_for(after):
    return pl.pallas_call(
        wait_kernel,
        in_specs=[ANYWHERE] * len(after),
        out_specs=IN_VMEM,
        out_shape=jax.ShapeDtypeStruct((8, LANES), jnp.float32),
        compiler_params=pltpu.CompilerParams(vmem_limit_bytes=24 * MIB),
        cost_estimate=COST,
        name="wait",
    )(*after)


def combine_kernel(sources, k_all, per_step, mirror_ref, place_ref, *refs):
    pieces, out_ref, held = refs[: len(sources)], refs[-2], refs[-1]
    step = pl.program_id(0)

    @pl.when(step == 0)
    def _():
        for piece, (offsets, first) in zip(pieces, sources):
            for n, offset in enumerate(offsets):
                row = (place_ref[1] ^ offset) * k_all + first
                held[pl.ds(row, piece.shape[2])] = piece[n, 0]

    for n in range(per_step):
        k = step * per_step + n
        out_ref[n] = 0.5 * (held[k].astype(jnp.float32) + held[mirror_ref[k]].astype(jnp.float32))


def combine(pieces, sources, mirror, place, n_pair, after):
    block, lanes = pieces[0].shape[-2:]
    k_all = sum(CHUNKS)
    rows = n_pair * k_all
    per_step = max(1, 32 * 64 // block)
    return pl.pallas_call(
        functools.partial(combine_kernel, sources, k_all, per_step),
        grid_spec=pltpu.PrefetchScalarGridSpec(
            num_scalar_prefetch=2,
            grid=(rows // per_step,),
            in_specs=[IN_VMEM] * len(pieces) + [ANYWHERE] * len(after),
            out_specs=pl.BlockSpec((per_step, block, lanes), lambda k, m, place: (k, 0, 0)),
            scratch_shapes=[pltpu.VMEM((rows, block, lanes), jnp.bfloat16)],
        ),
        out_shape=jax.ShapeDtypeStruct((rows, block, lanes), jnp.float32),
        compiler_params=pltpu.CompilerParams(vmem_limit_bytes=24 * MIB),
        cost_estimate=COST,
        name="combine",
    )(mirror, place, *pieces, *after)


def flipped(x, axis, size, offset, name):
    with jax.named_scope(name):
        return lax.ppermute(x, axis, [(i, i ^ offset) for i in range(size)])


def digits(n_pair, sizes):
    bits = [1 << n for n in reversed(range(n_pair.bit_length() - 1))]
    masks = []
    while bits:
        size = sizes[min(len(masks), len(sizes) - 1)]
        some = bits[:size] if size > 0 else bits[size:]
        masks.append(sum(some))
        bits = [bit for bit in bits if bit not in some]
    return masks


def on_device(n_pair, n_mo, integrals, coeffs, mirror):
    rows = integrals.shape[1]
    padded = -(-rows // STEP) * STEP
    n_near = n_pair // 2
    by_r = jnp.transpose(integrals, (1, 0, 2))
    place = jnp.stack([lax.axis_index("mo"), lax.axis_index("pair")]).astype(jnp.int32)
    last = len(CHUNKS) - 1
    firsts = [sum(CHUNKS[:c]) for c in range(last + 1)]

    near, queue, token = [], [], []
    for batch, chunks in enumerate(BATCHES):
        (own, beside), far = quarter_of(place, by_r, coeffs, n_mo, padded, batch, token)
        beside = flipped(beside, "mo", n_mo, 1, f"beside{batch}")
        near += [(own, beside, sum(chunks[:c])) for c in range(len(chunks))]
        queue += far
        token = [own]

    def arrive(c):
        return [flipped(x, "mo", n_mo, o, f"y{2 * c + o - 2}") for o, x in enumerate(queue[c], 2)]

    arrived = [arrive(0)]
    turned, queue[1] = turn(coeffs, n_mo, padded, queue[1], arrived[0][:1] + token)
    arrived += [arrive(c) for c in range(1, last + 1)]

    steps = [(c, c, 0) for c in range(last + 1)]
    levels = [digits(n_pair, sizes) for sizes in SIZES]
    for c, masks in enumerate(levels):
        steps += [(c + n + n / 10 - 0.95 * (c == last), c, n) for n in range(1, len(masks))]
    parts, owners, offsets, token = [[] for _ in CHUNKS], [[] for _ in CHUNKS], [[] for _ in CHUNKS], []
    waiting = []

    def plan(c, level):
        mask, gone = levels[c][level], sum(levels[c][:level])
        flips = [o for o in range(1, n_pair) if not o & ~mask][::-1]
        left = [o for o in range(n_pair) if not o & gone]
        return [o for o in left if not o & mask], flips, [[o for o in left if o & mask == flip] for flip in flips]

    def send(c, level, messages):
        _, flips, sent = plan(c, level)
        before = [o for group in offsets[c] for o in group]
        for flip, some, message in zip(flips, sent, messages):
            offsets[c].append([o ^ flip for o in before])
            owners[c].append([o ^ flip for o in some])
            parts[c].append(flipped(message, "pair", n_pair, flip, f"z{flip}c{c}"))

    for _, c, level in sorted(steps):
        kept, _, sent = plan(c, level)
        if level == 0:
            blocks = [*near[c][:2], *arrived[c]]
            keep, *messages = half_of(place, blocks, turned, near[c][2], [kept, *sent], token)
            parts[c], owners[c], offsets[c] = [keep], [kept], [[0]]
        else:
            picks = [[[its.index(o) for o in some] for its in owners[c]] for some in sent]
            done = parts[c - 1][-1:] if level == 2 and c else []
            later = waiting if c == last and level == 1 else []
            messages, later = merge(parts[c], picks, later, token + done)
            if later:
                send(last - 1, 1, later)
        token = messages[:1]
        if c == last - 1 and level == 1:
            waiting = messages
        else:
            send(c, level, messages)
    for x in parts[last][-3:]:
        token = [wait_for([x, *token])]
    pieces = [x for chunk in parts for x in chunk]
    sources = [(tuple(group), first) for chunk, first in zip(offsets, firsts) for group in chunk]
    return combine(pieces, sources, mirror, place, n_pair, token)


def solution(mesh):
    return jax.shard_map(
        functools.partial(on_device, mesh.shape["pair"], mesh.shape["mo"]),
        mesh=mesh,
        in_specs=(P("pair", "mo", None), P(), P()),
        out_specs=P(None, "pair", "mo"),
        check_vma=False,
    )
```

```python
import functools

import jax
import jax.numpy as jnp
from jax import lax
from jax.experimental import pallas as pl
from jax.experimental.pallas import tpu as pltpu
from jax.sharding import PartitionSpec as P

LANES = 128
STEP = 64
BATCHES = ((4, 4), (4, 4))
CHUNKS = sum(BATCHES, ())
SIZES = ((1,), (1,), (1, 2), (-1, 2))
PART = 256
MIB = 1024 * 1024
COST = pl.CostEstimate(flops=1024, bytes_accessed=1024, transcendentals=0)
IN_VMEM = pl.BlockSpec(memory_space=pltpu.VMEM)
IN_SMEM = pl.BlockSpec(memory_space=pltpu.SMEM)
ANYWHERE = pl.BlockSpec(memory_space=pl.ANY)
IN_HBM = pl.BlockSpec(memory_space=pltpu.MemorySpace.HBM)


def quarter_kernel(batch, n_mo, blocks, n_after, place_ref, x_hbm, c_hbm, *refs):
    outs, (x_ref, c_ref, turn_ref, x_sems, c_sem) = refs[n_after:-5], refs[-5:]
    rows, depth = x_hbm.shape[0], x_hbm.shape[2]
    padded, some, _ = x_ref.shape
    many = PART // some

    columns = []
    for o in range(n_mo):
        mine = pl.ds(pl.multiple_of((place_ref[0] ^ o) * LANES, LANES), LANES)
        columns.append(pltpu.make_async_copy(c_hbm.at[:, mine], c_ref.at[:, o * LANES : (o + 1) * LANES], c_sem.at[o]))
    parts = []
    for n, first in enumerate(range(0, padded, STEP)):
        lines = pl.ds(first, min(STEP, rows - first))
        source = x_hbm.at[lines, pl.ds(batch * some, some)]
        parts.append(pltpu.make_async_copy(source, x_ref.at[lines], x_sems.at[n]))
    for copy in parts[:1] + columns + parts[1:]:
        copy.start()
    x_ref[rows:] = jnp.zeros((padded - rows, some, depth), jnp.bfloat16)
    to = lax.broadcasted_iota(jnp.int32, (PART, PART), 0)
    source = lax.broadcasted_iota(jnp.int32, (PART, PART), 1)
    is_source = source == (to & (many - 1)) * some + (to >> (many.bit_length() - 1))
    turn_ref[...] = jnp.where(is_source, 1.0, 0.0).astype(jnp.bfloat16)
    for copy in columns:
        copy.wait()
    for n, first in enumerate(range(0, padded, STEP)):
        parts[n].wait()
        x = x_ref[first : first + STEP].reshape(STEP * some, depth)
        product = jnp.dot(x, c_ref[...], preferred_element_type=jnp.float32).astype(jnp.bfloat16)
        for part in range(STEP // many):
            lines = jnp.dot(
                turn_ref[...], product[part * PART : (part + 1) * PART], preferred_element_type=jnp.float32
            ).astype(jnp.bfloat16)
            at = first + part * many
            for out, (o, k) in zip(outs, blocks):
                for row in range(out.shape[0]):
                    line = (k + row) * many
                    out[row, at : at + many] = lines[line : line + many, o * LANES : (o + 1) * LANES]


def quarter_of(place, by_r, coeffs, n_mo, padded, batch, after):
    depth, orbitals = coeffs.shape
    chunks = BATCHES[batch]
    some = sum(chunks)
    blocks = [(0, 0), (1, 0)] + [(o, sum(chunks[:c])) for c in range(len(chunks)) for o in range(2, n_mo)]
    sizes = [some] * 2 + [kc for kc in chunks for _ in range(2, n_mo)]
    outs = [jax.ShapeDtypeStruct((kc, padded, LANES), jnp.bfloat16) for kc in sizes]
    out = pl.pallas_call(
        functools.partial(quarter_kernel, batch, n_mo, blocks, len(after)),
        in_specs=[IN_SMEM] + [IN_HBM] * 2 + [ANYWHERE] * len(after),
        out_specs=[IN_VMEM] * len(outs),
        out_shape=outs,
        scratch_shapes=[
            pltpu.VMEM((padded, some, depth), jnp.bfloat16),
            pltpu.VMEM((depth, orbitals), jnp.bfloat16),
            pltpu.VMEM((PART, PART), jnp.bfloat16),
            pltpu.SemaphoreType.DMA((padded // STEP,)),
            pltpu.SemaphoreType.DMA((n_mo,)),
        ],
        compiler_params=pltpu.CompilerParams(vmem_limit_bytes=51 * MIB),
        cost_estimate=COST,
        name="quarter",
    )(place, by_r, coeffs, *after)
    far = n_mo - 2
    return out[:2], [list(out[2 + far * c : 2 + far * (c + 1)]) for c in range(len(chunks))]


def turn_kernel(rows, c_ref, *refs):
    out_ref = refs[-1]
    n_mo, orbitals, padded = out_ref.shape
    none = jnp.zeros((padded - rows, orbitals), jnp.float32)
    for n in range(n_mo):
        part = c_ref[n * rows : (n + 1) * rows, :].astype(jnp.float32)
        out_ref[n] = jnp.concatenate([part, none], axis=0).T.astype(jnp.bfloat16)


def turn(coeffs, n_mo, padded, later, after):
    depth, orbitals = coeffs.shape
    out = pl.pallas_call(
        functools.partial(turn_kernel, depth // n_mo),
        in_specs=[IN_VMEM] + [IN_HBM] * len(later) + [ANYWHERE] * len(after),
        out_specs=[IN_HBM] * len(later) + [IN_VMEM],
        out_shape=[jax.ShapeDtypeStruct(x.shape, x.dtype) for x in later]
        + [jax.ShapeDtypeStruct((n_mo, orbitals, padded), jnp.bfloat16)],
        input_output_aliases={1 + n: n for n in range(len(later))},
        compiler_params=pltpu.CompilerParams(vmem_limit_bytes=24 * MIB),
        cost_estimate=COST,
        name="turn",
    )(coeffs, *later, *after)
    return out[-1], list(out[:-1])


def half_kernel(n_mo, first, owners, place_ref, *refs):
    blocks, t_ref, held = refs[:n_mo], refs[n_mo], refs[-1]
    outs = refs[-1 - len(owners) : -1]
    kc, block, lanes = outs[0].shape[2:]
    firsts = [first if x.shape[0] > kc else 0 for x in blocks]
    columns = [jnp.concatenate([x[at + k] for k in range(kc)], axis=1) for x, at in zip(blocks, firsts)]
    turned = [t_ref[place_ref[0] ^ o] for o in range(n_mo)]
    held[...] = jnp.dot(
        jnp.concatenate(turned, axis=1), jnp.concatenate(columns, axis=0), preferred_element_type=jnp.float32
    )
    for out, its in zip(outs, owners):
        for at, o in enumerate(its):
            start = pl.multiple_of((place_ref[1] ^ o) * block, block)
            for k in range(kc):
                out[0, at, k] = held[pl.ds(start, block), k * lanes : (k + 1) * lanes].astype(jnp.bfloat16)


def half_of(place, blocks, turned, first, owners, after):
    n_mo, orbitals, _ = turned.shape
    kc, _, lanes = blocks[-1].shape
    block = orbitals // sum(len(its) for its in owners)
    return pl.pallas_call(
        functools.partial(half_kernel, n_mo, first, owners),
        in_specs=[IN_SMEM] + [IN_VMEM] * (n_mo + 1) + [ANYWHERE] * len(after),
        out_specs=[IN_VMEM] * len(owners),
        out_shape=[jax.ShapeDtypeStruct((1, len(its), kc, block, lanes), jnp.bfloat16) for its in owners],
        scratch_shapes=[pltpu.VMEM((orbitals, kc * lanes), jnp.float32)],
        compiler_params=pltpu.CompilerParams(vmem_limit_bytes=24 * MIB),
        cost_estimate=COST,
        name="half",
    )(place, *blocks, turned, *after)


def merge_kernel(n_parts, picks, *refs):
    outs = refs[len(refs) - len(picks) :]
    for out, its in zip(outs, picks):
        at = 0
        for x, pick in zip(refs[:n_parts], its):
            for i in range(x.shape[0]):
                for n, o in enumerate(pick):
                    out[at, n] = x[i, o]
                at += 1


def merge(parts, picks, later, after):
    lines, n = sum(x.shape[0] for x in parts), len(parts)
    out = pl.pallas_call(
        functools.partial(merge_kernel, n, picks),
        in_specs=[IN_VMEM] * n + [IN_HBM] * len(later) + [ANYWHERE] * len(after),
        out_specs=[IN_HBM] * len(later) + [IN_VMEM] * len(picks),
        out_shape=[jax.ShapeDtypeStruct(x.shape, x.dtype) for x in later]
        + [jax.ShapeDtypeStruct((lines, len(its[0]), *parts[0].shape[2:]), jnp.bfloat16) for its in picks],
        input_output_aliases={n + m: m for m in range(len(later))},
        compiler_params=pltpu.CompilerParams(vmem_limit_bytes=24 * MIB),
        cost_estimate=COST,
        name="merge",
    )(*parts, *later, *after)
    return list(out[len(later) :]), list(out[: len(later)])


def wait_kernel(*refs):
    refs[-1][...] = jnp.zeros_like(refs[-1])


def wait_for(after):
    return pl.pallas_call(
        wait_kernel,
        in_specs=[ANYWHERE] * len(after),
        out_specs=IN_VMEM,
        out_shape=jax.ShapeDtypeStruct((8, LANES), jnp.float32),
        compiler_params=pltpu.CompilerParams(vmem_limit_bytes=24 * MIB),
        cost_estimate=COST,
        name="wait",
    )(*after)


def combine_kernel(sources, k_all, per_step, mirror_ref, place_ref, *refs):
    pieces, out_ref, held = refs[: len(sources)], refs[-2], refs[-1]
    step = pl.program_id(0)

    @pl.when(step == 0)
    def _():
        for piece, (offsets, first) in zip(pieces, sources):
            for n, offset in enumerate(offsets):
                row = (place_ref[1] ^ offset) * k_all + first
                held[pl.ds(row, piece.shape[2])] = piece[n, 0]

    for n in range(per_step):
        k = step * per_step + n
        out_ref[n] = 0.5 * (held[k].astype(jnp.float32) + held[mirror_ref[k]].astype(jnp.float32))


def combine(pieces, sources, mirror, place, n_pair, after):
    block, lanes = pieces[0].shape[-2:]
    k_all = sum(CHUNKS)
    rows = n_pair * k_all
    per_step = max(1, 32 * 64 // block)
    return pl.pallas_call(
        functools.partial(combine_kernel, sources, k_all, per_step),
        grid_spec=pltpu.PrefetchScalarGridSpec(
            num_scalar_prefetch=2,
            grid=(rows // per_step,),
            in_specs=[IN_VMEM] * len(pieces) + [ANYWHERE] * len(after),
            out_specs=pl.BlockSpec((per_step, block, lanes), lambda k, m, place: (k, 0, 0)),
            scratch_shapes=[pltpu.VMEM((rows, block, lanes), jnp.bfloat16)],
        ),
        out_shape=jax.ShapeDtypeStruct((rows, block, lanes), jnp.float32),
        compiler_params=pltpu.CompilerParams(vmem_limit_bytes=24 * MIB),
        cost_estimate=COST,
        name="combine",
    )(mirror, place, *pieces, *after)


def flipped(x, axis, size, offset, name):
    with jax.named_scope(name):
        return lax.ppermute(x, axis, [(i, i ^ offset) for i in range(size)])


def digits(n_pair, sizes):
    bits = [1 << n for n in reversed(range(n_pair.bit_length() - 1))]
    masks = []
    while bits:
        size = sizes[min(len(masks), len(sizes) - 1)]
        some = bits[:size] if size > 0 else bits[size:]
        masks.append(sum(some))
        bits = [bit for bit in bits if bit not in some]
    return masks


def on_device(n_pair, n_mo, integrals, coeffs, mirror):
    rows = integrals.shape[1]
    padded = -(-rows // STEP) * STEP
    n_near = n_pair // 2
    by_r = jnp.transpose(integrals, (1, 0, 2))
    place = jnp.stack([lax.axis_index("mo"), lax.axis_index("pair")]).astype(jnp.int32)
    last = len(CHUNKS) - 1
    firsts = [sum(CHUNKS[:c]) for c in range(last + 1)]

    near, queue, token = [], [], []
    for batch, chunks in enumerate(BATCHES):
        (own, beside), far = quarter_of(place, by_r, coeffs, n_mo, padded, batch, token)
        beside = flipped(beside, "mo", n_mo, 1, f"beside{batch}")
        near += [(own, beside, sum(chunks[:c])) for c in range(len(chunks))]
        queue += far
        token = [own]

    def arrive(c):
        return [flipped(x, "mo", n_mo, o, f"y{2 * c + o - 2}") for o, x in enumerate(queue[c], 2)]

    arrived = [arrive(0)]
    turned, queue[1] = turn(coeffs, n_mo, padded, queue[1], arrived[0][:1] + token)
    arrived += [arrive(c) for c in range(1, last + 1)]

    steps = [(c, c, 0) for c in range(last + 1)]
    levels = [digits(n_pair, sizes) for sizes in SIZES]
    for c, masks in enumerate(levels):
        steps += [(c + n + n / 10 - 0.95 * (c == last), c, n) for n in range(1, len(masks))]
    parts, owners, offsets, token = [[] for _ in CHUNKS], [[] for _ in CHUNKS], [[] for _ in CHUNKS], []
    waiting = []

    def plan(c, level):
        mask, gone = levels[c][level], sum(levels[c][:level])
        flips = [o for o in range(1, n_pair) if not o & ~mask][::-1]
        left = [o for o in range(n_pair) if not o & gone]
        return [o for o in left if not o & mask], flips, [[o for o in left if o & mask == flip] for flip in flips]

    def send(c, level, messages):
        _, flips, sent = plan(c, level)
        before = [o for group in offsets[c] for o in group]
        for flip, some, message in zip(flips, sent, messages):
            offsets[c].append([o ^ flip for o in before])
            owners[c].append([o ^ flip for o in some])
            parts[c].append(flipped(message, "pair", n_pair, flip, f"z{flip}c{c}"))

    for _, c, level in sorted(steps):
        kept, _, sent = plan(c, level)
        if level == 0:
            blocks = [*near[c][:2], *arrived[c]]
            keep, *messages = half_of(place, blocks, turned, near[c][2], [kept, *sent], token)
            parts[c], owners[c], offsets[c] = [keep], [kept], [[0]]
        else:
            picks = [[[its.index(o) for o in some] for its in owners[c]] for some in sent]
            done = parts[c - 1][-1:] if level == 2 and c else []
            later = waiting if c == last and level == 1 else []
            messages, later = merge(parts[c], picks, later, token + done)
            if later:
                send(last - 1, 1, later)
        token = messages[:1]
        if c == last - 1 and level == 1:
            waiting = messages
        else:
            send(c, level, messages)
    for x in parts[last][-3:]:
        token = [wait_for([x, *token])]
    pieces = [x for chunk in parts for x in chunk]
    sources = [(tuple(group), first) for chunk, first in zip(offsets, firsts) for group in chunk]
    return combine(pieces, sources, mirror, place, n_pair, token)


def solution(mesh):
    return jax.shard_map(
        functools.partial(on_device, mesh.shape["pair"], mesh.shape["mo"]),
        mesh=mesh,
        in_specs=(P("pair", "mo", None), P(), P()),
        out_specs=P(None, "pair", "mo"),
        check_vma=False,
    )
```

```python
import functools

import jax
import jax.numpy as jnp
from jax import lax
from jax.experimental import pallas as pl
from jax.experimental.pallas import tpu as pltpu
from jax.sharding import PartitionSpec as P

LANES = 128
STEP = 64
BATCHES = ((4, 4), (4, 4))
CHUNKS = sum(BATCHES, ())
SIZES = ((1,), (1,), (-1, 2), (-1, 2))
PART = 256
MIB = 1024 * 1024
COST = pl.CostEstimate(flops=1024, bytes_accessed=1024, transcendentals=0)
IN_VMEM = pl.BlockSpec(memory_space=pltpu.VMEM)
IN_SMEM = pl.BlockSpec(memory_space=pltpu.SMEM)
ANYWHERE = pl.BlockSpec(memory_space=pl.ANY)
IN_HBM = pl.BlockSpec(memory_space=pltpu.MemorySpace.HBM)


def quarter_kernel(batch, n_mo, blocks, n_after, place_ref, x_hbm, c_hbm, *refs):
    outs, (x_ref, c_ref, turn_ref, x_sems, c_sem) = refs[n_after:-5], refs[-5:]
    rows, depth = x_hbm.shape[0], x_hbm.shape[2]
    padded, some, _ = x_ref.shape
    many = PART // some

    columns = []
    for o in range(n_mo):
        mine = pl.ds(pl.multiple_of((place_ref[0] ^ o) * LANES, LANES), LANES)
        columns.append(pltpu.make_async_copy(c_hbm.at[:, mine], c_ref.at[:, o * LANES : (o + 1) * LANES], c_sem.at[o]))
    parts = []
    for n, first in enumerate(range(0, padded, STEP)):
        lines = pl.ds(first, min(STEP, rows - first))
        source = x_hbm.at[lines, pl.ds(batch * some, some)]
        parts.append(pltpu.make_async_copy(source, x_ref.at[lines], x_sems.at[n]))
    for copy in parts[:1] + columns + parts[1:]:
        copy.start()
    x_ref[rows:] = jnp.zeros((padded - rows, some, depth), jnp.bfloat16)
    to = lax.broadcasted_iota(jnp.int32, (PART, PART), 0)
    source = lax.broadcasted_iota(jnp.int32, (PART, PART), 1)
    is_source = source == (to & (many - 1)) * some + (to >> (many.bit_length() - 1))
    turn_ref[...] = jnp.where(is_source, 1.0, 0.0).astype(jnp.bfloat16)
    for copy in columns:
        copy.wait()
    for n, first in enumerate(range(0, padded, STEP)):
        parts[n].wait()
        x = x_ref[first : first + STEP].reshape(STEP * some, depth)
        product = jnp.dot(x, c_ref[...], preferred_element_type=jnp.float32).astype(jnp.bfloat16)
        for part in range(STEP // many):
            lines = jnp.dot(
                turn_ref[...], product[part * PART : (part + 1) * PART], preferred_element_type=jnp.float32
            ).astype(jnp.bfloat16)
            at = first + part * many
            for out, (o, k) in zip(outs, blocks):
                for row in range(out.shape[0]):
                    line = (k + row) * many
                    out[row, at : at + many] = lines[line : line + many, o * LANES : (o + 1) * LANES]


def quarter_of(place, by_r, coeffs, n_mo, padded, batch, after):
    depth, orbitals = coeffs.shape
    chunks = BATCHES[batch]
    some = sum(chunks)
    blocks = [(0, 0), (1, 0)] + [(o, sum(chunks[:c])) for c in range(len(chunks)) for o in range(2, n_mo)]
    sizes = [some] * 2 + [kc for kc in chunks for _ in range(2, n_mo)]
    outs = [jax.ShapeDtypeStruct((kc, padded, LANES), jnp.bfloat16) for kc in sizes]
    out = pl.pallas_call(
        functools.partial(quarter_kernel, batch, n_mo, blocks, len(after)),
        in_specs=[IN_SMEM] + [IN_HBM] * 2 + [ANYWHERE] * len(after),
        out_specs=[IN_VMEM] * len(outs),
        out_shape=outs,
        scratch_shapes=[
            pltpu.VMEM((padded, some, depth), jnp.bfloat16),
            pltpu.VMEM((depth, orbitals), jnp.bfloat16),
            pltpu.VMEM((PART, PART), jnp.bfloat16),
            pltpu.SemaphoreType.DMA((padded // STEP,)),
            pltpu.SemaphoreType.DMA((n_mo,)),
        ],
        compiler_params=pltpu.CompilerParams(vmem_limit_bytes=51 * MIB),
        cost_estimate=COST,
        name="quarter",
    )(place, by_r, coeffs, *after)
    far = n_mo - 2
    return out[:2], [list(out[2 + far * c : 2 + far * (c + 1)]) for c in range(len(chunks))]


def turn_kernel(rows, c_ref, *refs):
    out_ref = refs[-1]
    n_mo, orbitals, padded = out_ref.shape
    none = jnp.zeros((padded - rows, orbitals), jnp.float32)
    for n in range(n_mo):
        part = c_ref[n * rows : (n + 1) * rows, :].astype(jnp.float32)
        out_ref[n] = jnp.concatenate([part, none], axis=0).T.astype(jnp.bfloat16)


def turn(coeffs, n_mo, padded, later, after):
    depth, orbitals = coeffs.shape
    out = pl.pallas_call(
        functools.partial(turn_kernel, depth // n_mo),
        in_specs=[IN_VMEM] + [IN_HBM] * len(later) + [ANYWHERE] * len(after),
        out_specs=[IN_HBM] * len(later) + [IN_VMEM],
        out_shape=[jax.ShapeDtypeStruct(x.shape, x.dtype) for x in later]
        + [jax.ShapeDtypeStruct((n_mo, orbitals, padded), jnp.bfloat16)],
        input_output_aliases={1 + n: n for n in range(len(later))},
        compiler_params=pltpu.CompilerParams(vmem_limit_bytes=24 * MIB),
        cost_estimate=COST,
        name="turn",
    )(coeffs, *later, *after)
    return out[-1], list(out[:-1])


def half_kernel(n_mo, first, owners, place_ref, *refs):
    blocks, t_ref, held = refs[:n_mo], refs[n_mo], refs[-1]
    outs = refs[-1 - len(owners) : -1]
    kc, block, lanes = outs[0].shape[2:]
    firsts = [first if x.shape[0] > kc else 0 for x in blocks]
    columns = [jnp.concatenate([x[at + k] for k in range(kc)], axis=1) for x, at in zip(blocks, firsts)]
    turned = [t_ref[place_ref[0] ^ o] for o in range(n_mo)]
    held[...] = jnp.dot(
        jnp.concatenate(turned, axis=1), jnp.concatenate(columns, axis=0), preferred_element_type=jnp.float32
    )
    for out, its in zip(outs, owners):
        for at, o in enumerate(its):
            start = pl.multiple_of((place_ref[1] ^ o) * block, block)
            for k in range(kc):
                out[0, at, k] = held[pl.ds(start, block), k * lanes : (k + 1) * lanes].astype(jnp.bfloat16)


def half_of(place, blocks, turned, first, owners, after):
    n_mo, orbitals, _ = turned.shape
    kc, _, lanes = blocks[-1].shape
    block = orbitals // sum(len(its) for its in owners)
    return pl.pallas_call(
        functools.partial(half_kernel, n_mo, first, owners),
        in_specs=[IN_SMEM] + [IN_VMEM] * (n_mo + 1) + [ANYWHERE] * len(after),
        out_specs=[IN_VMEM] * len(owners),
        out_shape=[jax.ShapeDtypeStruct((1, len(its), kc, block, lanes), jnp.bfloat16) for its in owners],
        scratch_shapes=[pltpu.VMEM((orbitals, kc * lanes), jnp.float32)],
        compiler_params=pltpu.CompilerParams(vmem_limit_bytes=24 * MIB),
        cost_estimate=COST,
        name="half",
    )(place, *blocks, turned, *after)


def merge_kernel(n_parts, picks, *refs):
    outs = refs[len(refs) - len(picks) :]
    for out, its in zip(outs, picks):
        at = 0
        for x, pick in zip(refs[:n_parts], its):
            for i in range(x.shape[0]):
                for n, o in enumerate(pick):
                    out[at, n] = x[i, o]
                at += 1


def merge(parts, picks, after):
    lines = sum(x.shape[0] for x in parts)
    out = pl.pallas_call(
        functools.partial(merge_kernel, len(parts), picks),
        in_specs=[IN_VMEM] * len(parts) + [ANYWHERE] * len(after),
        out_specs=[IN_VMEM] * len(picks),
        out_shape=[
            jax.ShapeDtypeStruct((lines, len(its[0]), *parts[0].shape[2:]), jnp.bfloat16) for its in picks
        ],
        compiler_params=pltpu.CompilerParams(vmem_limit_bytes=24 * MIB),
        cost_estimate=COST,
        name="merge",
    )(*parts, *after)
    return list(out)


def wait_kernel(*refs):
    refs[-1][...] = jnp.zeros_like(refs[-1])


def wait_for(after):
    return pl.pallas_call(
        wait_kernel,
        in_specs=[ANYWHERE] * len(after),
        out_specs=IN_VMEM,
        out_shape=jax.ShapeDtypeStruct((8, LANES), jnp.float32),
        compiler_params=pltpu.CompilerParams(vmem_limit_bytes=24 * MIB),
        cost_estimate=COST,
        name="wait",
    )(*after)


def combine_kernel(sources, k_all, per_step, mirror_ref, place_ref, *refs):
    pieces, out_ref, held = refs[: len(sources)], refs[-2], refs[-1]
    step = pl.program_id(0)

    @pl.when(step == 0)
    def _():
        for piece, (offsets, first) in zip(pieces, sources):
            for n, offset in enumerate(offsets):
                row = (place_ref[1] ^ offset) * k_all + first
                held[pl.ds(row, piece.shape[2])] = piece[n, 0]

    for n in range(per_step):
        k = step * per_step + n
        out_ref[n] = 0.5 * (held[k].astype(jnp.float32) + held[mirror_ref[k]].astype(jnp.float32))


def combine(pieces, sources, mirror, place, n_pair, after):
    block, lanes = pieces[0].shape[-2:]
    k_all = sum(CHUNKS)
    rows = n_pair * k_all
    per_step = max(1, 32 * 64 // block)
    return pl.pallas_call(
        functools.partial(combine_kernel, sources, k_all, per_step),
        grid_spec=pltpu.PrefetchScalarGridSpec(
            num_scalar_prefetch=2,
            grid=(rows // per_step,),
            in_specs=[IN_VMEM] * len(pieces) + [ANYWHERE] * len(after),
            out_specs=pl.BlockSpec((per_step, block, lanes), lambda k, m, place: (k, 0, 0)),
            scratch_shapes=[pltpu.VMEM((rows, block, lanes), jnp.bfloat16)],
        ),
        out_shape=jax.ShapeDtypeStruct((rows, block, lanes), jnp.float32),
        compiler_params=pltpu.CompilerParams(vmem_limit_bytes=24 * MIB),
        cost_estimate=COST,
        name="combine",
    )(mirror, place, *pieces, *after)


def flipped(x, axis, size, offset, name):
    with jax.named_scope(name):
        return lax.ppermute(x, axis, [(i, i ^ offset) for i in range(size)])


def digits(n_pair, sizes):
    bits = [1 << n for n in reversed(range(n_pair.bit_length() - 1))]
    masks = []
    while bits:
        size = sizes[min(len(masks), len(sizes) - 1)]
        some = bits[:size] if size > 0 else bits[size:]
        masks.append(sum(some))
        bits = [bit for bit in bits if bit not in some]
    return masks


def on_device(n_pair, n_mo, integrals, coeffs, mirror):
    rows = integrals.shape[1]
    padded = -(-rows // STEP) * STEP
    n_near = n_pair // 2
    by_r = jnp.transpose(integrals, (1, 0, 2))
    place = jnp.stack([lax.axis_index("mo"), lax.axis_index("pair")]).astype(jnp.int32)
    last = len(CHUNKS) - 1
    firsts = [sum(CHUNKS[:c]) for c in range(last + 1)]

    near, queue, token = [], [], []
    for batch, chunks in enumerate(BATCHES):
        (own, beside), far = quarter_of(place, by_r, coeffs, n_mo, padded, batch, token)
        beside = flipped(beside, "mo", n_mo, 1, f"beside{batch}")
        near += [(own, beside, sum(chunks[:c])) for c in range(len(chunks))]
        queue += far
        token = [own]

    def arrive(c):
        return [flipped(x, "mo", n_mo, o, f"y{2 * c + o - 2}") for o, x in enumerate(queue[c], 2)]

    arrived = [arrive(0)]
    turned, queue[1] = turn(coeffs, n_mo, padded, queue[1], arrived[0][:1] + token)
    arrived += [arrive(c) for c in range(1, last + 1)]

    levels = [digits(n_pair, sizes) for sizes in SIZES]
    steps = [(c, c, 0) for c in range(last + 1)]
    for c, masks in enumerate(levels):
        steps += [(c + (n + n / 10 if SIZES[c][0] > 0 else n * 3 / 10), c, n) for n in range(1, len(masks))]
    parts, owners, offsets, token = [[] for _ in CHUNKS], [[] for _ in CHUNKS], [[] for _ in CHUNKS], []

    def plan(c, level):
        mask, gone = levels[c][level], sum(levels[c][:level])
        flips = [o for o in range(1, n_pair) if not o & ~mask][::-1]
        left = [o for o in range(n_pair) if not o & gone]
        return [o for o in left if not o & mask], flips, [[o for o in left if o & mask == flip] for flip in flips]

    def send(c, level, messages):
        _, flips, sent = plan(c, level)
        before = [o for group in offsets[c] for o in group]
        for flip, some, message in zip(flips, sent, messages):
            offsets[c].append([o ^ flip for o in before])
            owners[c].append([o ^ flip for o in some])
            parts[c].append(flipped(message, "pair", n_pair, flip, f"z{flip}c{c}"))

    for _, c, level in sorted(steps):
        kept, _, sent = plan(c, level)
        if level == 0:
            blocks = [*near[c][:2], *arrived[c]]
            keep, *messages = half_of(place, blocks, turned, near[c][2], [kept, *sent], token)
            parts[c], owners[c], offsets[c] = [keep], [kept], [[0]]
        else:
            picks = [[[its.index(o) for o in some] for its in owners[c]] for some in sent]
            done = {(0, 2): arrived[last][:1], (last - 1, 1): arrived[last][1:], (last, 1): parts[0][-1:]}
            done = list(done.get((c, level), []))
            messages = merge(parts[c], picks, token + done)
        token = messages[:1]
        send(c, level, messages)
    for x in parts[last - 1][-3:] + parts[last][-3:]:
        token = [wait_for([x, *token])]
    pieces = [x for chunk in parts for x in chunk]
    sources = [(tuple(group), first) for chunk, first in zip(offsets, firsts) for group in chunk]
    return combine(pieces, sources, mirror, place, n_pair, token)


def solution(mesh):
    return jax.shard_map(
        functools.partial(on_device, mesh.shape["pair"], mesh.shape["mo"]),
        mesh=mesh,
        in_specs=(P("pair", "mo", None), P(), P()),
        out_specs=P(None, "pair", "mo"),
        check_vma=False,
    )
```

```python
import functools

import jax
import jax.numpy as jnp
from jax import lax
from jax.experimental import pallas as pl
from jax.experimental.pallas import tpu as pltpu
from jax.sharding import PartitionSpec as P

LANES = 128
STEP = 64
BATCHES = ((4, 4), (4, 4))
CHUNKS = sum(BATCHES, ())
SIZES = ((1,), (1,), (-1, 2), (-1, 2))
PART = 256
MIB = 1024 * 1024
COST = pl.CostEstimate(flops=1024, bytes_accessed=1024, transcendentals=0)
IN_VMEM = pl.BlockSpec(memory_space=pltpu.VMEM)
IN_SMEM = pl.BlockSpec(memory_space=pltpu.SMEM)
ANYWHERE = pl.BlockSpec(memory_space=pl.ANY)
IN_HBM = pl.BlockSpec(memory_space=pltpu.MemorySpace.HBM)


def quarter_kernel(batch, n_mo, blocks, n_after, place_ref, x_hbm, c_hbm, *refs):
    outs, (x_ref, c_ref, turn_ref, x_sems, c_sem) = refs[n_after:-5], refs[-5:]
    rows, depth = x_hbm.shape[0], x_hbm.shape[2]
    padded, some, _ = x_ref.shape
    many = PART // some

    columns = []
    for o in range(n_mo):
        mine = pl.ds(pl.multiple_of((place_ref[0] ^ o) * LANES, LANES), LANES)
        columns.append(pltpu.make_async_copy(c_hbm.at[:, mine], c_ref.at[:, o * LANES : (o + 1) * LANES], c_sem.at[o]))
    parts = []
    for n, first in enumerate(range(0, padded, STEP)):
        lines = pl.ds(first, min(STEP, rows - first))
        source = x_hbm.at[lines, pl.ds(batch * some, some)]
        parts.append(pltpu.make_async_copy(source, x_ref.at[lines], x_sems.at[n]))
    for copy in parts[:1] + columns + parts[1:]:
        copy.start()
    x_ref[rows:] = jnp.zeros((padded - rows, some, depth), jnp.bfloat16)
    to = lax.broadcasted_iota(jnp.int32, (PART, PART), 0)
    source = lax.broadcasted_iota(jnp.int32, (PART, PART), 1)
    is_source = source == (to & (many - 1)) * some + (to >> (many.bit_length() - 1))
    turn_ref[...] = jnp.where(is_source, 1.0, 0.0).astype(jnp.bfloat16)
    for copy in columns:
        copy.wait()
    for n, first in enumerate(range(0, padded, STEP)):
        parts[n].wait()
        x = x_ref[first : first + STEP].reshape(STEP * some, depth)
        product = jnp.dot(x, c_ref[...], preferred_element_type=jnp.float32).astype(jnp.bfloat16)
        for part in range(STEP // many):
            lines = jnp.dot(
                turn_ref[...], product[part * PART : (part + 1) * PART], preferred_element_type=jnp.float32
            ).astype(jnp.bfloat16)
            at = first + part * many
            for out, (o, k) in zip(outs, blocks):
                for row in range(out.shape[0]):
                    line = (k + row) * many
                    out[row, at : at + many] = lines[line : line + many, o * LANES : (o + 1) * LANES]


def quarter_of(place, by_r, coeffs, n_mo, padded, batch, after):
    depth, orbitals = coeffs.shape
    chunks = BATCHES[batch]
    some = sum(chunks)
    blocks = [(0, 0), (1, 0)] + [(o, sum(chunks[:c])) for c in range(len(chunks)) for o in range(2, n_mo)]
    sizes = [some] * 2 + [kc for kc in chunks for _ in range(2, n_mo)]
    outs = [jax.ShapeDtypeStruct((kc, padded, LANES), jnp.bfloat16) for kc in sizes]
    out = pl.pallas_call(
        functools.partial(quarter_kernel, batch, n_mo, blocks, len(after)),
        in_specs=[IN_SMEM] + [IN_HBM] * 2 + [ANYWHERE] * len(after),
        out_specs=[IN_VMEM] * len(outs),
        out_shape=outs,
        scratch_shapes=[
            pltpu.VMEM((padded, some, depth), jnp.bfloat16),
            pltpu.VMEM((depth, orbitals), jnp.bfloat16),
            pltpu.VMEM((PART, PART), jnp.bfloat16),
            pltpu.SemaphoreType.DMA((padded // STEP,)),
            pltpu.SemaphoreType.DMA((n_mo,)),
        ],
        compiler_params=pltpu.CompilerParams(vmem_limit_bytes=51 * MIB),
        cost_estimate=COST,
        name="quarter",
    )(place, by_r, coeffs, *after)
    far = n_mo - 2
    return out[:2], [list(out[2 + far * c : 2 + far * (c + 1)]) for c in range(len(chunks))]


def turn_kernel(rows, n_mo, n_pair, place_ref, c_ref, *refs):
    out_ref = refs[-1]
    orbitals, padded = out_ref.shape[0], out_ref.shape[1] // n_mo
    block = orbitals // n_pair
    none = jnp.zeros((padded - rows, orbitals), jnp.float32)
    for n in range(n_mo):
        part = c_ref[n * rows : (n + 1) * rows, :].astype(jnp.float32)
        part = jnp.concatenate([part, none], axis=0).T
        columns = pl.ds(pl.multiple_of((place_ref[0] ^ n) * padded, padded), padded)
        for o in range(n_pair):
            lines = pl.ds(pl.multiple_of((place_ref[1] ^ o) * block, block), block)
            out_ref[lines, columns] = part[o * block : (o + 1) * block].astype(jnp.bfloat16)


def turn(place, coeffs, n_mo, n_pair, padded, later, after):
    depth, orbitals = coeffs.shape
    out = pl.pallas_call(
        functools.partial(turn_kernel, depth // n_mo, n_mo, n_pair),
        in_specs=[IN_SMEM, IN_VMEM] + [IN_HBM] * len(later) + [ANYWHERE] * len(after),
        out_specs=[IN_HBM] * len(later) + [IN_VMEM],
        out_shape=[jax.ShapeDtypeStruct(x.shape, x.dtype) for x in later]
        + [jax.ShapeDtypeStruct((orbitals, n_mo * padded), jnp.bfloat16)],
        input_output_aliases={2 + n: n for n in range(len(later))},
        compiler_params=pltpu.CompilerParams(vmem_limit_bytes=24 * MIB),
        cost_estimate=COST,
        name="turn",
    )(place, coeffs, *later, *after)
    return out[-1], list(out[:-1])


def half_kernel(first, owners, *refs):
    n_mo = len(refs) - len(owners) - 1
    blocks, t_ref, outs = refs[:n_mo], refs[n_mo], refs[n_mo + 1 :]
    kc, block, lanes = outs[0].shape[2:]
    firsts = [first if x.shape[0] > kc else 0 for x in blocks]
    columns = [jnp.concatenate([x[at + k] for k in range(kc)], axis=1) for x, at in zip(blocks, firsts)]
    half = jnp.dot(t_ref[...], jnp.concatenate(columns, axis=0), preferred_element_type=jnp.float32)
    for out, its in zip(outs, owners):
        for at, o in enumerate(its):
            for k in range(kc):
                piece = half[o * block : (o + 1) * block, k * lanes : (k + 1) * lanes]
                out[0, at, k] = piece.astype(jnp.bfloat16)


def half_kernel_after(n_blocks, n_after, first, owners, *refs):
    half_kernel(first, owners, *refs[: n_blocks + 1], *refs[n_blocks + 1 + n_after :])


def half_of(blocks, turned, first, owners, after):
    kc, _, lanes = blocks[-1].shape
    block = turned.shape[0] // sum(len(its) for its in owners)
    return pl.pallas_call(
        functools.partial(half_kernel_after, len(blocks), len(after), first, owners),
        in_specs=[IN_VMEM] * (len(blocks) + 1) + [ANYWHERE] * len(after),
        out_specs=[IN_VMEM] * len(owners),
        out_shape=[jax.ShapeDtypeStruct((1, len(its), kc, block, lanes), jnp.bfloat16) for its in owners],
        compiler_params=pltpu.CompilerParams(vmem_limit_bytes=24 * MIB),
        cost_estimate=COST,
        name="half",
    )(*blocks, turned, *after)


def merge_kernel(n_parts, picks, *refs):
    outs = refs[len(refs) - len(picks) :]
    for out, its in zip(outs, picks):
        at = 0
        for x, pick in zip(refs[:n_parts], its):
            for i in range(x.shape[0]):
                for n, o in enumerate(pick):
                    out[at, n] = x[i, o]
                at += 1


def merge(parts, picks, after):
    lines = sum(x.shape[0] for x in parts)
    out = pl.pallas_call(
        functools.partial(merge_kernel, len(parts), picks),
        in_specs=[IN_VMEM] * len(parts) + [ANYWHERE] * len(after),
        out_specs=[IN_VMEM] * len(picks),
        out_shape=[
            jax.ShapeDtypeStruct((lines, len(its[0]), *parts[0].shape[2:]), jnp.bfloat16) for its in picks
        ],
        compiler_params=pltpu.CompilerParams(vmem_limit_bytes=24 * MIB),
        cost_estimate=COST,
        name="merge",
    )(*parts, *after)
    return list(out)


def wait_kernel(*refs):
    refs[-1][...] = jnp.zeros_like(refs[-1])


def wait_for(after):
    return pl.pallas_call(
        wait_kernel,
        in_specs=[ANYWHERE] * len(after),
        out_specs=IN_VMEM,
        out_shape=jax.ShapeDtypeStruct((8, LANES), jnp.float32),
        compiler_params=pltpu.CompilerParams(vmem_limit_bytes=24 * MIB),
        cost_estimate=COST,
        name="wait",
    )(*after)


def combine_kernel(sources, k_all, per_step, mirror_ref, place_ref, *refs):
    pieces, (out_hbm, held, done, sems) = refs[: len(sources)], refs[-4:]
    for piece, (offsets, first) in zip(pieces, sources):
        for n, offset in enumerate(offsets):
            row = (place_ref[1] ^ offset) * k_all + first
            held[pl.ds(row, piece.shape[2])] = piece[n, 0]

    def copy_of(step):
        rows = pl.ds(step * per_step, per_step)
        return pltpu.make_async_copy(done.at[rows], out_hbm.at[rows], sems.at[step])

    @pl.loop(0, held.shape[0] // per_step)
    def _(step):
        for n in range(per_step):
            k = step * per_step + n
            done[k] = 0.5 * (held[k].astype(jnp.float32) + held[mirror_ref[k]].astype(jnp.float32))
        copy_of(step).start()

    @pl.loop(0, held.shape[0] // per_step)
    def _(step):
        copy_of(step).wait()


def combine(pieces, sources, mirror, place, n_pair, after):
    block, lanes = pieces[0].shape[-2:]
    k_all = sum(CHUNKS)
    rows = n_pair * k_all
    per_step = max(1, 16 * 64 // block)
    return pl.pallas_call(
        functools.partial(combine_kernel, sources, k_all, per_step),
        in_specs=[IN_SMEM] * 2 + [IN_VMEM] * len(pieces) + [ANYWHERE] * len(after),
        out_specs=IN_HBM,
        out_shape=jax.ShapeDtypeStruct((rows, block, lanes), jnp.float32),
        scratch_shapes=[
            pltpu.VMEM((rows, block, lanes), jnp.bfloat16),
            pltpu.VMEM((rows, block, lanes), jnp.float32),
            pltpu.SemaphoreType.DMA((rows // per_step,)),
        ],
        compiler_params=pltpu.CompilerParams(vmem_limit_bytes=24 * MIB),
        cost_estimate=COST,
        name="combine",
    )(mirror, place, *pieces, *after)


def flipped(x, axis, size, offset, name):
    with jax.named_scope(name):
        return lax.ppermute(x, axis, [(i, i ^ offset) for i in range(size)])


def digits(n_pair, sizes):
    bits = [1 << n for n in reversed(range(n_pair.bit_length() - 1))]
    masks = []
    while bits:
        size = sizes[min(len(masks), len(sizes) - 1)]
        some = bits[:size] if size > 0 else bits[size:]
        masks.append(sum(some))
        bits = [bit for bit in bits if bit not in some]
    return masks


def on_device(n_pair, n_mo, integrals, coeffs, mirror):
    rows = integrals.shape[1]
    padded = -(-rows // STEP) * STEP
    n_near = n_pair // 2
    by_r = jnp.transpose(integrals, (1, 0, 2))
    place = jnp.stack([lax.axis_index("mo"), lax.axis_index("pair")]).astype(jnp.int32)
    last = len(CHUNKS) - 1
    firsts = [sum(CHUNKS[:c]) for c in range(last + 1)]

    near, queue, token = [], [], []
    for batch, chunks in enumerate(BATCHES):
        (own, beside), far = quarter_of(place, by_r, coeffs, n_mo, padded, batch, token)
        beside = flipped(beside, "mo", n_mo, 1, f"beside{batch}")
        near += [(own, beside, sum(chunks[:c])) for c in range(len(chunks))]
        queue += far
        token = [own]

    def arrive(c):
        return [flipped(x, "mo", n_mo, o, f"y{2 * c + o - 2}") for o, x in enumerate(queue[c], 2)]

    arrived = [arrive(0)]
    turned, queue[1] = turn(place, coeffs, n_mo, n_pair, padded, queue[1], arrived[0][:1] + token)
    arrived += [arrive(c) for c in range(1, last + 1)]

    levels = [digits(n_pair, sizes) for sizes in SIZES]
    steps = [(c, c, 0) for c in range(last + 1)]
    for c, masks in enumerate(levels):
        steps += [(c + (n + n / 10 if SIZES[c][0] > 0 else n * 3 / 10), c, n) for n in range(1, len(masks))]
    parts, owners, offsets, token = [[] for _ in CHUNKS], [[] for _ in CHUNKS], [[] for _ in CHUNKS], []

    def plan(c, level):
        mask, gone = levels[c][level], sum(levels[c][:level])
        flips = [o for o in range(1, n_pair) if not o & ~mask][::-1]
        left = [o for o in range(n_pair) if not o & gone]
        return [o for o in left if not o & mask], flips, [[o for o in left if o & mask == flip] for flip in flips]

    def send(c, level, messages):
        _, flips, sent = plan(c, level)
        before = [o for group in offsets[c] for o in group]
        for flip, some, message in zip(flips, sent, messages):
            offsets[c].append([o ^ flip for o in before])
            owners[c].append([o ^ flip for o in some])
            parts[c].append(flipped(message, "pair", n_pair, flip, f"z{flip}c{c}"))

    for _, c, level in sorted(steps):
        kept, _, sent = plan(c, level)
        if level == 0:
            blocks = [*near[c][:2], *arrived[c]]
            keep, *messages = half_of(blocks, turned, near[c][2], [kept, *sent], token)
            parts[c], owners[c], offsets[c] = [keep], [kept], [[0]]
        else:
            picks = [[[its.index(o) for o in some] for its in owners[c]] for some in sent]
            done = {(0, 2): arrived[last][:1], (last - 1, 1): arrived[last][1:], (last, 1): parts[0][-1:]}
            done = list(done.get((c, level), []))
            messages = merge(parts[c], picks, token + done)
        token = messages[:1]
        send(c, level, messages)
    for x in parts[last - 1][-3:] + parts[last][-3:]:
        token = [wait_for([x, *token])]
    pieces = [x for chunk in parts for x in chunk]
    sources = [(tuple(group), first) for chunk, first in zip(offsets, firsts) for group in chunk]
    return combine(pieces, sources, mirror, place, n_pair, token)


def solution(mesh):
    return jax.shard_map(
        functools.partial(on_device, mesh.shape["pair"], mesh.shape["mo"]),
        mesh=mesh,
        in_specs=(P("pair", "mo", None), P(), P()),
        out_specs=P(None, "pair", "mo"),
        check_vma=False,
    )
```

```python
import functools

import jax
import jax.numpy as jnp
from jax import lax
from jax.experimental import pallas as pl
from jax.experimental.pallas import tpu as pltpu
from jax.sharding import PartitionSpec as P

LANES = 128
STEP = 64
LATER = {0: (2, [2, 3]), 1: (3, [2]), 2: (3, [3])}
BATCHES = ((4, 4), (5, 3))
CHUNKS = sum(BATCHES, ())
SIZES = ((1,), (1,), (-1, 2), (-1, 2))
PART = 256
MIB = 1024 * 1024
COST = pl.CostEstimate(flops=1024, bytes_accessed=1024, transcendentals=0)
IN_VMEM = pl.BlockSpec(memory_space=pltpu.VMEM)
IN_SMEM = pl.BlockSpec(memory_space=pltpu.SMEM)
ANYWHERE = pl.BlockSpec(memory_space=pl.ANY)
IN_HBM = pl.BlockSpec(memory_space=pltpu.MemorySpace.HBM)


def quarter_kernel(batch, n_mo, blocks, n_after, place_ref, x_hbm, c_hbm, *refs):
    outs, (x_ref, c_ref, turn_ref, x_sems, c_sem) = refs[n_after:-5], refs[-5:]
    rows, depth = x_hbm.shape[0], x_hbm.shape[2]
    padded, some, _ = x_ref.shape
    many = PART // some

    columns = []
    for o in range(n_mo):
        mine = pl.ds(pl.multiple_of((place_ref[0] ^ o) * LANES, LANES), LANES)
        columns.append(pltpu.make_async_copy(c_hbm.at[:, mine], c_ref.at[:, o * LANES : (o + 1) * LANES], c_sem.at[o]))
    parts = []
    for n, first in enumerate(range(0, padded, STEP)):
        lines = pl.ds(first, min(STEP, rows - first))
        source = x_hbm.at[lines, pl.ds(batch * some, some)]
        parts.append(pltpu.make_async_copy(source, x_ref.at[lines], x_sems.at[n]))
    for copy in parts[:1] + columns + parts[1:]:
        copy.start()
    x_ref[rows:] = jnp.zeros((padded - rows, some, depth), jnp.bfloat16)
    to = lax.broadcasted_iota(jnp.int32, (PART, PART), 0)
    source = lax.broadcasted_iota(jnp.int32, (PART, PART), 1)
    is_source = source == (to & (many - 1)) * some + (to >> (many.bit_length() - 1))
    turn_ref[...] = jnp.where(is_source, 1.0, 0.0).astype(jnp.bfloat16)
    for copy in columns:
        copy.wait()
    for n, first in enumerate(range(0, padded, STEP)):
        parts[n].wait()
        x = x_ref[first : first + STEP].reshape(STEP * some, depth)
        product = jnp.dot(x, c_ref[...], preferred_element_type=jnp.float32).astype(jnp.bfloat16)
        for part in range(STEP // many):
            lines = jnp.dot(
                turn_ref[...], product[part * PART : (part + 1) * PART], preferred_element_type=jnp.float32
            ).astype(jnp.bfloat16)
            at = first + part * many
            for out, (o, k) in zip(outs, blocks):
                for row in range(out.shape[0]):
                    line = (k + row) * many
                    out[row, at : at + many] = lines[line : line + many, o * LANES : (o + 1) * LANES]


def quarter_of(place, by_r, coeffs, n_mo, padded, batch, after):
    depth, orbitals = coeffs.shape
    chunks = BATCHES[batch]
    some = sum(chunks)
    blocks = [(0, 0), (1, 0)] + [(o, sum(chunks[:c])) for c in range(len(chunks)) for o in range(2, n_mo)]
    sizes = [some] * 2 + [kc for kc in chunks for _ in range(2, n_mo)]
    outs = [jax.ShapeDtypeStruct((kc, padded, LANES), jnp.bfloat16) for kc in sizes]
    out = pl.pallas_call(
        functools.partial(quarter_kernel, batch, n_mo, blocks, len(after)),
        in_specs=[IN_SMEM] + [IN_HBM] * 2 + [ANYWHERE] * len(after),
        out_specs=[IN_VMEM] * len(outs),
        out_shape=outs,
        scratch_shapes=[
            pltpu.VMEM((padded, some, depth), jnp.bfloat16),
            pltpu.VMEM((depth, orbitals), jnp.bfloat16),
            pltpu.VMEM((PART, PART), jnp.bfloat16),
            pltpu.SemaphoreType.DMA((padded // STEP,)),
            pltpu.SemaphoreType.DMA((n_mo,)),
        ],
        compiler_params=pltpu.CompilerParams(vmem_limit_bytes=51 * MIB),
        cost_estimate=COST,
        name="quarter",
    )(place, by_r, coeffs, *after)
    far = n_mo - 2
    return out[:2], [list(out[2 + far * c : 2 + far * (c + 1)]) for c in range(len(chunks))]


def turn_kernel(rows, n_mo, n_pair, place_ref, c_ref, *refs):
    out_ref = refs[-1]
    orbitals, padded = out_ref.shape[0], out_ref.shape[1] // n_mo
    block = orbitals // n_pair
    none = jnp.zeros((padded - rows, orbitals), jnp.float32)
    for n in range(n_mo):
        part = c_ref[n * rows : (n + 1) * rows, :].astype(jnp.float32)
        part = jnp.concatenate([part, none], axis=0).T
        columns = pl.ds(pl.multiple_of((place_ref[0] ^ n) * padded, padded), padded)
        for o in range(n_pair):
            lines = pl.ds(pl.multiple_of((place_ref[1] ^ o) * block, block), block)
            out_ref[lines, columns] = part[o * block : (o + 1) * block].astype(jnp.bfloat16)


def turn(place, coeffs, n_mo, n_pair, padded, later, after):
    depth, orbitals = coeffs.shape
    out = pl.pallas_call(
        functools.partial(turn_kernel, depth // n_mo, n_mo, n_pair),
        in_specs=[IN_SMEM, IN_VMEM] + [IN_HBM] * len(later) + [ANYWHERE] * len(after),
        out_specs=[IN_HBM] * len(later) + [IN_VMEM],
        out_shape=[jax.ShapeDtypeStruct(x.shape, x.dtype) for x in later]
        + [jax.ShapeDtypeStruct((orbitals, n_mo * padded), jnp.bfloat16)],
        input_output_aliases={2 + n: n for n in range(len(later))},
        compiler_params=pltpu.CompilerParams(vmem_limit_bytes=24 * MIB),
        cost_estimate=COST,
        name="turn",
    )(place, coeffs, *later, *after)
    return out[-1], list(out[:-1])


def half_kernel(first, owners, *refs):
    n_mo = len(refs) - len(owners) - 1
    blocks, t_ref, outs = refs[:n_mo], refs[n_mo], refs[n_mo + 1 :]
    kc, block, lanes = outs[0].shape[2:]
    firsts = [first if x.shape[0] > kc else 0 for x in blocks]
    columns = [jnp.concatenate([x[at + k] for k in range(kc)], axis=1) for x, at in zip(blocks, firsts)]
    half = jnp.dot(t_ref[...], jnp.concatenate(columns, axis=0), preferred_element_type=jnp.float32)
    for out, its in zip(outs, owners):
        for at, o in enumerate(its):
            for k in range(kc):
                piece = half[o * block : (o + 1) * block, k * lanes : (k + 1) * lanes]
                out[0, at, k] = piece.astype(jnp.bfloat16)


def half_kernel_after(n_blocks, n_outs, first, owners, *refs):
    half_kernel(first, owners, *refs[: n_blocks + 1], *refs[len(refs) - n_outs :])


def half_of(blocks, turned, first, owners, later, after):
    kc, _, lanes = blocks[-1].shape
    block = turned.shape[0] // sum(len(its) for its in owners)
    n = len(blocks) + 1
    out = pl.pallas_call(
        functools.partial(half_kernel_after, len(blocks), len(owners), first, owners),
        in_specs=[IN_VMEM] * n + [IN_HBM] * len(later) + [ANYWHERE] * len(after),
        out_specs=[IN_HBM] * len(later) + [IN_VMEM] * len(owners),
        out_shape=[jax.ShapeDtypeStruct(x.shape, x.dtype) for x in later]
        + [jax.ShapeDtypeStruct((1, len(its), kc, block, lanes), jnp.bfloat16) for its in owners],
        input_output_aliases={n + m: m for m in range(len(later))},
        compiler_params=pltpu.CompilerParams(vmem_limit_bytes=24 * MIB),
        cost_estimate=COST,
        name="half",
    )(*blocks, turned, *later, *after)
    return list(out[len(later) :]), list(out[: len(later)])


def merge_kernel(n_parts, picks, *refs):
    outs = refs[len(refs) - len(picks) :]
    for out, its in zip(outs, picks):
        at = 0
        for x, pick in zip(refs[:n_parts], its):
            for i in range(x.shape[0]):
                for n, o in enumerate(pick):
                    out[at, n] = x[i, o]
                at += 1


def merge(parts, picks, after):
    lines = sum(x.shape[0] for x in parts)
    out = pl.pallas_call(
        functools.partial(merge_kernel, len(parts), picks),
        in_specs=[IN_VMEM] * len(parts) + [ANYWHERE] * len(after),
        out_specs=[IN_VMEM] * len(picks),
        out_shape=[
            jax.ShapeDtypeStruct((lines, len(its[0]), *parts[0].shape[2:]), jnp.bfloat16) for its in picks
        ],
        compiler_params=pltpu.CompilerParams(vmem_limit_bytes=24 * MIB),
        cost_estimate=COST,
        name="merge",
    )(*parts, *after)
    return list(out)


def wait_kernel(*refs):
    refs[-1][...] = jnp.zeros_like(refs[-1])


def wait_for(after):
    return pl.pallas_call(
        wait_kernel,
        in_specs=[ANYWHERE] * len(after),
        out_specs=IN_VMEM,
        out_shape=jax.ShapeDtypeStruct((8, LANES), jnp.float32),
        compiler_params=pltpu.CompilerParams(vmem_limit_bytes=24 * MIB),
        cost_estimate=COST,
        name="wait",
    )(*after)


def combine_kernel(sources, k_all, per_step, mirror_ref, place_ref, *refs):
    pieces, (out_hbm, held, done, sems) = refs[: len(sources)], refs[-4:]
    for piece, (offsets, first) in zip(pieces, sources):
        for n, offset in enumerate(offsets):
            row = (place_ref[1] ^ offset) * k_all + first
            held[pl.ds(row, piece.shape[2])] = piece[n, 0]

    def copy_of(step):
        rows = pl.ds(step * per_step, per_step)
        return pltpu.make_async_copy(done.at[rows], out_hbm.at[rows], sems.at[step])

    @pl.loop(0, held.shape[0] // per_step)
    def _(step):
        for n in range(per_step):
            k = step * per_step + n
            done[k] = 0.5 * (held[k].astype(jnp.float32) + held[mirror_ref[k]].astype(jnp.float32))
        copy_of(step).start()

    @pl.loop(0, held.shape[0] // per_step)
    def _(step):
        copy_of(step).wait()


def combine(pieces, sources, mirror, place, n_pair, after):
    block, lanes = pieces[0].shape[-2:]
    k_all = sum(CHUNKS)
    rows = n_pair * k_all
    per_step = max(1, 16 * 64 // block)
    return pl.pallas_call(
        functools.partial(combine_kernel, sources, k_all, per_step),
        in_specs=[IN_SMEM] * 2 + [IN_VMEM] * len(pieces) + [ANYWHERE] * len(after),
        out_specs=IN_HBM,
        out_shape=jax.ShapeDtypeStruct((rows, block, lanes), jnp.float32),
        scratch_shapes=[
            pltpu.VMEM((rows, block, lanes), jnp.bfloat16),
            pltpu.VMEM((rows, block, lanes), jnp.float32),
            pltpu.SemaphoreType.DMA((rows // per_step,)),
        ],
        compiler_params=pltpu.CompilerParams(vmem_limit_bytes=24 * MIB),
        cost_estimate=COST,
        name="combine",
    )(mirror, place, *pieces, *after)


def flipped(x, axis, size, offset, name):
    with jax.named_scope(name):
        return lax.ppermute(x, axis, [(i, i ^ offset) for i in range(size)])


def digits(n_pair, sizes):
    bits = [1 << n for n in reversed(range(n_pair.bit_length() - 1))]
    masks = []
    while bits:
        size = sizes[min(len(masks), len(sizes) - 1)]
        some = bits[:size] if size > 0 else bits[size:]
        masks.append(sum(some))
        bits = [bit for bit in bits if bit not in some]
    return masks


def on_device(n_pair, n_mo, integrals, coeffs, mirror):
    rows = integrals.shape[1]
    padded = -(-rows // STEP) * STEP
    n_near = n_pair // 2
    by_r = jnp.transpose(integrals, (1, 0, 2))
    place = jnp.stack([lax.axis_index("mo"), lax.axis_index("pair")]).astype(jnp.int32)
    last = len(CHUNKS) - 1
    firsts = [sum(CHUNKS[:c]) for c in range(last + 1)]

    near, queue, token = [], [], []
    for batch, chunks in enumerate(BATCHES):
        (own, beside), far = quarter_of(place, by_r, coeffs, n_mo, padded, batch, token)
        beside = flipped(beside, "mo", n_mo, 1, f"beside{batch}")
        near += [(own, beside, sum(chunks[:c])) for c in range(len(chunks))]
        queue += far
        token = [own]

    def fetch(c, o, x):
        return flipped(x, "mo", n_mo, o, f"y{2 * c + o - 2}")

    def arrive(c):
        return [fetch(c, o, x) for o, x in enumerate(queue[c], 2)]

    arrived = [arrive(0)]
    turned, queue[1] = turn(place, coeffs, n_mo, n_pair, padded, queue[1], arrived[0][:1] + token)
    arrived += [arrive(1)] + [[] for _ in range(2, last + 1)]

    levels = [digits(n_pair, sizes) for sizes in SIZES]
    steps = [(c, c, 0) for c in range(last + 1)]
    for c, masks in enumerate(levels):
        steps += [(c + (n + n / 10 if SIZES[c][0] > 0 else n * 3 / 10), c, n) for n in range(1, len(masks))]
    parts, owners, offsets, token = [[] for _ in CHUNKS], [[] for _ in CHUNKS], [[] for _ in CHUNKS], []

    def plan(c, level):
        mask, gone = levels[c][level], sum(levels[c][:level])
        flips = [o for o in range(1, n_pair) if not o & ~mask][::-1]
        left = [o for o in range(n_pair) if not o & gone]
        return [o for o in left if not o & mask], flips, [[o for o in left if o & mask == flip] for flip in flips]

    def send(c, level, messages):
        _, flips, sent = plan(c, level)
        before = [o for group in offsets[c] for o in group]
        for flip, some, message in zip(flips, sent, messages):
            offsets[c].append([o ^ flip for o in before])
            owners[c].append([o ^ flip for o in some])
            parts[c].append(flipped(message, "pair", n_pair, flip, f"z{flip}c{c}"))

    for _, c, level in sorted(steps):
        kept, _, sent = plan(c, level)
        if level == 0:
            blocks = [*near[c][:2], *arrived[c]]
            later, coming = LATER.get(c, (0, []))
            wait = [queue[later][o - 2] for o in coming]
            (keep, *messages), wait = half_of(blocks, turned, near[c][2], [kept, *sent], wait, token)
            arrived[later] += [fetch(later, o, x) for o, x in zip(coming, wait)]
            parts[c], owners[c], offsets[c] = [keep], [kept], [[0]]
        else:
            picks = [[[its.index(o) for o in some] for its in owners[c]] for some in sent]
            done = {(1, 1): arrived[last][:1], (last, 1): parts[0][-1:] + parts[last - 1][-2:-1]}
            done = list(done.get((c, level), []))
            messages = merge(parts[c], picks, token + done)
        token = messages[:1]
        send(c, level, messages)
    for x in [parts[last - 1][-3], parts[last - 1][-1]] + parts[last][-3:]:
        token = [wait_for([x, *token])]
    pieces = [x for chunk in parts for x in chunk]
    sources = [(tuple(group), first) for chunk, first in zip(offsets, firsts) for group in chunk]
    return combine(pieces, sources, mirror, place, n_pair, token)


def solution(mesh):
    return jax.shard_map(
        functools.partial(on_device, mesh.shape["pair"], mesh.shape["mo"]),
        mesh=mesh,
        in_specs=(P("pair", "mo", None), P(), P()),
        out_specs=P(None, "pair", "mo"),
        check_vma=False,
    )
```

```python
import functools

import jax
import jax.numpy as jnp
from jax import lax
from jax.experimental import pallas as pl
from jax.experimental.pallas import tpu as pltpu
from jax.sharding import PartitionSpec as P

LANES = 128
STEP = 64
LATER = {0: (2, [2, 3]), 1: (3, [2]), 2: (3, [3])}
BATCHES = ((4, 4), (4, 4))
CHUNKS = sum(BATCHES, ())
SIZES = ((1,), (1,), (-1, 2), (-1, 2))
PART = 256
MIB = 1024 * 1024
COST = pl.CostEstimate(flops=1024, bytes_accessed=1024, transcendentals=0)
IN_VMEM = pl.BlockSpec(memory_space=pltpu.VMEM)
IN_SMEM = pl.BlockSpec(memory_space=pltpu.SMEM)
ANYWHERE = pl.BlockSpec(memory_space=pl.ANY)
IN_HBM = pl.BlockSpec(memory_space=pltpu.MemorySpace.HBM)


def quarter_kernel(batch, n_mo, blocks, n_after, place_ref, x_hbm, c_hbm, *refs):
    outs, (x_ref, c_ref, turn_ref, x_sems, c_sem) = refs[n_after:-5], refs[-5:]
    rows, depth = x_hbm.shape[0], x_hbm.shape[2]
    padded, some, _ = x_ref.shape
    many = PART // some

    columns = []
    for o in range(n_mo):
        mine = pl.ds(pl.multiple_of((place_ref[0] ^ o) * LANES, LANES), LANES)
        columns.append(pltpu.make_async_copy(c_hbm.at[:, mine], c_ref.at[:, o * LANES : (o + 1) * LANES], c_sem.at[o]))
    parts = []
    for n, first in enumerate(range(0, padded, STEP)):
        lines = pl.ds(first, min(STEP, rows - first))
        source = x_hbm.at[lines, pl.ds(batch * some, some)]
        parts.append(pltpu.make_async_copy(source, x_ref.at[lines], x_sems.at[n]))
    for copy in parts[:1] + columns + parts[1:]:
        copy.start()
    x_ref[rows:] = jnp.zeros((padded - rows, some, depth), jnp.bfloat16)
    to = lax.broadcasted_iota(jnp.int32, (PART, PART), 0)
    source = lax.broadcasted_iota(jnp.int32, (PART, PART), 1)
    is_source = source == (to & (many - 1)) * some + (to >> (many.bit_length() - 1))
    turn_ref[...] = jnp.where(is_source, 1.0, 0.0).astype(jnp.bfloat16)
    for copy in columns:
        copy.wait()
    for n, first in enumerate(range(0, padded, STEP)):
        parts[n].wait()
        x = x_ref[first : first + STEP].reshape(STEP * some, depth)
        product = jnp.dot(x, c_ref[...], preferred_element_type=jnp.float32).astype(jnp.bfloat16)
        for part in range(STEP // many):
            lines = jnp.dot(
                turn_ref[...], product[part * PART : (part + 1) * PART], preferred_element_type=jnp.float32
            ).astype(jnp.bfloat16)
            at = first + part * many
            for out, (o, k) in zip(outs, blocks):
                for row in range(out.shape[0]):
                    line = (k + row) * many
                    out[row, at : at + many] = lines[line : line + many, o * LANES : (o + 1) * LANES]


def quarter_of(place, by_r, coeffs, n_mo, padded, batch, after):
    depth, orbitals = coeffs.shape
    chunks = BATCHES[batch]
    some = sum(chunks)
    blocks = [(0, 0), (1, 0)] + [(o, sum(chunks[:c])) for c in range(len(chunks)) for o in range(2, n_mo)]
    sizes = [some] * 2 + [kc for kc in chunks for _ in range(2, n_mo)]
    outs = [jax.ShapeDtypeStruct((kc, padded, LANES), jnp.bfloat16) for kc in sizes]
    out = pl.pallas_call(
        functools.partial(quarter_kernel, batch, n_mo, blocks, len(after)),
        in_specs=[IN_SMEM] + [IN_HBM] * 2 + [ANYWHERE] * len(after),
        out_specs=[IN_VMEM] * len(outs),
        out_shape=outs,
        scratch_shapes=[
            pltpu.VMEM((padded, some, depth), jnp.bfloat16),
            pltpu.VMEM((depth, orbitals), jnp.bfloat16),
            pltpu.VMEM((PART, PART), jnp.bfloat16),
            pltpu.SemaphoreType.DMA((padded // STEP,)),
            pltpu.SemaphoreType.DMA((n_mo,)),
        ],
        compiler_params=pltpu.CompilerParams(vmem_limit_bytes=51 * MIB),
        cost_estimate=COST,
        name="quarter",
    )(place, by_r, coeffs, *after)
    far = n_mo - 2
    return out[:2], [list(out[2 + far * c : 2 + far * (c + 1)]) for c in range(len(chunks))]


def turn_kernel(rows, n_mo, n_pair, place_ref, c_ref, *refs):
    out_ref = refs[-1]
    orbitals, padded = out_ref.shape[0], out_ref.shape[1] // n_mo
    block = orbitals // n_pair
    none = jnp.zeros((padded - rows, orbitals), jnp.float32)
    for n in range(n_mo):
        part = c_ref[n * rows : (n + 1) * rows, :].astype(jnp.float32)
        part = jnp.concatenate([part, none], axis=0).T
        columns = pl.ds(pl.multiple_of((place_ref[0] ^ n) * padded, padded), padded)
        for o in range(n_pair):
            lines = pl.ds(pl.multiple_of((place_ref[1] ^ o) * block, block), block)
            out_ref[lines, columns] = part[o * block : (o + 1) * block].astype(jnp.bfloat16)


def turn(place, coeffs, n_mo, n_pair, padded, later, after):
    depth, orbitals = coeffs.shape
    out = pl.pallas_call(
        functools.partial(turn_kernel, depth // n_mo, n_mo, n_pair),
        in_specs=[IN_SMEM, IN_VMEM] + [IN_HBM] * len(later) + [ANYWHERE] * len(after),
        out_specs=[IN_HBM] * len(later) + [IN_VMEM],
        out_shape=[jax.ShapeDtypeStruct(x.shape, x.dtype) for x in later]
        + [jax.ShapeDtypeStruct((orbitals, n_mo * padded), jnp.bfloat16)],
        input_output_aliases={2 + n: n for n in range(len(later))},
        compiler_params=pltpu.CompilerParams(vmem_limit_bytes=24 * MIB),
        cost_estimate=COST,
        name="turn",
    )(place, coeffs, *later, *after)
    return out[-1], list(out[:-1])


def half_kernel(first, owners, *refs):
    n_mo = len(refs) - len(owners) - 1
    blocks, t_ref, outs = refs[:n_mo], refs[n_mo], refs[n_mo + 1 :]
    kc, block, lanes = outs[0].shape[2:]
    firsts = [first if x.shape[0] > kc else 0 for x in blocks]
    columns = [jnp.concatenate([x[at + k] for k in range(kc)], axis=1) for x, at in zip(blocks, firsts)]
    half = jnp.dot(t_ref[...], jnp.concatenate(columns, axis=0), preferred_element_type=jnp.float32)
    for out, its in zip(outs, owners):
        for at, o in enumerate(its):
            for k in range(kc):
                piece = half[o * block : (o + 1) * block, k * lanes : (k + 1) * lanes]
                out[0, at, k] = piece.astype(jnp.bfloat16)


def half_kernel_after(n_blocks, n_outs, first, owners, *refs):
    half_kernel(first, owners, *refs[: n_blocks + 1], *refs[len(refs) - n_outs :])


def half_of(blocks, turned, first, owners, later, after):
    kc, _, lanes = blocks[-1].shape
    block = turned.shape[0] // sum(len(its) for its in owners)
    n = len(blocks) + 1
    out = pl.pallas_call(
        functools.partial(half_kernel_after, len(blocks), len(owners), first, owners),
        in_specs=[IN_VMEM] * n + [IN_HBM] * len(later) + [ANYWHERE] * len(after),
        out_specs=[IN_HBM] * len(later) + [IN_VMEM] * len(owners),
        out_shape=[jax.ShapeDtypeStruct(x.shape, x.dtype) for x in later]
        + [jax.ShapeDtypeStruct((1, len(its), kc, block, lanes), jnp.bfloat16) for its in owners],
        input_output_aliases={n + m: m for m in range(len(later))},
        compiler_params=pltpu.CompilerParams(vmem_limit_bytes=24 * MIB),
        cost_estimate=COST,
        name="half",
    )(*blocks, turned, *later, *after)
    return list(out[len(later) :]), list(out[: len(later)])


def merge_kernel(n_parts, picks, *refs):
    outs = refs[len(refs) - len(picks) :]
    for out, its in zip(outs, picks):
        at = 0
        for x, pick in zip(refs[:n_parts], its):
            for i in range(x.shape[0]):
                for n, o in enumerate(pick):
                    out[at, n] = x[i, o]
                at += 1


def merge(parts, picks, after):
    lines = sum(x.shape[0] for x in parts)
    out = pl.pallas_call(
        functools.partial(merge_kernel, len(parts), picks),
        in_specs=[IN_VMEM] * len(parts) + [ANYWHERE] * len(after),
        out_specs=[IN_VMEM] * len(picks),
        out_shape=[
            jax.ShapeDtypeStruct((lines, len(its[0]), *parts[0].shape[2:]), jnp.bfloat16) for its in picks
        ],
        compiler_params=pltpu.CompilerParams(vmem_limit_bytes=24 * MIB),
        cost_estimate=COST,
        name="merge",
    )(*parts, *after)
    return list(out)


def wait_kernel(*refs):
    refs[-1][...] = jnp.zeros_like(refs[-1])


def wait_for(after):
    return pl.pallas_call(
        wait_kernel,
        in_specs=[ANYWHERE] * len(after),
        out_specs=IN_VMEM,
        out_shape=jax.ShapeDtypeStruct((8, LANES), jnp.float32),
        compiler_params=pltpu.CompilerParams(vmem_limit_bytes=24 * MIB),
        cost_estimate=COST,
        name="wait",
    )(*after)


def combine_kernel(sources, k_all, per_step, mirror_ref, place_ref, *refs):
    pieces, (out_hbm, held, done, sems) = refs[: len(sources)], refs[-4:]
    for piece, (offsets, first) in zip(pieces, sources):
        for n, offset in enumerate(offsets):
            row = (place_ref[1] ^ offset) * k_all + first
            held[pl.ds(row, piece.shape[2])] = piece[n, 0]

    def copy_of(step):
        rows = pl.ds(step * per_step, per_step)
        return pltpu.make_async_copy(done.at[rows], out_hbm.at[rows], sems.at[step])

    @pl.loop(0, held.shape[0] // per_step)
    def _(step):
        for n in range(per_step):
            k = step * per_step + n
            done[k] = 0.5 * (held[k].astype(jnp.float32) + held[mirror_ref[k]].astype(jnp.float32))
        copy_of(step).start()

    @pl.loop(0, held.shape[0] // per_step)
    def _(step):
        copy_of(step).wait()


def combine(pieces, sources, mirror, place, n_pair, after):
    block, lanes = pieces[0].shape[-2:]
    k_all = sum(CHUNKS)
    rows = n_pair * k_all
    per_step = max(1, 16 * 64 // block)
    return pl.pallas_call(
        functools.partial(combine_kernel, sources, k_all, per_step),
        in_specs=[IN_SMEM] * 2 + [IN_VMEM] * len(pieces) + [ANYWHERE] * len(after),
        out_specs=IN_HBM,
        out_shape=jax.ShapeDtypeStruct((rows, block, lanes), jnp.float32),
        scratch_shapes=[
            pltpu.VMEM((rows, block, lanes), jnp.bfloat16),
            pltpu.VMEM((rows, block, lanes), jnp.float32),
            pltpu.SemaphoreType.DMA((rows // per_step,)),
        ],
        compiler_params=pltpu.CompilerParams(vmem_limit_bytes=24 * MIB),
        cost_estimate=COST,
        name="combine",
    )(mirror, place, *pieces, *after)


def flipped(x, axis, size, offset, name):
    with jax.named_scope(name):
        return lax.ppermute(x, axis, [(i, i ^ offset) for i in range(size)])


def digits(n_pair, sizes):
    bits = [1 << n for n in reversed(range(n_pair.bit_length() - 1))]
    masks = []
    while bits:
        size = sizes[min(len(masks), len(sizes) - 1)]
        some = bits[:size] if size > 0 else bits[size:]
        masks.append(sum(some))
        bits = [bit for bit in bits if bit not in some]
    return masks


def on_device(n_pair, n_mo, integrals, coeffs, mirror):
    rows = integrals.shape[1]
    padded = -(-rows // STEP) * STEP
    n_near = n_pair // 2
    by_r = jnp.transpose(integrals, (1, 0, 2))
    place = jnp.stack([lax.axis_index("mo"), lax.axis_index("pair")]).astype(jnp.int32)
    last = len(CHUNKS) - 1
    firsts = [sum(CHUNKS[:c]) for c in range(last + 1)]

    near, queue, token = [], [], []
    for batch, chunks in enumerate(BATCHES):
        (own, beside), far = quarter_of(place, by_r, coeffs, n_mo, padded, batch, token)
        beside = flipped(beside, "mo", n_mo, 1, f"beside{batch}")
        near += [(own, beside, sum(chunks[:c])) for c in range(len(chunks))]
        queue += far
        token = [own]

    def fetch(c, o, x):
        return flipped(x, "mo", n_mo, o, f"y{2 * c + o - 2}")

    def arrive(c):
        return [fetch(c, o, x) for o, x in enumerate(queue[c], 2)]

    arrived = [arrive(0)]
    turned, queue[1] = turn(place, coeffs, n_mo, n_pair, padded, queue[1], arrived[0][:1] + token)
    arrived += [arrive(1)] + [[] for _ in range(2, last + 1)]

    levels = [digits(n_pair, sizes) for sizes in SIZES]
    steps = [(c, c, 0) for c in range(last + 1)]
    for c, masks in enumerate(levels):
        steps += [(c + (n + n / 10 if SIZES[c][0] > 0 else n * 3 / 10), c, n) for n in range(1, len(masks))]
    parts, owners, offsets, token = [[] for _ in CHUNKS], [[] for _ in CHUNKS], [[] for _ in CHUNKS], []

    def plan(c, level):
        mask, gone = levels[c][level], sum(levels[c][:level])
        flips = [o for o in range(1, n_pair) if not o & ~mask][::-1]
        left = [o for o in range(n_pair) if not o & gone]
        return [o for o in left if not o & mask], flips, [[o for o in left if o & mask == flip] for flip in flips]

    def send(c, level, messages):
        _, flips, sent = plan(c, level)
        before = [o for group in offsets[c] for o in group]
        for flip, some, message in zip(flips, sent, messages):
            offsets[c].append([o ^ flip for o in before])
            owners[c].append([o ^ flip for o in some])
            parts[c].append(flipped(message, "pair", n_pair, flip, f"z{flip}c{c}"))

    for _, c, level in sorted(steps):
        kept, _, sent = plan(c, level)
        if level == 0:
            blocks = [*near[c][:2], *arrived[c]]
            later, coming = LATER.get(c, (0, []))
            wait = [queue[later][o - 2] for o in coming]
            (keep, *messages), wait = half_of(blocks, turned, near[c][2], [kept, *sent], wait, token)
            arrived[later] += [fetch(later, o, x) for o, x in zip(coming, wait)]
            parts[c], owners[c], offsets[c] = [keep], [kept], [[0]]
        else:
            picks = [[[its.index(o) for o in some] for its in owners[c]] for some in sent]
            done = {(1, 1): arrived[last][:1], (last, 1): parts[0][-1:]}
            done = list(done.get((c, level), []))
            messages = merge(parts[c], picks, token + done)
        token = messages[:1]
        send(c, level, messages)
    for x in parts[last - 1][-3:] + parts[last][-3:]:
        token = [wait_for([x, *token])]
    pieces = [x for chunk in parts for x in chunk]
    sources = [(tuple(group), first) for chunk, first in zip(offsets, firsts) for group in chunk]
    return combine(pieces, sources, mirror, place, n_pair, token)


def solution(mesh):
    return jax.shard_map(
        functools.partial(on_device, mesh.shape["pair"], mesh.shape["mo"]),
        mesh=mesh,
        in_specs=(P("pair", "mo", None), P(), P()),
        out_specs=P(None, "pair", "mo"),
        check_vma=False,
    )
```

```python
import functools

import jax
import jax.numpy as jnp
from jax import lax
from jax.experimental import pallas as pl
from jax.experimental.pallas import tpu as pltpu
from jax.sharding import PartitionSpec as P

LANES = 128
STEP = 64
LATER = {0: (2, [2, 3]), 1: (3, [2]), 2: (3, [3])}
BATCHES = ((4, 4), (4, 4))
CHUNKS = sum(BATCHES, ())
SIZES = ((1,), (1,), (-1, 2), (-1, 2))
PART = 256
MIB = 1024 * 1024
COST = pl.CostEstimate(flops=1024, bytes_accessed=1024, transcendentals=0)
IN_VMEM = pl.BlockSpec(memory_space=pltpu.VMEM)
IN_SMEM = pl.BlockSpec(memory_space=pltpu.SMEM)
ANYWHERE = pl.BlockSpec(memory_space=pl.ANY)
IN_HBM = pl.BlockSpec(memory_space=pltpu.MemorySpace.HBM)


def quarter_kernel(batch, n_mo, blocks, n_after, place_ref, x_hbm, c_hbm, *refs):
    outs, (x_ref, c_ref, turn_ref, x_sems, c_sem) = refs[n_after:-5], refs[-5:]
    rows, depth = x_hbm.shape[0], x_hbm.shape[2]
    padded, some, _ = x_ref.shape
    many = PART // some

    columns = []
    for o in range(n_mo):
        mine = pl.ds(pl.multiple_of((place_ref[0] ^ o) * LANES, LANES), LANES)
        columns.append(pltpu.make_async_copy(c_hbm.at[:, mine], c_ref.at[:, o * LANES : (o + 1) * LANES], c_sem.at[o]))
    parts = []
    for n, first in enumerate(range(0, padded, STEP)):
        lines = pl.ds(first, min(STEP, rows - first))
        source = x_hbm.at[lines, pl.ds(batch * some, some)]
        parts.append(pltpu.make_async_copy(source, x_ref.at[lines], x_sems.at[n]))
    for copy in parts[:1] + columns + parts[1:]:
        copy.start()
    x_ref[rows:] = jnp.zeros((padded - rows, some, depth), jnp.bfloat16)
    to = lax.broadcasted_iota(jnp.int32, (PART, PART), 0)
    source = lax.broadcasted_iota(jnp.int32, (PART, PART), 1)
    is_source = source == (to & (many - 1)) * some + (to >> (many.bit_length() - 1))
    turn_ref[...] = jnp.where(is_source, 1.0, 0.0).astype(jnp.bfloat16)
    for copy in columns:
        copy.wait()
    for n, first in enumerate(range(0, padded, STEP)):
        parts[n].wait()
        x = x_ref[first : first + STEP].reshape(STEP * some, depth)
        product = jnp.dot(x, c_ref[...], preferred_element_type=jnp.float32).astype(jnp.bfloat16)
        for part in range(STEP // many):
            lines = jnp.dot(
                turn_ref[...], product[part * PART : (part + 1) * PART], preferred_element_type=jnp.float32
            ).astype(jnp.bfloat16)
            at = first + part * many
            for out, (o, k) in zip(outs, blocks):
                for row in range(out.shape[0]):
                    line = (k + row) * many
                    out[row, at : at + many] = lines[line : line + many, o * LANES : (o + 1) * LANES]


def quarter_of(place, by_r, coeffs, n_mo, padded, batch, after):
    depth, orbitals = coeffs.shape
    chunks = BATCHES[batch]
    some = sum(chunks)
    blocks = [(0, 0), (1, 0)] + [(o, sum(chunks[:c])) for c in range(len(chunks)) for o in range(2, n_mo)]
    sizes = [some] * 2 + [kc for kc in chunks for _ in range(2, n_mo)]
    outs = [jax.ShapeDtypeStruct((kc, padded, LANES), jnp.bfloat16) for kc in sizes]
    out = pl.pallas_call(
        functools.partial(quarter_kernel, batch, n_mo, blocks, len(after)),
        in_specs=[IN_SMEM] + [IN_HBM] * 2 + [ANYWHERE] * len(after),
        out_specs=[IN_VMEM] * len(outs),
        out_shape=outs,
        scratch_shapes=[
            pltpu.VMEM((padded, some, depth), jnp.bfloat16),
            pltpu.VMEM((depth, orbitals), jnp.bfloat16),
            pltpu.VMEM((PART, PART), jnp.bfloat16),
            pltpu.SemaphoreType.DMA((padded // STEP,)),
            pltpu.SemaphoreType.DMA((n_mo,)),
        ],
        compiler_params=pltpu.CompilerParams(vmem_limit_bytes=51 * MIB),
        cost_estimate=COST,
        name="quarter",
    )(place, by_r, coeffs, *after)
    far = n_mo - 2
    return out[:2], [list(out[2 + far * c : 2 + far * (c + 1)]) for c in range(len(chunks))]


def turn_kernel(rows, n_mo, n_pair, place_ref, c_ref, *refs):
    out_ref = refs[-1]
    orbitals, padded = out_ref.shape[0], out_ref.shape[1] // n_mo
    block = orbitals // n_pair
    none = jnp.zeros((padded - rows, orbitals), jnp.float32)
    for n in range(n_mo):
        part = c_ref[n * rows : (n + 1) * rows, :].astype(jnp.float32)
        part = jnp.concatenate([part, none], axis=0).T
        columns = pl.ds(pl.multiple_of((place_ref[0] ^ n) * padded, padded), padded)
        for o in range(n_pair):
            lines = pl.ds(pl.multiple_of((place_ref[1] ^ o) * block, block), block)
            out_ref[lines, columns] = part[o * block : (o + 1) * block].astype(jnp.bfloat16)


def turn(place, coeffs, n_mo, n_pair, padded, later, after):
    depth, orbitals = coeffs.shape
    out = pl.pallas_call(
        functools.partial(turn_kernel, depth // n_mo, n_mo, n_pair),
        in_specs=[IN_SMEM, IN_VMEM] + [IN_HBM] * len(later) + [ANYWHERE] * len(after),
        out_specs=[IN_HBM] * len(later) + [IN_VMEM],
        out_shape=[jax.ShapeDtypeStruct(x.shape, x.dtype) for x in later]
        + [jax.ShapeDtypeStruct((orbitals, n_mo * padded), jnp.bfloat16)],
        input_output_aliases={2 + n: n for n in range(len(later))},
        compiler_params=pltpu.CompilerParams(vmem_limit_bytes=24 * MIB),
        cost_estimate=COST,
        name="turn",
    )(place, coeffs, *later, *after)
    return out[-1], list(out[:-1])


def half_kernel(first, owners, *refs):
    n_mo = len(refs) - len(owners) - 1
    blocks, t_ref, outs = refs[:n_mo], refs[n_mo], refs[n_mo + 1 :]
    kc, block, lanes = outs[0].shape[2:]
    firsts = [first if x.shape[0] > kc else 0 for x in blocks]
    columns = [jnp.concatenate([x[at + k] for k in range(kc)], axis=1) for x, at in zip(blocks, firsts)]
    half = jnp.dot(t_ref[...], jnp.concatenate(columns, axis=0), preferred_element_type=jnp.float32)
    for out, its in zip(outs, owners):
        for at, o in enumerate(its):
            for k in range(kc):
                piece = half[o * block : (o + 1) * block, k * lanes : (k + 1) * lanes]
                out[0, at, k] = piece.astype(jnp.bfloat16)


def half_kernel_after(n_blocks, n_outs, first, owners, *refs):
    half_kernel(first, owners, *refs[: n_blocks + 1], *refs[len(refs) - n_outs :])


def half_of(blocks, turned, first, owners, later, after):
    kc, _, lanes = blocks[-1].shape
    block = turned.shape[0] // sum(len(its) for its in owners)
    n = len(blocks) + 1
    out = pl.pallas_call(
        functools.partial(half_kernel_after, len(blocks), len(owners), first, owners),
        in_specs=[IN_VMEM] * n + [IN_HBM] * len(later) + [ANYWHERE] * len(after),
        out_specs=[IN_HBM] * len(later) + [IN_VMEM] * len(owners),
        out_shape=[jax.ShapeDtypeStruct(x.shape, x.dtype) for x in later]
        + [jax.ShapeDtypeStruct((1, len(its), kc, block, lanes), jnp.bfloat16) for its in owners],
        input_output_aliases={n + m: m for m in range(len(later))},
        compiler_params=pltpu.CompilerParams(vmem_limit_bytes=24 * MIB),
        cost_estimate=COST,
        name="half",
    )(*blocks, turned, *later, *after)
    return list(out[len(later) :]), list(out[: len(later)])


def merge_kernel(n_parts, picks, *refs):
    outs = refs[len(refs) - len(picks) :]
    for out, its in zip(outs, picks):
        at = 0
        for x, pick in zip(refs[:n_parts], its):
            for i in range(x.shape[0]):
                for n, o in enumerate(pick):
                    out[at, n] = x[i, o]
                at += 1


def merge(parts, picks, after):
    lines = sum(x.shape[0] for x in parts)
    out = pl.pallas_call(
        functools.partial(merge_kernel, len(parts), picks),
        in_specs=[IN_VMEM] * len(parts) + [ANYWHERE] * len(after),
        out_specs=[IN_VMEM] * len(picks),
        out_shape=[
            jax.ShapeDtypeStruct((lines, len(its[0]), *parts[0].shape[2:]), jnp.bfloat16) for its in picks
        ],
        compiler_params=pltpu.CompilerParams(vmem_limit_bytes=24 * MIB),
        cost_estimate=COST,
        name="merge",
    )(*parts, *after)
    return list(out)


def wait_kernel(*refs):
    refs[-1][...] = jnp.zeros_like(refs[-1])


def wait_for(after):
    return pl.pallas_call(
        wait_kernel,
        in_specs=[ANYWHERE] * len(after),
        out_specs=IN_VMEM,
        out_shape=jax.ShapeDtypeStruct((8, LANES), jnp.float32),
        compiler_params=pltpu.CompilerParams(vmem_limit_bytes=24 * MIB),
        cost_estimate=COST,
        name="wait",
    )(*after)


def combine_kernel(sources, k_all, per_step, mirror_ref, place_ref, *refs):
    pieces, (out_hbm, held, done, sems) = refs[: len(sources)], refs[-4:]
    for piece, (offsets, first) in zip(pieces, sources):
        for n, offset in enumerate(offsets):
            row = (place_ref[1] ^ offset) * k_all + first
            held[pl.ds(row, piece.shape[2])] = piece[n, 0]

    def copy_of(step):
        rows = pl.ds(step * per_step, per_step)
        return pltpu.make_async_copy(done.at[rows], out_hbm.at[rows], sems.at[step])

    @pl.loop(0, held.shape[0] // per_step)
    def _(step):
        for n in range(per_step):
            k = step * per_step + n
            done[k] = 0.5 * (held[k].astype(jnp.float32) + held[mirror_ref[k]].astype(jnp.float32))
        copy_of(step).start()

    @pl.loop(0, held.shape[0] // per_step)
    def _(step):
        copy_of(step).wait()


def combine(pieces, sources, mirror, place, n_pair, after):
    block, lanes = pieces[0].shape[-2:]
    k_all = sum(CHUNKS)
    rows = n_pair * k_all
    per_step = max(1, 16 * 64 // block)
    return pl.pallas_call(
        functools.partial(combine_kernel, sources, k_all, per_step),
        in_specs=[IN_SMEM] * 2 + [IN_VMEM] * len(pieces) + [ANYWHERE] * len(after),
        out_specs=IN_HBM,
        out_shape=jax.ShapeDtypeStruct((rows, block, lanes), jnp.float32),
        scratch_shapes=[
            pltpu.VMEM((rows, block, lanes), jnp.bfloat16),
            pltpu.VMEM((rows, block, lanes), jnp.float32),
            pltpu.SemaphoreType.DMA((rows // per_step,)),
        ],
        compiler_params=pltpu.CompilerParams(vmem_limit_bytes=24 * MIB),
        cost_estimate=COST,
        name="combine",
    )(mirror, place, *pieces, *after)


def flipped(x, axis, size, offset, name):
    with jax.named_scope(name):
        return lax.ppermute(x, axis, [(i, i ^ offset) for i in range(size)])


def digits(n_pair, sizes):
    bits = [1 << n for n in reversed(range(n_pair.bit_length() - 1))]
    masks = []
    while bits:
        size = sizes[min(len(masks), len(sizes) - 1)]
        some = bits[:size] if size > 0 else bits[size:]
        masks.append(sum(some))
        bits = [bit for bit in bits if bit not in some]
    return masks


def on_device(n_pair, n_mo, integrals, coeffs, mirror):
    rows = integrals.shape[1]
    padded = -(-rows // STEP) * STEP
    n_near = n_pair // 2
    by_r = jnp.transpose(integrals, (1, 0, 2))
    place = jnp.stack([lax.axis_index("mo"), lax.axis_index("pair")]).astype(jnp.int32)
    last = len(CHUNKS) - 1
    firsts = [sum(CHUNKS[:c]) for c in range(last + 1)]

    near, queue, token = [], [], []
    for batch, chunks in enumerate(BATCHES):
        (own, beside), far = quarter_of(place, by_r, coeffs, n_mo, padded, batch, token)
        beside = flipped(beside, "mo", n_mo, 1, f"beside{batch}")
        near += [(own, beside, sum(chunks[:c])) for c in range(len(chunks))]
        queue += far
        token = [own]

    def fetch(c, o, x):
        return flipped(x, "mo", n_mo, o, f"y{2 * c + o - 2}")

    def arrive(c):
        return [fetch(c, o, x) for o, x in enumerate(queue[c], 2)]

    arrived = [arrive(0)]
    turned, queue[1] = turn(place, coeffs, n_mo, n_pair, padded, queue[1], arrived[0][:1] + token)
    arrived += [arrive(1)] + [[] for _ in range(2, last + 1)]

    levels = [digits(n_pair, sizes) for sizes in SIZES]
    steps = [(c, c, 0) for c in range(last + 1)]
    for c, masks in enumerate(levels):
        steps += [(c + (n + n / 10 if SIZES[c][0] > 0 else n * 3 / 10), c, n) for n in range(1, len(masks))]
    parts, owners, offsets, token = [[] for _ in CHUNKS], [[] for _ in CHUNKS], [[] for _ in CHUNKS], []

    def plan(c, level):
        mask, gone = levels[c][level], sum(levels[c][:level])
        flips = [o for o in range(1, n_pair) if not o & ~mask][::-1]
        left = [o for o in range(n_pair) if not o & gone]
        return [o for o in left if not o & mask], flips, [[o for o in left if o & mask == flip] for flip in flips]

    def send(c, level, messages):
        _, flips, sent = plan(c, level)
        before = [o for group in offsets[c] for o in group]
        for flip, some, message in zip(flips, sent, messages):
            offsets[c].append([o ^ flip for o in before])
            owners[c].append([o ^ flip for o in some])
            parts[c].append(flipped(message, "pair", n_pair, flip, f"z{flip}c{c}"))

    for _, c, level in sorted(steps):
        kept, _, sent = plan(c, level)
        if level == 0:
            blocks = [*near[c][:2], *arrived[c]]
            later, coming = LATER.get(c, (0, []))
            wait = [queue[later][o - 2] for o in coming]
            (keep, *messages), wait = half_of(blocks, turned, near[c][2], [kept, *sent], wait, token)
            arrived[later] += [fetch(later, o, x) for o, x in zip(coming, wait)]
            parts[c], owners[c], offsets[c] = [keep], [kept], [[0]]
        else:
            picks = [[[its.index(o) for o in some] for its in owners[c]] for some in sent]
            done = {(1, 1): arrived[last][:1], (last, 1): parts[0][-1:]}
            done = list(done.get((c, level), []))
            messages = merge(parts[c], picks, token + done)
        token = messages[:1]
        send(c, level, messages)
    for x in [parts[last - 1][n] for n in (-2, -1, -3)] + parts[last][-3:]:
        token = [wait_for([x, *token])]
    pieces = [x for chunk in parts for x in chunk]
    sources = [(tuple(group), first) for chunk, first in zip(offsets, firsts) for group in chunk]
    return combine(pieces, sources, mirror, place, n_pair, token)


def solution(mesh):
    return jax.shard_map(
        functools.partial(on_device, mesh.shape["pair"], mesh.shape["mo"]),
        mesh=mesh,
        in_specs=(P("pair", "mo", None), P(), P()),
        out_specs=P(None, "pair", "mo"),
        check_vma=False,
    )
```

```python
import functools

import jax
import jax.numpy as jnp
from jax import lax
from jax.experimental import pallas as pl
from jax.experimental.pallas import tpu as pltpu
from jax.sharding import PartitionSpec as P

LANES = 128
STEP = 128
LATER = {0: (2, [2, 3]), 1: (3, [2]), 2: (3, [3])}
BATCHES = ((4, 4), (4, 4))
CHUNKS = sum(BATCHES, ())
SIZES = ((1,), (1,), (-1, 2), (-1, 2))
PART = 256
MIB = 1024 * 1024
COST = pl.CostEstimate(flops=1024, bytes_accessed=1024, transcendentals=0)
IN_VMEM = pl.BlockSpec(memory_space=pltpu.VMEM)
IN_SMEM = pl.BlockSpec(memory_space=pltpu.SMEM)
ANYWHERE = pl.BlockSpec(memory_space=pl.ANY)
IN_HBM = pl.BlockSpec(memory_space=pltpu.MemorySpace.HBM)


def quarter_kernel(batch, n_mo, blocks, n_after, place_ref, x_hbm, c_hbm, *refs):
    outs, (x_ref, c_ref, turn_ref, x_sems, c_sem) = refs[n_after:-5], refs[-5:]
    rows, depth = x_hbm.shape[0], x_hbm.shape[2]
    padded, some, _ = x_ref.shape
    many = PART // some

    columns = []
    for o in range(n_mo):
        mine = pl.ds(pl.multiple_of((place_ref[0] ^ o) * LANES, LANES), LANES)
        columns.append(pltpu.make_async_copy(c_hbm.at[:, mine], c_ref.at[:, o * LANES : (o + 1) * LANES], c_sem.at[o]))
    parts = []
    for n, first in enumerate(range(0, padded, STEP)):
        lines = pl.ds(first, min(STEP, rows - first))
        source = x_hbm.at[lines, pl.ds(batch * some, some)]
        parts.append(pltpu.make_async_copy(source, x_ref.at[lines], x_sems.at[n]))
    for copy in parts[:1] + columns + parts[1:]:
        copy.start()
    x_ref[rows:] = jnp.zeros((padded - rows, some, depth), jnp.bfloat16)
    to = lax.broadcasted_iota(jnp.int32, (PART, PART), 0)
    source = lax.broadcasted_iota(jnp.int32, (PART, PART), 1)
    is_source = source == (to & (many - 1)) * some + (to >> (many.bit_length() - 1))
    turn_ref[...] = jnp.where(is_source, 1.0, 0.0).astype(jnp.bfloat16)
    for copy in columns:
        copy.wait()
    for n, first in enumerate(range(0, padded, STEP)):
        parts[n].wait()
        x = x_ref[first : first + STEP].reshape(STEP * some, depth)
        product = jnp.dot(x, c_ref[...], preferred_element_type=jnp.float32).astype(jnp.bfloat16)
        for part in range(STEP // many):
            lines = jnp.dot(
                turn_ref[...], product[part * PART : (part + 1) * PART], preferred_element_type=jnp.float32
            ).astype(jnp.bfloat16)
            at = first + part * many
            for out, (o, k) in zip(outs, blocks):
                for row in range(out.shape[0]):
                    line = (k + row) * many
                    out[row, at : at + many] = lines[line : line + many, o * LANES : (o + 1) * LANES]


def quarter_of(place, by_r, coeffs, n_mo, padded, batch, after):
    depth, orbitals = coeffs.shape
    chunks = BATCHES[batch]
    some = sum(chunks)
    blocks = [(0, 0), (1, 0)] + [(o, sum(chunks[:c])) for c in range(len(chunks)) for o in range(2, n_mo)]
    sizes = [some] * 2 + [kc for kc in chunks for _ in range(2, n_mo)]
    outs = [jax.ShapeDtypeStruct((kc, padded, LANES), jnp.bfloat16) for kc in sizes]
    out = pl.pallas_call(
        functools.partial(quarter_kernel, batch, n_mo, blocks, len(after)),
        in_specs=[IN_SMEM] + [IN_HBM] * 2 + [ANYWHERE] * len(after),
        out_specs=[IN_VMEM] * len(outs),
        out_shape=outs,
        scratch_shapes=[
            pltpu.VMEM((padded, some, depth), jnp.bfloat16),
            pltpu.VMEM((depth, orbitals), jnp.bfloat16),
            pltpu.VMEM((PART, PART), jnp.bfloat16),
            pltpu.SemaphoreType.DMA((padded // STEP,)),
            pltpu.SemaphoreType.DMA((n_mo,)),
        ],
        compiler_params=pltpu.CompilerParams(vmem_limit_bytes=51 * MIB),
        cost_estimate=COST,
        name="quarter",
    )(place, by_r, coeffs, *after)
    far = n_mo - 2
    return out[:2], [list(out[2 + far * c : 2 + far * (c + 1)]) for c in range(len(chunks))]


def turn_kernel(rows, n_mo, n_pair, place_ref, c_ref, *refs):
    out_ref = refs[-1]
    orbitals, padded = out_ref.shape[0], out_ref.shape[1] // n_mo
    block = orbitals // n_pair
    none = jnp.zeros((padded - rows, orbitals), jnp.float32)
    for n in range(n_mo):
        part = c_ref[n * rows : (n + 1) * rows, :].astype(jnp.float32)
        part = jnp.concatenate([part, none], axis=0).T
        columns = pl.ds(pl.multiple_of((place_ref[0] ^ n) * padded, padded), padded)
        for o in range(n_pair):
            lines = pl.ds(pl.multiple_of((place_ref[1] ^ o) * block, block), block)
            out_ref[lines, columns] = part[o * block : (o + 1) * block].astype(jnp.bfloat16)


def turn(place, coeffs, n_mo, n_pair, padded, later, after):
    depth, orbitals = coeffs.shape
    out = pl.pallas_call(
        functools.partial(turn_kernel, depth // n_mo, n_mo, n_pair),
        in_specs=[IN_SMEM, IN_VMEM] + [IN_HBM] * len(later) + [ANYWHERE] * len(after),
        out_specs=[IN_HBM] * len(later) + [IN_VMEM],
        out_shape=[jax.ShapeDtypeStruct(x.shape, x.dtype) for x in later]
        + [jax.ShapeDtypeStruct((orbitals, n_mo * padded), jnp.bfloat16)],
        input_output_aliases={2 + n: n for n in range(len(later))},
        compiler_params=pltpu.CompilerParams(vmem_limit_bytes=24 * MIB),
        cost_estimate=COST,
        name="turn",
    )(place, coeffs, *later, *after)
    return out[-1], list(out[:-1])


def half_kernel(first, owners, *refs):
    n_mo = len(refs) - len(owners) - 1
    blocks, t_ref, outs = refs[:n_mo], refs[n_mo], refs[n_mo + 1 :]
    kc, block, lanes = outs[0].shape[2:]
    firsts = [first if x.shape[0] > kc else 0 for x in blocks]
    columns = [jnp.concatenate([x[at + k] for k in range(kc)], axis=1) for x, at in zip(blocks, firsts)]
    half = jnp.dot(t_ref[...], jnp.concatenate(columns, axis=0), preferred_element_type=jnp.float32)
    for out, its in zip(outs, owners):
        for at, o in enumerate(its):
            for k in range(kc):
                piece = half[o * block : (o + 1) * block, k * lanes : (k + 1) * lanes]
                out[0, at, k] = piece.astype(jnp.bfloat16)


def half_kernel_after(n_blocks, n_outs, first, owners, *refs):
    half_kernel(first, owners, *refs[: n_blocks + 1], *refs[len(refs) - n_outs :])


def half_of(blocks, turned, first, owners, later, after):
    kc, _, lanes = blocks[-1].shape
    block = turned.shape[0] // sum(len(its) for its in owners)
    n = len(blocks) + 1
    out = pl.pallas_call(
        functools.partial(half_kernel_after, len(blocks), len(owners), first, owners),
        in_specs=[IN_VMEM] * n + [IN_HBM] * len(later) + [ANYWHERE] * len(after),
        out_specs=[IN_HBM] * len(later) + [IN_VMEM] * len(owners),
        out_shape=[jax.ShapeDtypeStruct(x.shape, x.dtype) for x in later]
        + [jax.ShapeDtypeStruct((1, len(its), kc, block, lanes), jnp.bfloat16) for its in owners],
        input_output_aliases={n + m: m for m in range(len(later))},
        compiler_params=pltpu.CompilerParams(vmem_limit_bytes=24 * MIB),
        cost_estimate=COST,
        name="half",
    )(*blocks, turned, *later, *after)
    return list(out[len(later) :]), list(out[: len(later)])


def merge_kernel(n_parts, picks, *refs):
    outs = refs[len(refs) - len(picks) :]
    for out, its in zip(outs, picks):
        at = 0
        for x, pick in zip(refs[:n_parts], its):
            for i in range(x.shape[0]):
                for n, o in enumerate(pick):
                    out[at, n] = x[i, o]
                at += 1


def merge(parts, picks, after):
    lines = sum(x.shape[0] for x in parts)
    out = pl.pallas_call(
        functools.partial(merge_kernel, len(parts), picks),
        in_specs=[IN_VMEM] * len(parts) + [ANYWHERE] * len(after),
        out_specs=[IN_VMEM] * len(picks),
        out_shape=[
            jax.ShapeDtypeStruct((lines, len(its[0]), *parts[0].shape[2:]), jnp.bfloat16) for its in picks
        ],
        compiler_params=pltpu.CompilerParams(vmem_limit_bytes=24 * MIB),
        cost_estimate=COST,
        name="merge",
    )(*parts, *after)
    return list(out)


def wait_kernel(*refs):
    refs[-1][...] = jnp.zeros_like(refs[-1])


def wait_for(after):
    return pl.pallas_call(
        wait_kernel,
        in_specs=[ANYWHERE] * len(after),
        out_specs=IN_VMEM,
        out_shape=jax.ShapeDtypeStruct((8, LANES), jnp.float32),
        compiler_params=pltpu.CompilerParams(vmem_limit_bytes=24 * MIB),
        cost_estimate=COST,
        name="wait",
    )(*after)


def place_rows(pieces, sources, k_all, place_ref, held):
    for piece, (offsets, first) in zip(pieces, sources):
        for n, offset in enumerate(offsets):
            row = (place_ref[1] ^ offset) * k_all + first
            held[pl.ds(row, piece.shape[2])] = piece[n, 0]


def collect_kernel(sources, k_all, place_ref, *refs):
    place_rows(refs, sources, k_all, place_ref, refs[-1])


def collect(pieces, sources, place, n_pair, after):
    block, lanes = pieces[0].shape[-2:]
    k_all = sum(CHUNKS)
    return pl.pallas_call(
        functools.partial(collect_kernel, sources, k_all),
        in_specs=[IN_SMEM] + [IN_VMEM] * len(pieces) + [ANYWHERE] * len(after),
        out_specs=IN_VMEM,
        out_shape=jax.ShapeDtypeStruct((n_pair * k_all, block, lanes), jnp.bfloat16),
        compiler_params=pltpu.CompilerParams(vmem_limit_bytes=24 * MIB),
        cost_estimate=COST,
        name="collect",
    )(place, *pieces, *after)


def combine_kernel(sources, k_all, per_step, mirror_ref, place_ref, *refs):
    out_hbm, held, done, sems = refs[-4:]
    place_rows(refs[1:], sources, k_all, place_ref, held)

    def copy_of(step):
        rows = pl.ds(step * per_step, per_step)
        return pltpu.make_async_copy(done.at[rows], out_hbm.at[rows], sems.at[step])

    @pl.loop(0, held.shape[0] // per_step)
    def _(step):
        for n in range(per_step):
            k = step * per_step + n
            done[k] = 0.5 * (held[k].astype(jnp.float32) + held[mirror_ref[k]].astype(jnp.float32))
        copy_of(step).start()

    @pl.loop(0, held.shape[0] // per_step)
    def _(step):
        copy_of(step).wait()


def combine(held, pieces, sources, mirror, place, after):
    rows, block, lanes = held.shape
    per_step = max(1, 16 * 64 // block)
    return pl.pallas_call(
        functools.partial(combine_kernel, sources, sum(CHUNKS), per_step),
        in_specs=[IN_SMEM] * 2 + [IN_VMEM] * (1 + len(pieces)) + [ANYWHERE] * len(after),
        out_specs=[IN_HBM, IN_VMEM],
        out_shape=[
            jax.ShapeDtypeStruct((rows, block, lanes), jnp.float32),
            jax.ShapeDtypeStruct((rows, block, lanes), jnp.bfloat16),
        ],
        input_output_aliases={2: 1},
        scratch_shapes=[
            pltpu.VMEM((rows, block, lanes), jnp.float32),
            pltpu.SemaphoreType.DMA((rows // per_step,)),
        ],
        compiler_params=pltpu.CompilerParams(vmem_limit_bytes=24 * MIB),
        cost_estimate=COST,
        name="combine",
    )(mirror, place, held, *pieces, *after)[0]


def flipped(x, axis, size, offset, name):
    with jax.named_scope(name):
        return lax.ppermute(x, axis, [(i, i ^ offset) for i in range(size)])


def digits(n_pair, sizes):
    bits = [1 << n for n in reversed(range(n_pair.bit_length() - 1))]
    masks = []
    while bits:
        size = sizes[min(len(masks), len(sizes) - 1)]
        some = bits[:size] if size > 0 else bits[size:]
        masks.append(sum(some))
        bits = [bit for bit in bits if bit not in some]
    return masks


def on_device(n_pair, n_mo, integrals, coeffs, mirror):
    rows = integrals.shape[1]
    padded = -(-rows // STEP) * STEP
    n_near = n_pair // 2
    by_r = jnp.transpose(integrals, (1, 0, 2))
    place = jnp.stack([lax.axis_index("mo"), lax.axis_index("pair")]).astype(jnp.int32)
    last = len(CHUNKS) - 1
    firsts = [sum(CHUNKS[:c]) for c in range(last + 1)]

    near, queue, token = [], [], []
    for batch, chunks in enumerate(BATCHES):
        (own, beside), far = quarter_of(place, by_r, coeffs, n_mo, padded, batch, token)
        beside = flipped(beside, "mo", n_mo, 1, f"beside{batch}")
        near += [(own, beside, sum(chunks[:c])) for c in range(len(chunks))]
        queue += far
        token = [own]

    def fetch(c, o, x):
        return flipped(x, "mo", n_mo, o, f"y{2 * c + o - 2}")

    def arrive(c):
        return [fetch(c, o, x) for o, x in enumerate(queue[c], 2)]

    arrived = [arrive(0)]
    turned, queue[1] = turn(place, coeffs, n_mo, n_pair, padded, queue[1], arrived[0][:1] + token)
    arrived += [arrive(1)] + [[] for _ in range(2, last + 1)]

    levels = [digits(n_pair, sizes) for sizes in SIZES]
    steps = [(c, c, 0) for c in range(last + 1)]
    for c, masks in enumerate(levels):
        steps += [(c + (n + n / 10 if SIZES[c][0] > 0 else n * 3 / 10), c, n) for n in range(1, len(masks))]
    parts, owners, offsets, token = [[] for _ in CHUNKS], [[] for _ in CHUNKS], [[] for _ in CHUNKS], []

    def plan(c, level):
        mask, gone = levels[c][level], sum(levels[c][:level])
        flips = [o for o in range(1, n_pair) if not o & ~mask][::-1]
        left = [o for o in range(n_pair) if not o & gone]
        return [o for o in left if not o & mask], flips, [[o for o in left if o & mask == flip] for flip in flips]

    def send(c, level, messages):
        _, flips, sent = plan(c, level)
        before = [o for group in offsets[c] for o in group]
        for flip, some, message in zip(flips, sent, messages):
            offsets[c].append([o ^ flip for o in before])
            owners[c].append([o ^ flip for o in some])
            parts[c].append(flipped(message, "pair", n_pair, flip, f"z{flip}c{c}"))

    for _, c, level in sorted(steps):
        kept, _, sent = plan(c, level)
        if level == 0:
            blocks = [*near[c][:2], *arrived[c]]
            later, coming = LATER.get(c, (0, []))
            wait = [queue[later][o - 2] for o in coming]
            (keep, *messages), wait = half_of(blocks, turned, near[c][2], [kept, *sent], wait, token)
            arrived[later] += [fetch(later, o, x) for o, x in zip(coming, wait)]
            parts[c], owners[c], offsets[c] = [keep], [kept], [[0]]
        else:
            picks = [[[its.index(o) for o in some] for its in owners[c]] for some in sent]
            done = {(1, 1): arrived[last][:1], (last, 1): parts[0][-1:]}
            done = list(done.get((c, level), []))
            messages = merge(parts[c], picks, token + done)
        token = messages[:1]
        send(c, level, messages)
    for n in (-2, -1, -3):
        token = [wait_for([parts[last - 1][n], *token])]
    late = [parts[1][-1], *parts[last][-3:]]
    both = [
        (x, (tuple(group), first))
        for chunk, its, first in zip(parts, offsets, firsts)
        for x, group in zip(chunk, its)
    ]
    early = [entry for entry in both if all(entry[0] is not x for x in late)]
    held = collect(*zip(*early), place, n_pair, token)
    token = [held]
    for x in late[1:]:
        token = [wait_for([x, *token])]
    rest = [entry for entry in both if any(entry[0] is x for x in late)]
    return combine(held, *zip(*rest), mirror, place, token[:1] if token[0] is not held else [])


def solution(mesh):
    return jax.shard_map(
        functools.partial(on_device, mesh.shape["pair"], mesh.shape["mo"]),
        mesh=mesh,
        in_specs=(P("pair", "mo", None), P(), P()),
        out_specs=P(None, "pair", "mo"),
        check_vma=False,
    )
```

```python
import functools

import jax
import jax.numpy as jnp
from jax import lax
from jax.experimental import pallas as pl
from jax.experimental.pallas import tpu as pltpu
from jax.sharding import PartitionSpec as P

LANES = 128
STEP = 64
LATER = {0: (2, [2, 3]), 1: (3, [2]), 2: (3, [3])}
BATCHES = ((4, 4), (4, 4))
CHUNKS = sum(BATCHES, ())
SIZES = ((1,), (1,), (-1, 2), (-1, 2))
PART = 256
MIB = 1024 * 1024
COST = pl.CostEstimate(flops=1024, bytes_accessed=1024, transcendentals=0)
IN_VMEM = pl.BlockSpec(memory_space=pltpu.VMEM)
IN_SMEM = pl.BlockSpec(memory_space=pltpu.SMEM)
ANYWHERE = pl.BlockSpec(memory_space=pl.ANY)
IN_HBM = pl.BlockSpec(memory_space=pltpu.MemorySpace.HBM)


def quarter_kernel(batch, n_mo, blocks, n_after, place_ref, x_hbm, c_hbm, *refs):
    outs, (x_ref, c_ref, turn_ref, x_sems, c_sem) = refs[n_after:-5], refs[-5:]
    rows, depth = x_hbm.shape[0], x_hbm.shape[2]
    padded, some, _ = x_ref.shape
    many = PART // some

    columns = []
    for o in range(n_mo):
        mine = pl.ds(pl.multiple_of((place_ref[0] ^ o) * LANES, LANES), LANES)
        columns.append(pltpu.make_async_copy(c_hbm.at[:, mine], c_ref.at[:, o * LANES : (o + 1) * LANES], c_sem.at[o]))
    parts = []
    steps = [(0, STEP), (STEP, padded - STEP)]
    for n, (first, step) in enumerate(steps):
        lines = pl.ds(first, min(step, rows - first))
        source = x_hbm.at[lines, pl.ds(batch * some, some)]
        parts.append(pltpu.make_async_copy(source, x_ref.at[lines], x_sems.at[n]))
    for copy in columns + parts:
        copy.start()
    x_ref[rows:] = jnp.zeros((padded - rows, some, depth), jnp.bfloat16)
    to = lax.broadcasted_iota(jnp.int32, (PART, PART), 0)
    source = lax.broadcasted_iota(jnp.int32, (PART, PART), 1)
    is_source = source == (to & (many - 1)) * some + (to >> (many.bit_length() - 1))
    turn_ref[...] = jnp.where(is_source, 1.0, 0.0).astype(jnp.bfloat16)
    for copy in columns:
        copy.wait()
    for n, (first, step) in enumerate(steps):
        parts[n].wait()
        x = x_ref[first : first + step].reshape(step * some, depth)
        product = jnp.dot(x, c_ref[...], preferred_element_type=jnp.float32).astype(jnp.bfloat16)
        for part in range(step // many):
            lines = jnp.dot(
                turn_ref[...], product[part * PART : (part + 1) * PART], preferred_element_type=jnp.float32
            ).astype(jnp.bfloat16)
            at = first + part * many
            for out, (o, k) in zip(outs, blocks):
                for row in range(out.shape[0]):
                    line = (k + row) * many
                    out[row, at : at + many] = lines[line : line + many, o * LANES : (o + 1) * LANES]


def quarter_of(place, by_r, coeffs, n_mo, padded, batch, after):
    depth, orbitals = coeffs.shape
    chunks = BATCHES[batch]
    some = sum(chunks)
    blocks = [(0, 0), (1, 0)] + [(o, sum(chunks[:c])) for c in range(len(chunks)) for o in range(2, n_mo)]
    sizes = [some] * 2 + [kc for kc in chunks for _ in range(2, n_mo)]
    outs = [jax.ShapeDtypeStruct((kc, padded, LANES), jnp.bfloat16) for kc in sizes]
    out = pl.pallas_call(
        functools.partial(quarter_kernel, batch, n_mo, blocks, len(after)),
        in_specs=[IN_SMEM] + [IN_HBM] * 2 + [ANYWHERE] * len(after),
        out_specs=[IN_VMEM] * len(outs),
        out_shape=outs,
        scratch_shapes=[
            pltpu.VMEM((padded, some, depth), jnp.bfloat16),
            pltpu.VMEM((depth, orbitals), jnp.bfloat16),
            pltpu.VMEM((PART, PART), jnp.bfloat16),
            pltpu.SemaphoreType.DMA((2,)),
            pltpu.SemaphoreType.DMA((n_mo,)),
        ],
        compiler_params=pltpu.CompilerParams(vmem_limit_bytes=51 * MIB),
        cost_estimate=COST,
        name="quarter",
    )(place, by_r, coeffs, *after)
    far = n_mo - 2
    return out[:2], [list(out[2 + far * c : 2 + far * (c + 1)]) for c in range(len(chunks))]


def turn_kernel(rows, n_mo, n_pair, place_ref, c_ref, *refs):
    out_ref = refs[-1]
    orbitals, padded = out_ref.shape[0], out_ref.shape[1] // n_mo
    block = orbitals // n_pair
    none = jnp.zeros((padded - rows, orbitals), jnp.float32)
    for n in range(n_mo):
        part = c_ref[n * rows : (n + 1) * rows, :].astype(jnp.float32)
        part = jnp.concatenate([part, none], axis=0).T
        columns = pl.ds(pl.multiple_of((place_ref[0] ^ n) * padded, padded), padded)
        for o in range(n_pair):
            lines = pl.ds(pl.multiple_of((place_ref[1] ^ o) * block, block), block)
            out_ref[lines, columns] = part[o * block : (o + 1) * block].astype(jnp.bfloat16)


def turn(place, coeffs, n_mo, n_pair, padded, later, after):
    depth, orbitals = coeffs.shape
    out = pl.pallas_call(
        functools.partial(turn_kernel, depth // n_mo, n_mo, n_pair),
        in_specs=[IN_SMEM, IN_VMEM] + [IN_HBM] * len(later) + [ANYWHERE] * len(after),
        out_specs=[IN_HBM] * len(later) + [IN_VMEM],
        out_shape=[jax.ShapeDtypeStruct(x.shape, x.dtype) for x in later]
        + [jax.ShapeDtypeStruct((orbitals, n_mo * padded), jnp.bfloat16)],
        input_output_aliases={2 + n: n for n in range(len(later))},
        compiler_params=pltpu.CompilerParams(vmem_limit_bytes=24 * MIB),
        cost_estimate=COST,
        name="turn",
    )(place, coeffs, *later, *after)
    return out[-1], list(out[:-1])


def half_kernel(first, owners, *refs):
    n_mo = len(refs) - len(owners) - 1
    blocks, t_ref, outs = refs[:n_mo], refs[n_mo], refs[n_mo + 1 :]
    kc, block, lanes = outs[0].shape[2:]
    firsts = [first if x.shape[0] > kc else 0 for x in blocks]
    columns = [jnp.concatenate([x[at + k] for k in range(kc)], axis=1) for x, at in zip(blocks, firsts)]
    half = jnp.dot(t_ref[...], jnp.concatenate(columns, axis=0), preferred_element_type=jnp.float32)
    for out, its in zip(outs, owners):
        for at, o in enumerate(its):
            for k in range(kc):
                piece = half[o * block : (o + 1) * block, k * lanes : (k + 1) * lanes]
                out[0, at, k] = piece.astype(jnp.bfloat16)


def half_kernel_after(n_blocks, n_outs, first, owners, *refs):
    half_kernel(first, owners, *refs[: n_blocks + 1], *refs[len(refs) - n_outs :])


def half_of(blocks, turned, first, owners, later, after):
    kc, _, lanes = blocks[-1].shape
    block = turned.shape[0] // sum(len(its) for its in owners)
    n = len(blocks) + 1
    out = pl.pallas_call(
        functools.partial(half_kernel_after, len(blocks), len(owners), first, owners),
        in_specs=[IN_VMEM] * n + [IN_HBM] * len(later) + [ANYWHERE] * len(after),
        out_specs=[IN_HBM] * len(later) + [IN_VMEM] * len(owners),
        out_shape=[jax.ShapeDtypeStruct(x.shape, x.dtype) for x in later]
        + [jax.ShapeDtypeStruct((1, len(its), kc, block, lanes), jnp.bfloat16) for its in owners],
        input_output_aliases={n + m: m for m in range(len(later))},
        compiler_params=pltpu.CompilerParams(vmem_limit_bytes=24 * MIB),
        cost_estimate=COST,
        name="half",
    )(*blocks, turned, *later, *after)
    return list(out[len(later) :]), list(out[: len(later)])


def merge_kernel(n_parts, picks, *refs):
    outs = refs[len(refs) - len(picks) :]
    for out, its in zip(outs, picks):
        at = 0
        for x, pick in zip(refs[:n_parts], its):
            for i in range(x.shape[0]):
                for n, o in enumerate(pick):
                    out[at, n] = x[i, o]
                at += 1


def merge(parts, picks, after):
    lines = sum(x.shape[0] for x in parts)
    out = pl.pallas_call(
        functools.partial(merge_kernel, len(parts), picks),
        in_specs=[IN_VMEM] * len(parts) + [ANYWHERE] * len(after),
        out_specs=[IN_VMEM] * len(picks),
        out_shape=[
            jax.ShapeDtypeStruct((lines, len(its[0]), *parts[0].shape[2:]), jnp.bfloat16) for its in picks
        ],
        compiler_params=pltpu.CompilerParams(vmem_limit_bytes=24 * MIB),
        cost_estimate=COST,
        name="merge",
    )(*parts, *after)
    return list(out)


def wait_kernel(*refs):
    refs[-1][...] = jnp.zeros_like(refs[-1])


def wait_for(after):
    return pl.pallas_call(
        wait_kernel,
        in_specs=[ANYWHERE] * len(after),
        out_specs=IN_VMEM,
        out_shape=jax.ShapeDtypeStruct((8, LANES), jnp.float32),
        compiler_params=pltpu.CompilerParams(vmem_limit_bytes=24 * MIB),
        cost_estimate=COST,
        name="wait",
    )(*after)


def place_rows(pieces, sources, k_all, place_ref, held):
    for piece, (offsets, first) in zip(pieces, sources):
        for n, offset in enumerate(offsets):
            row = (place_ref[1] ^ offset) * k_all + first
            held[pl.ds(row, piece.shape[2])] = piece[n, 0]


def collect_kernel(sources, k_all, place_ref, *refs):
    place_rows(refs, sources, k_all, place_ref, refs[-1])


def collect(pieces, sources, place, n_pair, after):
    block, lanes = pieces[0].shape[-2:]
    k_all = sum(CHUNKS)
    return pl.pallas_call(
        functools.partial(collect_kernel, sources, k_all),
        in_specs=[IN_SMEM] + [IN_VMEM] * len(pieces) + [ANYWHERE] * len(after),
        out_specs=IN_VMEM,
        out_shape=jax.ShapeDtypeStruct((n_pair * k_all, block, lanes), jnp.bfloat16),
        compiler_params=pltpu.CompilerParams(vmem_limit_bytes=24 * MIB),
        cost_estimate=COST,
        name="collect",
    )(place, *pieces, *after)


def combine_kernel(sources, k_all, per_step, mirror_ref, place_ref, *refs):
    out_hbm, held, done, sems = refs[-4:]
    place_rows(refs[1:], sources, k_all, place_ref, held)

    def copy_of(step):
        rows = pl.ds(step * per_step, per_step)
        return pltpu.make_async_copy(done.at[rows], out_hbm.at[rows], sems.at[step])

    @pl.loop(0, held.shape[0] // per_step)
    def _(step):
        for n in range(per_step):
            k = step * per_step + n
            done[k] = 0.5 * (held[k].astype(jnp.float32) + held[mirror_ref[k]].astype(jnp.float32))
        copy_of(step).start()

    @pl.loop(0, held.shape[0] // per_step)
    def _(step):
        copy_of(step).wait()


def combine(held, pieces, sources, mirror, place, after):
    rows, block, lanes = held.shape
    per_step = max(1, 16 * 64 // block)
    return pl.pallas_call(
        functools.partial(combine_kernel, sources, sum(CHUNKS), per_step),
        in_specs=[IN_SMEM] * 2 + [IN_VMEM] * (1 + len(pieces)) + [ANYWHERE] * len(after),
        out_specs=[IN_HBM, IN_VMEM],
        out_shape=[
            jax.ShapeDtypeStruct((rows, block, lanes), jnp.float32),
            jax.ShapeDtypeStruct((rows, block, lanes), jnp.bfloat16),
        ],
        input_output_aliases={2: 1},
        scratch_shapes=[
            pltpu.VMEM((rows, block, lanes), jnp.float32),
            pltpu.SemaphoreType.DMA((rows // per_step,)),
        ],
        compiler_params=pltpu.CompilerParams(vmem_limit_bytes=24 * MIB),
        cost_estimate=COST,
        name="combine",
    )(mirror, place, held, *pieces, *after)[0]


def flipped(x, axis, size, offset, name):
    with jax.named_scope(name):
        return lax.ppermute(x, axis, [(i, i ^ offset) for i in range(size)])


def digits(n_pair, sizes):
    bits = [1 << n for n in reversed(range(n_pair.bit_length() - 1))]
    masks = []
    while bits:
        size = sizes[min(len(masks), len(sizes) - 1)]
        some = bits[:size] if size > 0 else bits[size:]
        masks.append(sum(some))
        bits = [bit for bit in bits if bit not in some]
    return masks


def on_device(n_pair, n_mo, integrals, coeffs, mirror):
    rows = integrals.shape[1]
    padded = -(-rows // STEP) * STEP
    n_near = n_pair // 2
    by_r = jnp.transpose(integrals, (1, 0, 2))
    place = jnp.stack([lax.axis_index("mo"), lax.axis_index("pair")]).astype(jnp.int32)
    last = len(CHUNKS) - 1
    firsts = [sum(CHUNKS[:c]) for c in range(last + 1)]

    near, queue, token = [], [], []
    for batch, chunks in enumerate(BATCHES):
        (own, beside), far = quarter_of(place, by_r, coeffs, n_mo, padded, batch, token)
        beside = flipped(beside, "mo", n_mo, 1, f"beside{batch}")
        near += [(own, beside, sum(chunks[:c])) for c in range(len(chunks))]
        queue += far
        token = [own]

    def fetch(c, o, x):
        return flipped(x, "mo", n_mo, o, f"y{2 * c + o - 2}")

    def arrive(c):
        return [fetch(c, o, x) for o, x in enumerate(queue[c], 2)]

    arrived = [arrive(0)]
    turned, queue[1] = turn(place, coeffs, n_mo, n_pair, padded, queue[1], arrived[0][:1] + token)
    arrived += [arrive(1)] + [[] for _ in range(2, last + 1)]

    levels = [digits(n_pair, sizes) for sizes in SIZES]
    steps = [(c, c, 0) for c in range(last + 1)]
    for c, masks in enumerate(levels):
        steps += [(c + (n + n / 10 if SIZES[c][0] > 0 else n * 3 / 10), c, n) for n in range(1, len(masks))]
    parts, owners, offsets, token = [[] for _ in CHUNKS], [[] for _ in CHUNKS], [[] for _ in CHUNKS], []

    def plan(c, level):
        mask, gone = levels[c][level], sum(levels[c][:level])
        flips = [o for o in range(1, n_pair) if not o & ~mask][::-1]
        left = [o for o in range(n_pair) if not o & gone]
        return [o for o in left if not o & mask], flips, [[o for o in left if o & mask == flip] for flip in flips]

    def send(c, level, messages):
        _, flips, sent = plan(c, level)
        before = [o for group in offsets[c] for o in group]
        for flip, some, message in zip(flips, sent, messages):
            offsets[c].append([o ^ flip for o in before])
            owners[c].append([o ^ flip for o in some])
            parts[c].append(flipped(message, "pair", n_pair, flip, f"z{flip}c{c}"))

    for _, c, level in sorted(steps):
        kept, _, sent = plan(c, level)
        if level == 0:
            blocks = [*near[c][:2], *arrived[c]]
            later, coming = LATER.get(c, (0, []))
            wait = [queue[later][o - 2] for o in coming]
            (keep, *messages), wait = half_of(blocks, turned, near[c][2], [kept, *sent], wait, token)
            arrived[later] += [fetch(later, o, x) for o, x in zip(coming, wait)]
            parts[c], owners[c], offsets[c] = [keep], [kept], [[0]]
        else:
            picks = [[[its.index(o) for o in some] for its in owners[c]] for some in sent]
            done = {(1, 1): arrived[last][:1], (last, 1): parts[0][-1:]}
            done = list(done.get((c, level), []))
            messages = merge(parts[c], picks, token + done)
        token = messages[:1]
        send(c, level, messages)
    for n in (-2, -1, -3):
        token = [wait_for([parts[last - 1][n], *token])]
    late = [parts[1][-1], *parts[last][-3:]]
    both = [
        (x, (tuple(group), first))
        for chunk, its, first in zip(parts, offsets, firsts)
        for x, group in zip(chunk, its)
    ]
    early = [entry for entry in both if all(entry[0] is not x for x in late)]
    held = collect(*zip(*early), place, n_pair, token)
    token = [held]
    for x in late[1:]:
        token = [wait_for([x, *token])]
    rest = [entry for entry in both if any(entry[0] is x for x in late)]
    return combine(held, *zip(*rest), mirror, place, token[:1] if token[0] is not held else [])


def solution(mesh):
    return jax.shard_map(
        functools.partial(on_device, mesh.shape["pair"], mesh.shape["mo"]),
        mesh=mesh,
        in_specs=(P("pair", "mo", None), P(), P()),
        out_specs=P(None, "pair", "mo"),
        check_vma=False,
    )
```

```python
import functools

import jax
import jax.numpy as jnp
from jax import lax
from jax.experimental import pallas as pl
from jax.experimental.pallas import tpu as pltpu
from jax.sharding import PartitionSpec as P

LANES = 128
STEP = 128
LATER = {0: (2, [2, 3]), 1: (3, [2]), 2: (3, [3])}
BATCHES = ((4, 4), (4, 4))
CHUNKS = sum(BATCHES, ())
SIZES = ((1,), (1,), (-1, 2), (-1, 2))
PART = 256
MIB = 1024 * 1024
COST = pl.CostEstimate(flops=1024, bytes_accessed=1024, transcendentals=0)
IN_VMEM = pl.BlockSpec(memory_space=pltpu.VMEM)
IN_SMEM = pl.BlockSpec(memory_space=pltpu.SMEM)
ANYWHERE = pl.BlockSpec(memory_space=pl.ANY)
IN_HBM = pl.BlockSpec(memory_space=pltpu.MemorySpace.HBM)


def quarter_kernel(batch, n_mo, blocks, n_after, place_ref, x_hbm, c_hbm, *refs):
    outs, (x_ref, c_ref, turn_ref, x_sems, c_sem) = refs[n_after:-5], refs[-5:]
    rows, depth = x_hbm.shape[0], x_hbm.shape[2]
    padded, some, _ = x_ref.shape
    many = PART // some

    columns = []
    for o in range(n_mo):
        mine = pl.ds(pl.multiple_of((place_ref[0] ^ o) * LANES, LANES), LANES)
        columns.append(pltpu.make_async_copy(c_hbm.at[:, mine], c_ref.at[:, o * LANES : (o + 1) * LANES], c_sem.at[o]))
    parts = []
    for n, first in enumerate(range(0, padded, STEP)):
        lines = pl.ds(first, min(STEP, rows - first))
        source = x_hbm.at[lines, pl.ds(batch * some, some)]
        parts.append(pltpu.make_async_copy(source, x_ref.at[lines], x_sems.at[n]))
    for copy in parts[:1] + columns + parts[1:]:
        copy.start()
    x_ref[rows:] = jnp.zeros((padded - rows, some, depth), jnp.bfloat16)
    to = lax.broadcasted_iota(jnp.int32, (PART, PART), 0)
    source = lax.broadcasted_iota(jnp.int32, (PART, PART), 1)
    is_source = source == (to & (many - 1)) * some + (to >> (many.bit_length() - 1))
    turn_ref[...] = jnp.where(is_source, 1.0, 0.0).astype(jnp.bfloat16)
    for copy in columns:
        copy.wait()
    for n, first in enumerate(range(0, padded, STEP)):
        parts[n].wait()
        x = x_ref[first : first + STEP].reshape(STEP * some, depth)
        product = jnp.dot(x, c_ref[...], preferred_element_type=jnp.float32).astype(jnp.bfloat16)
        for part in range(STEP // many):
            lines = jnp.dot(
                turn_ref[...], product[part * PART : (part + 1) * PART], preferred_element_type=jnp.float32
            ).astype(jnp.bfloat16)
            at = first + part * many
            for out, (o, k) in zip(outs, blocks):
                for row in range(out.shape[0]):
                    line = (k + row) * many
                    out[row, at : at + many] = lines[line : line + many, o * LANES : (o + 1) * LANES]


def quarter_of(place, by_r, coeffs, n_mo, padded, batch, after):
    depth, orbitals = coeffs.shape
    chunks = BATCHES[batch]
    some = sum(chunks)
    blocks = [(0, 0), (1, 0)] + [(o, sum(chunks[:c])) for c in range(len(chunks)) for o in range(2, n_mo)]
    sizes = [some] * 2 + [kc for kc in chunks for _ in range(2, n_mo)]
    outs = [jax.ShapeDtypeStruct((kc, padded, LANES), jnp.bfloat16) for kc in sizes]
    out = pl.pallas_call(
        functools.partial(quarter_kernel, batch, n_mo, blocks, len(after)),
        in_specs=[IN_SMEM] + [IN_HBM] * 2 + [ANYWHERE] * len(after),
        out_specs=[IN_VMEM] * len(outs),
        out_shape=outs,
        scratch_shapes=[
            pltpu.VMEM((padded, some, depth), jnp.bfloat16),
            pltpu.VMEM((depth, orbitals), jnp.bfloat16),
            pltpu.VMEM((PART, PART), jnp.bfloat16),
            pltpu.SemaphoreType.DMA((padded // STEP,)),
            pltpu.SemaphoreType.DMA((n_mo,)),
        ],
        compiler_params=pltpu.CompilerParams(vmem_limit_bytes=51 * MIB),
        cost_estimate=COST,
        name="quarter",
    )(place, by_r, coeffs, *after)
    far = n_mo - 2
    return out[:2], [list(out[2 + far * c : 2 + far * (c + 1)]) for c in range(len(chunks))]


def turn_kernel(rows, n_mo, n_pair, place_ref, c_ref, *refs):
    out_ref = refs[-1]
    orbitals, padded = out_ref.shape[0], out_ref.shape[1] // n_mo
    block = orbitals // n_pair
    none = jnp.zeros((padded - rows, orbitals), jnp.float32)
    for n in range(n_mo):
        part = c_ref[n * rows : (n + 1) * rows, :].astype(jnp.float32)
        part = jnp.concatenate([part, none], axis=0).T
        columns = pl.ds(pl.multiple_of((place_ref[0] ^ n) * padded, padded), padded)
        for o in range(n_pair):
            lines = pl.ds(pl.multiple_of((place_ref[1] ^ o) * block, block), block)
            out_ref[lines, columns] = part[o * block : (o + 1) * block].astype(jnp.bfloat16)


def turn(place, coeffs, n_mo, n_pair, padded, later, after):
    depth, orbitals = coeffs.shape
    out = pl.pallas_call(
        functools.partial(turn_kernel, depth // n_mo, n_mo, n_pair),
        in_specs=[IN_SMEM, IN_VMEM] + [IN_HBM] * len(later) + [ANYWHERE] * len(after),
        out_specs=[IN_HBM] * len(later) + [IN_VMEM],
        out_shape=[jax.ShapeDtypeStruct(x.shape, x.dtype) for x in later]
        + [jax.ShapeDtypeStruct((orbitals, n_mo * padded), jnp.bfloat16)],
        input_output_aliases={2 + n: n for n in range(len(later))},
        compiler_params=pltpu.CompilerParams(vmem_limit_bytes=24 * MIB),
        cost_estimate=COST,
        name="turn",
    )(place, coeffs, *later, *after)
    return out[-1], list(out[:-1])


def half_kernel(first, owners, *refs):
    n_mo = len(refs) - len(owners) - 1
    blocks, t_ref, outs = refs[:n_mo], refs[n_mo], refs[n_mo + 1 :]
    kc, block, lanes = outs[0].shape[2:]
    firsts = [first if x.shape[0] > kc else 0 for x in blocks]
    columns = [jnp.concatenate([x[at + k] for k in range(kc)], axis=1) for x, at in zip(blocks, firsts)]
    half = jnp.dot(t_ref[...], jnp.concatenate(columns, axis=0), preferred_element_type=jnp.float32)
    for out, its in zip(outs, owners):
        for at, o in enumerate(its):
            for k in range(kc):
                piece = half[o * block : (o + 1) * block, k * lanes : (k + 1) * lanes]
                out[0, at, k] = piece.astype(jnp.bfloat16)


def half_kernel_after(n_blocks, n_outs, first, owners, *refs):
    half_kernel(first, owners, *refs[: n_blocks + 1], *refs[len(refs) - n_outs :])


def half_of(blocks, turned, first, owners, later, after):
    kc, _, lanes = blocks[-1].shape
    block = turned.shape[0] // sum(len(its) for its in owners)
    n = len(blocks) + 1
    out = pl.pallas_call(
        functools.partial(half_kernel_after, len(blocks), len(owners), first, owners),
        in_specs=[IN_VMEM] * n + [IN_HBM] * len(later) + [ANYWHERE] * len(after),
        out_specs=[IN_HBM] * len(later) + [IN_VMEM] * len(owners),
        out_shape=[jax.ShapeDtypeStruct(x.shape, x.dtype) for x in later]
        + [jax.ShapeDtypeStruct((1, len(its), kc, block, lanes), jnp.bfloat16) for its in owners],
        input_output_aliases={n + m: m for m in range(len(later))},
        compiler_params=pltpu.CompilerParams(vmem_limit_bytes=24 * MIB),
        cost_estimate=COST,
        name="half",
    )(*blocks, turned, *later, *after)
    return list(out[len(later) :]), list(out[: len(later)])


def merge_kernel(n_parts, picks, *refs):
    outs = refs[len(refs) - len(picks) :]
    for out, its in zip(outs, picks):
        at = 0
        for x, pick in zip(refs[:n_parts], its):
            for i in range(x.shape[0]):
                for n, o in enumerate(pick):
                    out[at, n] = x[i, o]
                at += 1


def merge(parts, picks, after):
    lines = sum(x.shape[0] for x in parts)
    out = pl.pallas_call(
        functools.partial(merge_kernel, len(parts), picks),
        in_specs=[IN_VMEM] * len(parts) + [ANYWHERE] * len(after),
        out_specs=[IN_VMEM] * len(picks),
        out_shape=[
            jax.ShapeDtypeStruct((lines, len(its[0]), *parts[0].shape[2:]), jnp.bfloat16) for its in picks
        ],
        compiler_params=pltpu.CompilerParams(vmem_limit_bytes=24 * MIB),
        cost_estimate=COST,
        name="merge",
    )(*parts, *after)
    return list(out)


def wait_kernel(*refs):
    refs[-1][...] = jnp.zeros_like(refs[-1])


def wait_for(after):
    return pl.pallas_call(
        wait_kernel,
        in_specs=[ANYWHERE] * len(after),
        out_specs=IN_VMEM,
        out_shape=jax.ShapeDtypeStruct((8, LANES), jnp.float32),
        compiler_params=pltpu.CompilerParams(vmem_limit_bytes=24 * MIB),
        cost_estimate=COST,
        name="wait",
    )(*after)


def place_rows(pieces, sources, k_all, place_ref, held):
    for piece, (offsets, first) in zip(pieces, sources):
        for n, offset in enumerate(offsets):
            row = (place_ref[1] ^ offset) * k_all + first
            held[pl.ds(row, piece.shape[2])] = 0.5 * piece[n, 0].astype(jnp.float32)


def collect_kernel(sources, k_all, place_ref, *refs):
    place_rows(refs, sources, k_all, place_ref, refs[-1])


def collect(pieces, sources, place, n_pair, after):
    block, lanes = pieces[0].shape[-2:]
    k_all = sum(CHUNKS)
    return pl.pallas_call(
        functools.partial(collect_kernel, sources, k_all),
        in_specs=[IN_SMEM] + [IN_VMEM] * len(pieces) + [ANYWHERE] * len(after),
        out_specs=IN_VMEM,
        out_shape=jax.ShapeDtypeStruct((n_pair * k_all, block, lanes), jnp.float32),
        compiler_params=pltpu.CompilerParams(vmem_limit_bytes=24 * MIB),
        cost_estimate=COST,
        name="collect",
    )(place, *pieces, *after)


def combine_kernel(sources, k_all, per_step, mirror_ref, place_ref, *refs):
    out_hbm, held, done, sems = refs[-4:]
    place_rows(refs[1:], sources, k_all, place_ref, held)

    def copy_of(step):
        rows = pl.ds(step * per_step, per_step)
        return pltpu.make_async_copy(done.at[rows], out_hbm.at[rows], sems.at[step])

    @pl.loop(0, held.shape[0] // per_step)
    def _(step):
        for n in range(per_step):
            k = step * per_step + n
            done[k] = held[k] + held[mirror_ref[k]]
        copy_of(step).start()

    @pl.loop(0, held.shape[0] // per_step)
    def _(step):
        copy_of(step).wait()


def combine(held, pieces, sources, mirror, place, after):
    rows, block, lanes = held.shape
    per_step = max(1, 16 * 64 // block)
    return pl.pallas_call(
        functools.partial(combine_kernel, sources, sum(CHUNKS), per_step),
        in_specs=[IN_SMEM] * 2 + [IN_VMEM] * (1 + len(pieces)) + [ANYWHERE] * len(after),
        out_specs=[IN_HBM, IN_VMEM],
        out_shape=[
            jax.ShapeDtypeStruct((rows, block, lanes), jnp.float32),
            jax.ShapeDtypeStruct((rows, block, lanes), jnp.float32),
        ],
        input_output_aliases={2: 1},
        scratch_shapes=[
            pltpu.VMEM((rows, block, lanes), jnp.float32),
            pltpu.SemaphoreType.DMA((rows // per_step,)),
        ],
        compiler_params=pltpu.CompilerParams(vmem_limit_bytes=24 * MIB),
        cost_estimate=COST,
        name="combine",
    )(mirror, place, held, *pieces, *after)[0]


def flipped(x, axis, size, offset, name):
    with jax.named_scope(name):
        return lax.ppermute(x, axis, [(i, i ^ offset) for i in range(size)])


def digits(n_pair, sizes):
    bits = [1 << n for n in reversed(range(n_pair.bit_length() - 1))]
    masks = []
    while bits:
        size = sizes[min(len(masks), len(sizes) - 1)]
        some = bits[:size] if size > 0 else bits[size:]
        masks.append(sum(some))
        bits = [bit for bit in bits if bit not in some]
    return masks


def on_device(n_pair, n_mo, integrals, coeffs, mirror):
    rows = integrals.shape[1]
    padded = -(-rows // STEP) * STEP
    n_near = n_pair // 2
    by_r = jnp.transpose(integrals, (1, 0, 2))
    place = jnp.stack([lax.axis_index("mo"), lax.axis_index("pair")]).astype(jnp.int32)
    last = len(CHUNKS) - 1
    firsts = [sum(CHUNKS[:c]) for c in range(last + 1)]

    near, queue, token = [], [], []
    for batch, chunks in enumerate(BATCHES):
        (own, beside), far = quarter_of(place, by_r, coeffs, n_mo, padded, batch, token)
        beside = flipped(beside, "mo", n_mo, 1, f"beside{batch}")
        near += [(own, beside, sum(chunks[:c])) for c in range(len(chunks))]
        queue += far
        token = [own]

    def fetch(c, o, x):
        return flipped(x, "mo", n_mo, o, f"y{2 * c + o - 2}")

    def arrive(c):
        return [fetch(c, o, x) for o, x in enumerate(queue[c], 2)]

    arrived = [arrive(0)]
    turned, queue[1] = turn(place, coeffs, n_mo, n_pair, padded, queue[1], arrived[0][:1] + token)
    arrived += [arrive(1)] + [[] for _ in range(2, last + 1)]

    levels = [digits(n_pair, sizes) for sizes in SIZES]
    steps = [(c, c, 0) for c in range(last + 1)]
    for c, masks in enumerate(levels):
        steps += [(c + (n + n / 10 if SIZES[c][0] > 0 else n * 3 / 10), c, n) for n in range(1, len(masks))]
    parts, owners, offsets, token = [[] for _ in CHUNKS], [[] for _ in CHUNKS], [[] for _ in CHUNKS], []

    def plan(c, level):
        mask, gone = levels[c][level], sum(levels[c][:level])
        flips = [o for o in range(1, n_pair) if not o & ~mask][::-1]
        left = [o for o in range(n_pair) if not o & gone]
        return [o for o in left if not o & mask], flips, [[o for o in left if o & mask == flip] for flip in flips]

    def send(c, level, messages):
        _, flips, sent = plan(c, level)
        before = [o for group in offsets[c] for o in group]
        for flip, some, message in zip(flips, sent, messages):
            offsets[c].append([o ^ flip for o in before])
            owners[c].append([o ^ flip for o in some])
            parts[c].append(flipped(message, "pair", n_pair, flip, f"z{flip}c{c}"))

    for _, c, level in sorted(steps):
        kept, _, sent = plan(c, level)
        if level == 0:
            blocks = [*near[c][:2], *arrived[c]]
            later, coming = LATER.get(c, (0, []))
            wait = [queue[later][o - 2] for o in coming]
            (keep, *messages), wait = half_of(blocks, turned, near[c][2], [kept, *sent], wait, token)
            arrived[later] += [fetch(later, o, x) for o, x in zip(coming, wait)]
            parts[c], owners[c], offsets[c] = [keep], [kept], [[0]]
        else:
            picks = [[[its.index(o) for o in some] for its in owners[c]] for some in sent]
            done = {(1, 1): arrived[last][:1], (last, 1): parts[0][-1:]}
            done = list(done.get((c, level), []))
            messages = merge(parts[c], picks, token + done)
        token = messages[:1]
        send(c, level, messages)
    for n in (-2, -1, -3):
        token = [wait_for([parts[last - 1][n], *token])]
    late = [parts[1][-1], *parts[last][-3:]]
    both = [
        (x, (tuple(group), first))
        for chunk, its, first in zip(parts, offsets, firsts)
        for x, group in zip(chunk, its)
    ]
    early = [entry for entry in both if all(entry[0] is not x for x in late)]
    held = collect(*zip(*early), place, n_pair, token)
    token = [held]
    for x in late[1:]:
        token = [wait_for([x, *token])]
    rest = [entry for entry in both if any(entry[0] is x for x in late)]
    return combine(held, *zip(*rest), mirror, place, token[:1] if token[0] is not held else [])


def solution(mesh):
    return jax.shard_map(
        functools.partial(on_device, mesh.shape["pair"], mesh.shape["mo"]),
        mesh=mesh,
        in_specs=(P("pair", "mo", None), P(), P()),
        out_specs=P(None, "pair", "mo"),
        check_vma=False,
    )
```

```python
import functools

import jax
import jax.numpy as jnp
from jax import lax
from jax.experimental import pallas as pl
from jax.experimental.pallas import tpu as pltpu
from jax.sharding import PartitionSpec as P

LANES = 128
STEP = 128
LATER = {0: (2, [2, 3]), 1: (3, [2]), 2: (3, [3])}
BATCHES = ((4, 4), (4, 4))
CHUNKS = sum(BATCHES, ())
SIZES = ((1,), (1,), (-1, 2), (-1, 2))
PART = 256
MIB = 1024 * 1024
COST = pl.CostEstimate(flops=1024, bytes_accessed=1024, transcendentals=0)
IN_VMEM = pl.BlockSpec(memory_space=pltpu.VMEM)
IN_SMEM = pl.BlockSpec(memory_space=pltpu.SMEM)
ANYWHERE = pl.BlockSpec(memory_space=pl.ANY)
IN_HBM = pl.BlockSpec(memory_space=pltpu.MemorySpace.HBM)


def quarter_kernel(batch, n_mo, blocks, n_after, place_ref, x_hbm, c_hbm, *refs):
    outs, (x_ref, c_ref, turn_ref, x_sems, c_sem) = refs[n_after:-5], refs[-5:]
    rows, depth = x_hbm.shape[0], x_hbm.shape[2]
    padded, some, _ = x_ref.shape
    many = PART // some

    columns = []
    for o in range(n_mo):
        mine = pl.ds(pl.multiple_of((place_ref[0] ^ o) * LANES, LANES), LANES)
        columns.append(pltpu.make_async_copy(c_hbm.at[:, mine], c_ref.at[:, o * LANES : (o + 1) * LANES], c_sem.at[o]))
    parts = []
    for n, first in enumerate(range(0, padded, STEP)):
        lines = pl.ds(first, min(STEP, rows - first))
        source = x_hbm.at[lines, pl.ds(batch * some, some)]
        parts.append(pltpu.make_async_copy(source, x_ref.at[lines], x_sems.at[n]))
    for copy in parts[:1] + columns + parts[1:]:
        copy.start()
    x_ref[rows:] = jnp.zeros((padded - rows, some, depth), jnp.bfloat16)
    to = lax.broadcasted_iota(jnp.int32, (PART, PART), 0)
    source = lax.broadcasted_iota(jnp.int32, (PART, PART), 1)
    is_source = source == (to & (many - 1)) * some + (to >> (many.bit_length() - 1))
    turn_ref[...] = jnp.where(is_source, 1.0, 0.0).astype(jnp.bfloat16)
    for copy in columns:
        copy.wait()
    for n, first in enumerate(range(0, padded, STEP)):
        parts[n].wait()
        x = x_ref[first : first + STEP].reshape(STEP * some, depth)
        product = jnp.dot(x, c_ref[...], preferred_element_type=jnp.float32).astype(jnp.bfloat16)
        for part in range(STEP // many):
            lines = jnp.dot(
                turn_ref[...], product[part * PART : (part + 1) * PART], preferred_element_type=jnp.float32
            ).astype(jnp.bfloat16)
            at = first + part * many
            for out, (o, k) in zip(outs, blocks):
                for row in range(out.shape[0]):
                    line = (k + row) * many
                    out[row, at : at + many] = lines[line : line + many, o * LANES : (o + 1) * LANES]


def quarter_of(place, by_r, coeffs, n_mo, padded, batch, after):
    depth, orbitals = coeffs.shape
    chunks = BATCHES[batch]
    some = sum(chunks)
    blocks = [(0, 0), (1, 0)] + [(o, sum(chunks[:c])) for c in range(len(chunks)) for o in range(2, n_mo)]
    sizes = [some] * 2 + [kc for kc in chunks for _ in range(2, n_mo)]
    outs = [jax.ShapeDtypeStruct((kc, padded, LANES), jnp.bfloat16) for kc in sizes]
    out = pl.pallas_call(
        functools.partial(quarter_kernel, batch, n_mo, blocks, len(after)),
        in_specs=[IN_SMEM] + [IN_HBM] * 2 + [ANYWHERE] * len(after),
        out_specs=[IN_VMEM] * len(outs),
        out_shape=outs,
        scratch_shapes=[
            pltpu.VMEM((padded, some, depth), jnp.bfloat16),
            pltpu.VMEM((depth, orbitals), jnp.bfloat16),
            pltpu.VMEM((PART, PART), jnp.bfloat16),
            pltpu.SemaphoreType.DMA((padded // STEP,)),
            pltpu.SemaphoreType.DMA((n_mo,)),
        ],
        compiler_params=pltpu.CompilerParams(vmem_limit_bytes=51 * MIB),
        cost_estimate=COST,
        name="quarter",
    )(place, by_r, coeffs, *after)
    far = n_mo - 2
    return out[:2], [list(out[2 + far * c : 2 + far * (c + 1)]) for c in range(len(chunks))]


def turn_kernel(rows, n_mo, n_pair, place_ref, c_ref, *refs):
    out_ref = refs[-1]
    orbitals, padded = out_ref.shape[0], out_ref.shape[1] // n_mo
    block = orbitals // n_pair
    none = jnp.zeros((padded - rows, orbitals), jnp.float32)
    for n in range(n_mo):
        part = c_ref[n * rows : (n + 1) * rows, :].astype(jnp.float32)
        part = jnp.concatenate([part, none], axis=0).T
        columns = pl.ds(pl.multiple_of((place_ref[0] ^ n) * padded, padded), padded)
        for o in range(n_pair):
            lines = pl.ds(pl.multiple_of((place_ref[1] ^ o) * block, block), block)
            out_ref[lines, columns] = part[o * block : (o + 1) * block].astype(jnp.bfloat16)


def turn(place, coeffs, n_mo, n_pair, padded, later, after):
    depth, orbitals = coeffs.shape
    out = pl.pallas_call(
        functools.partial(turn_kernel, depth // n_mo, n_mo, n_pair),
        in_specs=[IN_SMEM, IN_VMEM] + [IN_HBM] * len(later) + [ANYWHERE] * len(after),
        out_specs=[IN_HBM] * len(later) + [IN_VMEM],
        out_shape=[jax.ShapeDtypeStruct(x.shape, x.dtype) for x in later]
        + [jax.ShapeDtypeStruct((orbitals, n_mo * padded), jnp.bfloat16)],
        input_output_aliases={2 + n: n for n in range(len(later))},
        compiler_params=pltpu.CompilerParams(vmem_limit_bytes=24 * MIB),
        cost_estimate=COST,
        name="turn",
    )(place, coeffs, *later, *after)
    return out[-1], list(out[:-1])


def half_kernel(first, owners, *refs):
    n_mo = len(refs) - len(owners) - 1
    blocks, t_ref, outs = refs[:n_mo], refs[n_mo], refs[n_mo + 1 :]
    kc, block, lanes = outs[0].shape[2:]
    firsts = [first if x.shape[0] > kc else 0 for x in blocks]
    columns = [jnp.concatenate([x[at + k] for k in range(kc)], axis=1) for x, at in zip(blocks, firsts)]
    half = jnp.dot(t_ref[...], jnp.concatenate(columns, axis=0), preferred_element_type=jnp.float32)
    for out, its in zip(outs, owners):
        for at, o in enumerate(its):
            for k in range(kc):
                piece = half[o * block : (o + 1) * block, k * lanes : (k + 1) * lanes]
                out[0, at, k] = piece.astype(jnp.bfloat16)


def half_kernel_after(n_blocks, n_outs, first, owners, *refs):
    half_kernel(first, owners, *refs[: n_blocks + 1], *refs[len(refs) - n_outs :])


def half_of(blocks, turned, first, owners, later, after):
    kc, _, lanes = blocks[-1].shape
    block = turned.shape[0] // sum(len(its) for its in owners)
    n = len(blocks) + 1
    out = pl.pallas_call(
        functools.partial(half_kernel_after, len(blocks), len(owners), first, owners),
        in_specs=[IN_VMEM] * n + [IN_HBM] * len(later) + [ANYWHERE] * len(after),
        out_specs=[IN_HBM] * len(later) + [IN_VMEM] * len(owners),
        out_shape=[jax.ShapeDtypeStruct(x.shape, x.dtype) for x in later]
        + [jax.ShapeDtypeStruct((1, len(its), kc, block, lanes), jnp.bfloat16) for its in owners],
        input_output_aliases={n + m: m for m in range(len(later))},
        compiler_params=pltpu.CompilerParams(vmem_limit_bytes=24 * MIB),
        cost_estimate=COST,
        name="half",
    )(*blocks, turned, *later, *after)
    return list(out[len(later) :]), list(out[: len(later)])


def merge_kernel(n_parts, picks, *refs):
    outs = refs[len(refs) - len(picks) :]
    for out, its in zip(outs, picks):
        at = 0
        for x, pick in zip(refs[:n_parts], its):
            for i in range(x.shape[0]):
                for n, o in enumerate(pick):
                    out[at, n] = x[i, o]
                at += 1


def merge(parts, picks, after):
    lines = sum(x.shape[0] for x in parts)
    out = pl.pallas_call(
        functools.partial(merge_kernel, len(parts), picks),
        in_specs=[IN_VMEM] * len(parts) + [ANYWHERE] * len(after),
        out_specs=[IN_VMEM] * len(picks),
        out_shape=[
            jax.ShapeDtypeStruct((lines, len(its[0]), *parts[0].shape[2:]), jnp.bfloat16) for its in picks
        ],
        compiler_params=pltpu.CompilerParams(vmem_limit_bytes=24 * MIB),
        cost_estimate=COST,
        name="merge",
    )(*parts, *after)
    return list(out)


def wait_kernel(*refs):
    refs[-1][...] = jnp.zeros_like(refs[-1])


def wait_for(after):
    return pl.pallas_call(
        wait_kernel,
        in_specs=[ANYWHERE] * len(after),
        out_specs=IN_VMEM,
        out_shape=jax.ShapeDtypeStruct((8, LANES), jnp.float32),
        compiler_params=pltpu.CompilerParams(vmem_limit_bytes=24 * MIB),
        cost_estimate=COST,
        name="wait",
    )(*after)


def place_rows(pieces, sources, k_all, place_ref, held):
    for piece, (offsets, first) in zip(pieces, sources):
        for n, offset in enumerate(offsets):
            row = (place_ref[1] ^ offset) * k_all + first
            held[pl.ds(row, piece.shape[2])] = 0.5 * piece[n, 0].astype(jnp.float32)


def collect_kernel(sources, k_all, place_ref, *refs):
    place_rows(refs, sources, k_all, place_ref, refs[-1])


def collect(pieces, sources, place, n_pair, after):
    block, lanes = pieces[0].shape[-2:]
    k_all = sum(CHUNKS)
    return pl.pallas_call(
        functools.partial(collect_kernel, sources, k_all),
        in_specs=[IN_SMEM] + [IN_VMEM] * len(pieces) + [ANYWHERE] * len(after),
        out_specs=IN_VMEM,
        out_shape=jax.ShapeDtypeStruct((n_pair * k_all, block, lanes), jnp.float32),
        compiler_params=pltpu.CompilerParams(vmem_limit_bytes=24 * MIB),
        cost_estimate=COST,
        name="collect",
    )(place, *pieces, *after)


def combine_kernel(sources, k_all, per_step, mirror_ref, place_ref, *refs):
    out_hbm, held, done, sems = refs[-4:]
    place_rows(refs[1:], sources, k_all, place_ref, held)

    def copy_of(step):
        rows = pl.ds(step * per_step, per_step)
        return pltpu.make_async_copy(done.at[rows], out_hbm.at[rows], sems.at[step])

    @pl.loop(0, held.shape[0] // per_step)
    def _(step):
        for n in range(per_step):
            k = step * per_step + n
            done[k] = held[k] + held[mirror_ref[k]]
        copy_of(step).start()

    @pl.loop(0, held.shape[0] // per_step)
    def _(step):
        copy_of(step).wait()


def combine(held, pieces, sources, mirror, place, after):
    rows, block, lanes = held.shape
    per_step = max(1, 8 * 64 // block)
    return pl.pallas_call(
        functools.partial(combine_kernel, sources, sum(CHUNKS), per_step),
        in_specs=[IN_SMEM] * 2 + [IN_VMEM] * (1 + len(pieces)) + [ANYWHERE] * len(after),
        out_specs=[IN_HBM, IN_VMEM],
        out_shape=[
            jax.ShapeDtypeStruct((rows, block, lanes), jnp.float32),
            jax.ShapeDtypeStruct((rows, block, lanes), jnp.float32),
        ],
        input_output_aliases={2: 1},
        scratch_shapes=[
            pltpu.VMEM((rows, block, lanes), jnp.float32),
            pltpu.SemaphoreType.DMA((rows // per_step,)),
        ],
        compiler_params=pltpu.CompilerParams(vmem_limit_bytes=24 * MIB),
        cost_estimate=COST,
        name="combine",
    )(mirror, place, held, *pieces, *after)[0]


def flipped(x, axis, size, offset, name):
    with jax.named_scope(name):
        return lax.ppermute(x, axis, [(i, i ^ offset) for i in range(size)])


def digits(n_pair, sizes):
    bits = [1 << n for n in reversed(range(n_pair.bit_length() - 1))]
    masks = []
    while bits:
        size = sizes[min(len(masks), len(sizes) - 1)]
        some = bits[:size] if size > 0 else bits[size:]
        masks.append(sum(some))
        bits = [bit for bit in bits if bit not in some]
    return masks


def on_device(n_pair, n_mo, integrals, coeffs, mirror):
    rows = integrals.shape[1]
    padded = -(-rows // STEP) * STEP
    n_near = n_pair // 2
    by_r = jnp.transpose(integrals, (1, 0, 2))
    place = jnp.stack([lax.axis_index("mo"), lax.axis_index("pair")]).astype(jnp.int32)
    last = len(CHUNKS) - 1
    firsts = [sum(CHUNKS[:c]) for c in range(last + 1)]

    near, queue, token = [], [], []
    for batch, chunks in enumerate(BATCHES):
        (own, beside), far = quarter_of(place, by_r, coeffs, n_mo, padded, batch, token)
        beside = flipped(beside, "mo", n_mo, 1, f"beside{batch}")
        near += [(own, beside, sum(chunks[:c])) for c in range(len(chunks))]
        queue += far
        token = [own]

    def fetch(c, o, x):
        return flipped(x, "mo", n_mo, o, f"y{2 * c + o - 2}")

    def arrive(c):
        return [fetch(c, o, x) for o, x in enumerate(queue[c], 2)]

    arrived = [arrive(0)]
    turned, queue[1] = turn(place, coeffs, n_mo, n_pair, padded, queue[1], arrived[0][:1] + token)
    arrived += [arrive(1)] + [[] for _ in range(2, last + 1)]

    levels = [digits(n_pair, sizes) for sizes in SIZES]
    steps = [(c, c, 0) for c in range(last + 1)]
    for c, masks in enumerate(levels):
        steps += [(c + (n + n / 10 if SIZES[c][0] > 0 else n * 3 / 10), c, n) for n in range(1, len(masks))]
    parts, owners, offsets, token = [[] for _ in CHUNKS], [[] for _ in CHUNKS], [[] for _ in CHUNKS], []

    def plan(c, level):
        mask, gone = levels[c][level], sum(levels[c][:level])
        flips = [o for o in range(1, n_pair) if not o & ~mask][::-1]
        left = [o for o in range(n_pair) if not o & gone]
        return [o for o in left if not o & mask], flips, [[o for o in left if o & mask == flip] for flip in flips]

    def send(c, level, messages):
        _, flips, sent = plan(c, level)
        before = [o for group in offsets[c] for o in group]
        for flip, some, message in zip(flips, sent, messages):
            offsets[c].append([o ^ flip for o in before])
            owners[c].append([o ^ flip for o in some])
            parts[c].append(flipped(message, "pair", n_pair, flip, f"z{flip}c{c}"))

    for _, c, level in sorted(steps):
        kept, _, sent = plan(c, level)
        if level == 0:
            blocks = [*near[c][:2], *arrived[c]]
            later, coming = LATER.get(c, (0, []))
            wait = [queue[later][o - 2] for o in coming]
            (keep, *messages), wait = half_of(blocks, turned, near[c][2], [kept, *sent], wait, token)
            arrived[later] += [fetch(later, o, x) for o, x in zip(coming, wait)]
            parts[c], owners[c], offsets[c] = [keep], [kept], [[0]]
        else:
            picks = [[[its.index(o) for o in some] for its in owners[c]] for some in sent]
            done = {(1, 1): arrived[last][:1], (last, 1): parts[0][-1:]}
            done = list(done.get((c, level), []))
            messages = merge(parts[c], picks, token + done)
        token = messages[:1]
        send(c, level, messages)
    for n in (-2, -1, -3):
        token = [wait_for([parts[last - 1][n], *token])]
    late = [parts[1][-1], *parts[last][-3:]]
    both = [
        (x, (tuple(group), first))
        for chunk, its, first in zip(parts, offsets, firsts)
        for x, group in zip(chunk, its)
    ]
    early = [entry for entry in both if all(entry[0] is not x for x in late)]
    held = collect(*zip(*early), place, n_pair, token)
    token = [held]
    for x in late[1:]:
        token = [wait_for([x, *token])]
    rest = [entry for entry in both if any(entry[0] is x for x in late)]
    return combine(held, *zip(*rest), mirror, place, token[:1] if token[0] is not held else [])


def solution(mesh):
    return jax.shard_map(
        functools.partial(on_device, mesh.shape["pair"], mesh.shape["mo"]),
        mesh=mesh,
        in_specs=(P("pair", "mo", None), P(), P()),
        out_specs=P(None, "pair", "mo"),
        check_vma=False,
    )
```
